32 devices in a mesh: blk: 8 (over z, x), head: 2 (over y), dec: 2 (over core).
Axes of the slice: x: 2, y: 2, z: 4, core: 2. Of those that a mesh axis runs over, the one named last changes fastest.
Arguments:
- queries: bfloat16 [2048, 1536], P('blk', ('head', 'dec')), may hold values from -12 to 12
- key_vectors: bfloat16 [2048, 1536], P('blk', ('head', 'dec')), may hold values from -5 to 5
- values: bfloat16 [2048, 1536], P('blk', ('head', 'dec')), may hold values from -6 to 6
- lookback: int32 [12], replicated, may hold values from 0 to 5, as said below
- residual: bfloat16 [2048, 3072], P(('blk', 'head', 'dec')), may hold values from -0.1875 to 0.1875
- out_weight: bfloat16 [1536, 3072], P(('head', 'dec')), may hold values from -0.15625 to 0.15625
- branch_gate: float32 [3072], replicated, may hold values from 0.5 to 1.5
- final_shift: float32 [3072], replicated, may hold values from -0.5 to 0.5
- final_scale: float32 [3072], replicated, may hold values from -0.5 to 0.5
- final_weight: bfloat16 [3072, 64], replicated, may hold values from -0.109375 to 0.109375
- decoder_kernel: bfloat16 [432, 512], replicated, may hold values from -0.3125 to 0.3125
- decoder_bias: float32 [512], replicated, may hold values from -3 to 3
Outputs:
- features: bfloat16 [128, 64, 512], P(('blk', 'head', 'dec'))
The draws below stay inside these ranges and needn't reach their ends.
Inputs may be any that keep to these rules, and one draw needn't show every extreme that they name: lookback[h] is how many frames before its own the queries of head h may see; some head sees 5 earlier frames and some head none.
All inputs are finite; a program needn't handle non-finite values.
Results may differ from the reference program's by a relative error of at most 0.02.
Values may be sent and summed in bfloat16 or wider, within the bound.
A program may use at most 192 MiB of HBM per device.

```python
import jax
import jax.numpy as jnp
from jax import lax

HEADS = 12
DH = 128
D = 3072
LC = 16
CO = 512
FRAMES = 8
WINDOW = 5
PW = 32
SLAB = 256
HD = 1536
PC = 64
TOKENS = 2048


def anchor_pair(key):
    query_base = 3.0 * jax.random.normal(jax.random.fold_in(key, 11), (TOKENS, HD), jnp.float32)
    key_base = jax.random.normal(jax.random.fold_in(key, 12), (TOKENS, HD), jnp.float32)
    query_base = jnp.clip(query_base, -12.0, 12.0)
    key_base = jnp.clip(key_base, -5.0, 5.0)
    return (query_base, key_base)


def draw_queries(key, part):
    return anchor_pair(key)[0].astype(jnp.bfloat16)


def draw_key_vectors(key, part):
    return anchor_pair(key)[1].astype(jnp.bfloat16)


def draw_lookback(key, part):
    base = jax.random.randint(jax.random.fold_in(key, 21), (HEADS,), 0, WINDOW + 1, dtype=jnp.int32)
    widest_head = jax.random.randint(jax.random.fold_in(key, 22), (), 0, HEADS, dtype=jnp.int32)
    offset = jax.random.randint(jax.random.fold_in(key, 23), (), 1, HEADS, dtype=jnp.int32)
    narrow_head = (widest_head + offset) % HEADS
    head_ids = jnp.arange(HEADS, dtype=jnp.int32)
    base = jnp.where(head_ids == widest_head, WINDOW, base)
    base = jnp.where(head_ids == narrow_head, 0, base)
    return base.astype(jnp.int32)


def level_of(stream_key, extent, split, least, top_value):
    def one(position, shards_of):
        heights = jax.random.uniform(jax.random.fold_in(jax.random.fold_in(stream_key, 6), position), (shards_of,), jnp.float32, least / len(split), top_value / len(split))
        return jnp.repeat(jnp.exp(heights), extent[position] // shards_of).reshape((-1,) + (1,) * (len(extent) - position - 1))

    level = one(*split[0])
    for cut in split[1:]:
        level = level * one(*cut)
    return level


def centred(rng, extent, scale, bound, pieces=(), held_as=jnp.bfloat16):
    gain = level_of(rng, extent, pieces, -0.22, 0.18) if pieces else 1.0
    array = jax.random.normal(rng, extent, jnp.float32) * scale * gain
    return jnp.minimum(jnp.maximum(array, -bound), bound).astype(held_as)


def setup_inputs(seed: int = 0) -> dict:
    key_list = jax.random.split(jax.random.key(seed), 13)
    return {
        "queries": draw_queries(jax.random.fold_in(key_list[12], 71), 0),
        "key_vectors": draw_key_vectors(jax.random.fold_in(key_list[12], 71), 0),
        "values": centred(key_list[2], (TOKENS, HD), 1.0, 6.0, ((0, 8), (1, 4))),
        "lookback": draw_lookback(jax.random.fold_in(key_list[12], 71), 0),
        "residual": centred(key_list[4], (TOKENS, D), 0.03, 0.1875, ((0, 32),)),
        "out_weight": centred(key_list[5], (HD, D), HD ** -0.5, 0.15625, ((0, 4),)),
        "branch_gate": jnp.clip(jax.random.uniform(key_list[6], (D,), jnp.float32, 0.5, 1.5), 0.5, 1.5),
        "final_shift": jnp.clip(jax.random.uniform(key_list[7], (D,), jnp.float32, -0.5, 0.5), -0.5, 0.5),
        "final_scale": jnp.clip(jax.random.uniform(key_list[8], (D,), jnp.float32, -0.5, 0.5), -0.5, 0.5),
        "final_weight": centred(key_list[9], (D, PC), D ** -0.5, 0.109375),
        "decoder_kernel": centred(key_list[10], (27 * LC, CO), (27 * LC) ** -0.5, 0.3125),
        "decoder_bias": centred(key_list[11], (CO,), 0.5, 3.0, (), jnp.float32),
    }


def attend_head(query_head, key_head, value_head, lookback_head):
    frame_len = TOKENS // FRAMES
    key_frame = jnp.arange(TOKENS, dtype=jnp.int32) // frame_len
    query_blocks = query_head.reshape(TOKENS // SLAB, SLAB, DH)
    block_ids = jnp.arange(TOKENS // SLAB, dtype=jnp.int32)

    def one_block(inputs):
        block, block_id = inputs
        scores = jnp.dot(block, key_head.T, preferred_element_type=jnp.float32) * DH ** (-0.5)
        query_frame = (block_id * SLAB + jnp.arange(SLAB, dtype=jnp.int32)) // frame_len
        visible = (key_frame[None, :] <= query_frame[:, None]) & (key_frame[None, :] >= query_frame[:, None] - lookback_head)
        row_max = lax.optimization_barrier(jnp.max(jnp.where(visible, scores, -1e+30), axis=1))
        weights = jnp.where(visible, jnp.exp(scores - row_max[:, None]), 0.0).astype(jnp.bfloat16)
        row_total = lax.optimization_barrier(jnp.sum(weights.astype(jnp.float32), axis=1))
        mixed = jnp.dot(weights, value_head, preferred_element_type=jnp.float32)
        return mixed / row_total[:, None]
    return lax.map(one_block, (query_blocks, block_ids)).reshape(TOKENS, DH)

def reference(queries, key_vectors, values, lookback, residual, out_weight, branch_gate, final_shift, final_scale, final_weight, decoder_kernel, decoder_bias):
    query_heads = queries.reshape(TOKENS, HEADS, DH).transpose(1, 0, 2)
    key_heads = key_vectors.reshape(TOKENS, HEADS, DH).transpose(1, 0, 2)
    value_heads = values.reshape(TOKENS, HEADS, DH).transpose(1, 0, 2)

    def per_head(inputs):
        return attend_head(inputs[0], inputs[1], inputs[2], inputs[3])
    heads_out = lax.map(per_head, (query_heads, key_heads, value_heads, lookback))
    attended = heads_out.transpose(1, 0, 2).reshape(TOKENS, HD).astype(jnp.bfloat16)
    projected = jnp.dot(attended, out_weight, preferred_element_type=jnp.float32)
    hidden = residual.astype(jnp.float32) + branch_gate[None, :] * projected
    center = lax.optimization_barrier(jnp.mean(hidden, axis=1, keepdims=True))
    spread = lax.optimization_barrier(jnp.mean((hidden - center) ** 2, axis=1, keepdims=True))
    normed = ((hidden - center) * lax.rsqrt(spread + 1e-06) * (1.0 + final_scale[None, :]) + final_shift[None, :]).astype(jnp.bfloat16)
    patches = jnp.dot(normed, final_weight, preferred_element_type=jnp.float32).astype(jnp.bfloat16)
    frame_rows = TOKENS // (FRAMES * PW)
    height = 2 * frame_rows
    width = 2 * PW
    canvas = patches.reshape(FRAMES * frame_rows, PW, 2, 2, LC).transpose(0, 2, 1, 3, 4).reshape(FRAMES * height, width, LC)
    canvas = jnp.pad(canvas, ((1, 1), (0, 0), (0, 0)))
    framed = [canvas[g * height:g * height + height + 2] for g in range(FRAMES)]
    history = jnp.stack([framed[0], framed[0]] + framed)
    history = jnp.pad(history, ((0, 0), (0, 0), (1, 1), (0, 0)))
    summed = jnp.zeros((FRAMES * height * width, CO), jnp.float32)
    for time_tap in range(3):
        for row_tap in range(3):
            for column_tap in range(3):
                tap_index = (time_tap * 3 + row_tap) * 3 + column_tap
                window = history[time_tap:time_tap + FRAMES, row_tap:row_tap + height, column_tap:column_tap + width, :].reshape(-1, LC)
                summed = summed + jnp.dot(window, decoder_kernel[tap_index * LC:(tap_index + 1) * LC], preferred_element_type=jnp.float32)
    features = (summed + decoder_bias[None, :]).astype(jnp.bfloat16)
    return features.reshape(FRAMES * height, width, CO)
```

```python
import jax
import jax.numpy as jnp
from jax import lax
from jax.experimental import pallas as pl
from jax.experimental.pallas import tpu as pltpu
from jax.sharding import PartitionSpec as P

DH = 128
LC = 16
FRAMES = 8
PW = 32


def padded_2(cells, sides, width):
    for axis, dim in sides:
        count = lax.axis_size(axis)
        ends = count - 1
        head = lax.slice_in_dim(cells, 0, width, axis=dim)
        tail = lax.slice_in_dim(cells, cells.shape[dim] - width, cells.shape[dim], axis=dim)
        cells = jnp.concatenate(
            [
                lax.ppermute(tail, axis, [(i, (i + 1) % count) for i in range(ends)]),
                cells,
                lax.ppermute(head, axis, [((i + 1) % count, i) for i in range(ends)]),
            ],
            axis=dim,
        )
    return cells


def from_behind(x, axis, by):
    peers = lax.axis_size(axis)
    pairs = [(i, i + by) for i in range(peers) if 0 <= i + by < peers]
    return lax.ppermute(x, axis, pairs)


def attend_block(carry, shard_pair, query_heads, query_frame, lookback_heads, frame_len):
    running_max, row_total, accumulated = carry
    key_block, value_block = shard_pair
    key_count = key_block.shape[0]
    head_count = query_heads.shape[1]
    key_heads = key_block.reshape(key_count, head_count, DH)
    value_heads = value_block.reshape(key_count, head_count, DH)
    scores = jnp.einsum(
        "qhd,khd->hqk", query_heads, key_heads, preferred_element_type=jnp.float32
    ) * DH ** (-0.5)
    key_pos = jnp.arange(key_count, dtype=jnp.int32)
    key_frame = key_pos // frame_len
    visible = (
        (key_pos >= 0)[None, None, :]
        & (key_frame[None, None, :] <= query_frame[None, :, None])
        & (key_frame[None, None, :] >= query_frame[None, :, None] - lookback_heads[:, None, None])
    )
    masked = jnp.where(visible, scores, -1e30)
    newest_max = jnp.maximum(running_max, jnp.max(masked, axis=2))
    weights = jnp.where(visible, jnp.exp(scores - newest_max[:, :, None]), 0.0).astype(jnp.bfloat16)
    row_total = jnp.sum(weights.astype(jnp.float32), axis=2)
    accumulated = jnp.einsum(
        "hqk,khd->hqd", weights, value_heads, preferred_element_type=jnp.float32
    )
    return (newest_max, row_total, accumulated)


def per_device(
    queries,
    key_vectors,
    values,
    lookback,
    residual,
    out_weight,
    branch_gate,
    final_shift,
    final_scale,
    final_weight,
    decoder_kernel,
    decoder_bias,
):
    slab_rows = queries.shape[0]
    head_count = queries.shape[1] // DH
    blocks = lax.axis_size("blk")
    block_index = lax.axis_index("blk")
    frame_len = slab_rows * blocks // FRAMES
    query_heads = queries.reshape(slab_rows, head_count, DH)
    query_frame = (block_index * slab_rows + jnp.arange(slab_rows, dtype=jnp.int32)) // frame_len
    lookback_heads = lax.dynamic_slice_in_dim(
        lookback, lax.axis_index(("head", "dec")) * head_count, head_count
    )
    initial = (
        jnp.full((head_count, slab_rows), -1e30, jnp.float32),
        jnp.zeros((head_count, slab_rows), jnp.float32),
        jnp.zeros((head_count, slab_rows, DH), jnp.float32),
    )
    carry = attend_block(
        initial,
        (
            lax.all_gather(key_vectors, "blk", axis=0, tiled=True),
            lax.all_gather(values, "blk", axis=0, tiled=True),
        ),
        query_heads,
        query_frame,
        lookback_heads,
        frame_len,
    )
    newest_max, row_total, accumulated = carry
    attended = (
        (accumulated / row_total[:, :, None])
        .transpose(1, 0, 2)
        .reshape(slab_rows, head_count * DH)
        .astype(jnp.bfloat16)
    )
    tokens_dev = slab_rows // lax.axis_size(("head", "dec"))
    projected = lax.psum_scatter(
        jnp.dot(attended, out_weight, preferred_element_type=jnp.float32).astype(jnp.bfloat16),
        ("head", "dec"),
        scatter_dimension=0,
        tiled=True,
    ).astype(jnp.float32)
    hidden = residual.astype(jnp.float32) + branch_gate[None, :] * projected
    center = jnp.mean(hidden, axis=1, keepdims=True)
    spread = jnp.mean((hidden - center) ** 2, axis=1, keepdims=True)
    normed = (
        (hidden - center) * lax.rsqrt(spread + 1e-06) * (1.0 + final_scale[None, :])
        + final_shift[None, :]
    ).astype(jnp.bfloat16)
    patches = jnp.dot(normed, final_weight, preferred_element_type=jnp.float32).astype(jnp.bfloat16)
    patch_rows = tokens_dev // PW
    tile_rows = 2 * patch_rows
    width = 2 * PW
    tile = (
        patches.reshape(patch_rows, PW, 2, 2, LC)
        .transpose(0, 2, 1, 3, 4)
        .reshape(tile_rows, width * LC)
    )
    padded = padded_2(tile, ((("blk", "head", "dec"), 0),), 1)
    frame_stride = blocks // FRAMES
    frame_index = block_index // frame_stride
    prior_one = from_behind(padded, "blk", frame_stride)
    prior_one = jnp.where(frame_index >= 1, prior_one, padded)
    prior_two = from_behind(prior_one, "blk", frame_stride)
    prior_two = jnp.where(frame_index >= 1, prior_two, padded)
    history = jnp.stack([prior_two, prior_one, padded]).reshape(3, tile_rows + 2, width, LC)
    history = jnp.pad(history, ((0, 0), (0, 0), (1, 1), (0, 0)))
    windows = [
        history[time_tap, row_tap : row_tap + tile_rows, column_tap : column_tap + width, :]
        for time_tap in range(3)
        for row_tap in range(3)
        for column_tap in range(3)
    ]
    columns = jnp.concatenate(windows, axis=-1).reshape(tile_rows * width, 27 * LC)
    summed = (
        jnp.dot(columns, decoder_kernel, preferred_element_type=jnp.float32) + decoder_bias[None, :]
    )
    return summed.astype(jnp.bfloat16).reshape(tile_rows, width, decoder_kernel.shape[1])


HIGH = 3
CHUNKS = 4
MESH = pl.DeviceIdType.MESH


def fused_kernel(
    q_hbm, k_hbm, v_hbm, lookback, res_hbm, w_hbm, gate_hbm, shift_hbm, scale_hbm, fw_hbm, dk_hbm, db_hbm,
    out_ref,
    kz, kx, qv, wv, resv, gatev, shiftv, scalev, fwv, dkv, dbv,
    top, total, acc, att, part, from_dec, to_y, from_y, hid, halo, wide, canvas,
    load_sem, kv_sem, zs, zr, xs, xr, ds, dr, ys, yr, hs, hr,
):
    f = lax.axis_index("blk")
    hd = lax.axis_index("head")
    dc = lax.axis_index("dec")
    z, x = f // 2, f % 2
    n = f * 4 + hd * 2 + dc
    slab = q_hbm.shape[0]
    columns = w_hbm.shape[1] // CHUNKS

    kv_loads = []
    for h in range(HIGH):
        for which, src in enumerate((k_hbm, v_hbm)):
            kv_loads.append(
                pltpu.make_async_copy(
                    src.at[:, pl.ds(h * DH, DH)], kz.at[0, h, which], kv_sem.at[2 * h + which]
                )
            )
    loads = [
        pltpu.make_async_copy(src, dst, load_sem.at[i])
        for i, (src, dst) in enumerate(
            (
                (q_hbm, qv), (dk_hbm, dkv), (w_hbm, wv), (res_hbm, resv), (gate_hbm, gatev),
                (shift_hbm, shiftv), (scale_hbm, scalev), (fw_hbm, fwv), (db_hbm, dbv),
            )
        )
    ]
    for c in kv_loads + loads:
        c.start()

    def up(j, h):
        return pltpu.make_async_remote_copy(
            src_ref=kz.at[j, h], dst_ref=kz.at[j + 1, h], send_sem=zs.at[j, h], recv_sem=zr.at[j + 1, h],
            device_id=(f + 2, hd, dc), device_id_type=MESH,
        )

    def across(j, h):
        return pltpu.make_async_remote_copy(
            src_ref=kz.at[j + x, h], dst_ref=kx.at[j, h], send_sem=xs.at[j, h], recv_sem=xr.at[j, h],
            device_id=(f + 1 - 2 * x, hd, dc), device_id_type=MESH,
        )

    def up_goes(j):
        return (z >= j) & (z < 3) & ((x == 1) | (j < 2))

    def up_comes(j):
        return (z >= j) & ((x == 1) | (j < 3))

    def across_goes(j):
        return z >= j + x

    def across_comes(j):
        return z >= j + 1 - x

    for h in range(HIGH):
        kv_loads[2 * h].wait()
        kv_loads[2 * h + 1].wait()

        @pl.when(up_goes(0))
        def _():
            up(0, h).start()

        @pl.when(x == 0)
        def _():
            across(0, h).start()

    def attend(h, key, value, distance):
        query = qv[:, h * DH : (h + 1) * DH]
        scores = lax.dot_general(
            query, key, (((1,), (1,)), ((), ())), preferred_element_type=jnp.float32
        ) * DH ** (-0.5)
        if distance == 0:
            newest = jnp.max(scores, axis=1, keepdims=True)
        else:
            seen = lookback[(hd * 2 + dc) * HIGH + h] >= distance
            scores = scores + jnp.where(seen, 0.0, -1e30)
            newest = jnp.maximum(top[h], jnp.max(scores, axis=1, keepdims=True))
        weights = jnp.exp(scores - newest).astype(jnp.bfloat16)
        added = jnp.sum(weights.astype(jnp.float32), axis=1, keepdims=True)
        mixed = jnp.dot(weights, value, preferred_element_type=jnp.float32)
        if distance == 0:
            total[h] = added
            acc[h] = mixed
        else:
            shrink = jnp.exp(top[h] - newest)
            total[h] = total[h] * shrink + added
            acc[h] = acc[h] * shrink + mixed
        top[h] = newest

    loads[0].wait()
    for h in range(HIGH):
        attend(h, kz[0, h, 0], kz[0, h, 1], 0)

    loads[1].wait()
    wide[...] = jnp.zeros_like(wide)
    for a in range(2):
        for b in range(2):
            for t in range(3):
                for i in range(3):
                    for j in range(3):
                        ya, xb = a + i - 1, b + j - 1
                        row = ((t * 2 + ya // 2 - (a - 1)) * 2 + xb // 2 - (b - 1)) * 64
                        row += ((ya % 2) * 2 + xb % 2) * LC
                        tap = (t * 3 + i) * 3 + j
                        wide[a * 2 + b, row : row + LC, :] = dkv[tap * LC : (tap + 1) * LC, :]

    def z_part(j, h):
        @pl.when(up_comes(j))
        def _():
            up(j - 1, h).wait_recv()
            if j <= 2:

                @pl.when(up_goes(j))
                def _():
                    up(j, h).start()

                @pl.when(x == 0)
                def _():
                    across(j, h).start()

            @pl.when(x == 1)
            def _():
                across(j - 1, h).start()

            if j <= 2:
                attend(h, kz[j, h, 0], kz[j, h, 1], 2 * j)

    def x_part(j, h):
        @pl.when(across_comes(j))
        def _():
            across(j, h).wait_recv()
            attend(h, kx[j, h, 0], kx[j, h, 1], 2 * j + 1)

    order = [(j, h) for j in range(1, 4) for h in range(HIGH)]
    for place, (j, h) in enumerate(order):
        z_part(j, h)
        if place:
            x_part(order[place - 1][0] - 1, order[place - 1][1])
    x_part(order[-1][0] - 1, order[-1][1])

    for h in range(HIGH):
        att[:, h * DH : (h + 1) * DH] = (acc[h] / total[h]).astype(jnp.bfloat16)

    def to_core(c):
        return pltpu.make_async_remote_copy(
            src_ref=part.at[c, :, 1 - dc], dst_ref=from_dec.at[c], send_sem=ds.at[c], recv_sem=dr.at[c],
            device_id=(f, hd, 1 - dc), device_id_type=MESH,
        )

    def to_row(c):
        return pltpu.make_async_remote_copy(
            src_ref=to_y.at[c], dst_ref=from_y.at[c], send_sem=ys.at[c], recv_sem=yr.at[c],
            device_id=(f, 1 - hd, dc), device_id_type=MESH,
        )

    loads[2].wait()
    for c in range(CHUNKS):
        share = jnp.dot(
            att[...], wv[:, c * columns : (c + 1) * columns], preferred_element_type=jnp.float32
        ).astype(jnp.bfloat16)
        part[c] = share.reshape(2, 2, slab // 4, columns)
        to_core(c).start()
    for c in range(CHUNKS):
        to_core(c).wait_recv()
        to_y[c] = (
            part[c, 1 - hd, dc].astype(jnp.float32) + from_dec[c, 1 - hd].astype(jnp.float32)
        ).astype(jnp.bfloat16)
        to_row(c).start()
    for load in loads[3:]:
        load.wait()
    summed = jnp.zeros((slab // 4, 1), jnp.float32)
    for c in range(CHUNKS):
        cols = slice(c * columns, (c + 1) * columns)
        mine = part[c, hd, dc].astype(jnp.float32) + from_dec[c, hd].astype(jnp.float32)
        to_row(c).wait_recv()
        hidden = resv[:, cols].astype(jnp.float32) + gatev[:, cols] * (mine + from_y[c].astype(jnp.float32))
        hid[c] = hidden
        summed = summed + jnp.sum(hidden, axis=1, keepdims=True)
    center = summed / (CHUNKS * columns)
    squares = jnp.zeros((slab // 4, 1), jnp.float32)
    for c in range(CHUNKS):
        squares = squares + jnp.sum((hid[c] - center) ** 2, axis=1, keepdims=True)
    inverse = lax.rsqrt(squares / (CHUNKS * columns) + 1e-06)
    patches = jnp.zeros((slab // 4, fwv.shape[1]), jnp.float32)
    for c in range(CHUNKS):
        cols = slice(c * columns, (c + 1) * columns)
        normed = ((hid[c] - center) * inverse * (1.0 + scalev[:, cols]) + shiftv[:, cols]).astype(jnp.bfloat16)
        patches = patches + jnp.dot(normed, fwv[cols, :], preferred_element_type=jnp.float32)
    halo[0, 1] = jnp.concatenate([patches, patches], axis=1).astype(jnp.bfloat16)

    def tile_to(back, side):
        m = n + 4 * back - side
        copy = pltpu.make_async_remote_copy(
            src_ref=halo.at[0, 1], dst_ref=halo.at[back, side + 1],
            send_sem=hs.at[back, side + 1], recv_sem=hr.at[back, side + 1],
            device_id=(m // 4, (m % 4) // 2, m % 2), device_id_type=MESH,
        )
        return copy, (m >= 4 * back) & (m < 32)

    def tile_comes(back, side):
        source = n - 4 * back + side
        return (f >= back) & (source >= 0) & (source < 32)

    reach = [(back, side) for back in (2, 1, 0) for side in (-1, 0, 1) if (back, side) != (0, 0)]
    for back, side in reach:
        copy, goes = tile_to(back, side)

        @pl.when(goes)
        def _():
            copy.start()

    for back, side in reach:

        @pl.when(tile_comes(back, side))
        def _():
            tile_to(back, side)[0].wait_recv()

    rows = 4 * PW
    lane = lax.broadcasted_iota(jnp.int32, (rows, 128), 1)
    token = lax.broadcasted_iota(jnp.int32, (rows, 128), 0) % PW
    pairs = []
    for t in range(3):
        back = jnp.minimum(2 - t, f)
        first = n - 4 * back
        above = jnp.where(first >= 1, halo[back, 0, PW:, :].astype(jnp.float32), 0.0)
        below = jnp.where(first <= 30, halo[back, 2, :PW, :].astype(jnp.float32), 0.0)
        ext = jnp.concatenate([above, halo[back, 1].astype(jnp.float32), below], axis=0)
        before = jnp.where(token == 0, 0.0, pltpu.roll(ext, 1, 0))
        after = jnp.where(token == PW - 1, 0.0, pltpu.roll(ext, rows - 1, 0))
        pairs.append(
            (
                jnp.where(lane < 64, before, ext).astype(jnp.bfloat16),
                jnp.where(lane < 64, ext, after).astype(jnp.bfloat16),
            )
        )
    for a in range(2):
        for b in range(2):
            lhs = jnp.concatenate(
                [
                    pairs[t][b][(a + d) * PW : (a + d) * PW + 2 * PW]
                    for t in range(3)
                    for d in range(2)
                ],
                axis=1,
            )
            got = jnp.dot(lhs, wide[a * 2 + b], preferred_element_type=jnp.float32) + dbv[...]
            for r in range(2):
                for g in range(got.shape[1] // 128):
                    canvas[g, pl.ds((2 * r + a) * 2 * PW + b, PW, stride=2), :] = got[
                        r * PW : (r + 1) * PW, g * 128 : (g + 1) * 128
                    ]
    for y in range(4):
        for g in range(canvas.shape[0]):
            out_ref[y, :, g * 128 : (g + 1) * 128] = canvas[g, y * 2 * PW : (y + 1) * 2 * PW, :].astype(jnp.bfloat16)

    for j in range(3):
        for h in range(HIGH):

            @pl.when(up_goes(j))
            def _():
                up(j, h).wait_send()

            @pl.when(across_goes(j))
            def _():
                across(j, h).wait_send()

    for c in range(CHUNKS):
        to_core(c).wait_send()
        to_row(c).wait_send()
    for back, side in reach:
        copy, goes = tile_to(back, side)

        @pl.when(goes)
        def _():
            copy.wait_send()


def fused(
    queries, key_vectors, values, lookback, residual, out_weight,
    branch_gate, final_shift, final_scale, final_weight, decoder_kernel, decoder_bias,
):
    slab, width = queries.shape
    model = out_weight.shape[1]
    quarter, columns = slab // 4, model // CHUNKS
    outputs = decoder_kernel.shape[1]
    bf, f32 = jnp.bfloat16, jnp.float32
    vm, dma = pltpu.VMEM, pltpu.SemaphoreType.DMA
    hbm = pl.BlockSpec(memory_space=pl.ANY)
    return pl.pallas_call(
        fused_kernel,
        out_shape=jax.ShapeDtypeStruct((4, 2 * PW, outputs), bf),
        in_specs=[hbm] * 3 + [pl.BlockSpec(memory_space=pltpu.SMEM)] + [hbm] * 8,
        out_specs=pl.BlockSpec(memory_space=pltpu.VMEM),
        scratch_shapes=[
            vm((4, HIGH, 2, slab, DH), bf), vm((3, HIGH, 2, slab, DH), bf), vm((slab, width), bf),
            vm((width, model), bf), vm((quarter, model), bf),
            vm((1, model), f32), vm((1, model), f32), vm((1, model), f32),
            vm(final_weight.shape, bf), vm(decoder_kernel.shape, bf), vm((1, outputs), f32),
            vm((HIGH, slab, 1), f32), vm((HIGH, slab, 1), f32), vm((HIGH, slab, DH), f32),
            vm((slab, width), bf), vm((CHUNKS, 2, 2, quarter, columns), bf),
            vm((CHUNKS, 2, quarter, columns), bf), vm((CHUNKS, quarter, columns), bf),
            vm((CHUNKS, quarter, columns), bf), vm((CHUNKS, quarter, columns), f32),
            vm((3, 3, quarter, 128), bf), vm((4, 768, outputs), bf), vm((outputs // 128, 256, 128), f32),
            dma((9,)), dma((6,)), dma((3, HIGH)), dma((4, HIGH)), dma((3, HIGH)), dma((3, HIGH)),
            dma((CHUNKS,)), dma((CHUNKS,)), dma((CHUNKS,)), dma((CHUNKS,)), dma((3, 3)), dma((3, 3)),
        ],
        compiler_params=pltpu.CompilerParams(has_side_effects=True, vmem_limit_bytes=48 * 1024 * 1024),
    )(
        queries, key_vectors, values, lookback, residual, out_weight,
        branch_gate.reshape(1, -1), final_shift.reshape(1, -1), final_scale.reshape(1, -1),
        final_weight, decoder_kernel, decoder_bias.reshape(1, -1),
    )


def one_slab_a_frame(mesh):
    return (mesh.shape["blk"], mesh.shape["head"], mesh.shape["dec"]) == (FRAMES, 2, 2)


def solution(mesh):
    in_specs = (
        P("blk", ("head", "dec")),
        P("blk", ("head", "dec")),
        P("blk", ("head", "dec")),
        P(),
        P(("blk", "head", "dec"), None),
        P(("head", "dec"), None),
        P(),
        P(),
        P(),
        P(),
        P(),
        P(),
    )
    out_specs = P(("blk", "head", "dec"), None, None)
    body = fused if one_slab_a_frame(mesh) else per_device
    return jax.shard_map(
        body, mesh=mesh, in_specs=in_specs, out_specs=out_specs, check_vma=False
    )
```

```python
import jax
import jax.numpy as jnp
from jax import lax
from jax.experimental import pallas as pl
from jax.experimental.pallas import tpu as pltpu
from jax.sharding import PartitionSpec as P

DH = 128
LC = 16
FRAMES = 8
PW = 32


def padded_2(cells, sides, width):
    for axis, dim in sides:
        count = lax.axis_size(axis)
        ends = count - 1
        head = lax.slice_in_dim(cells, 0, width, axis=dim)
        tail = lax.slice_in_dim(cells, cells.shape[dim] - width, cells.shape[dim], axis=dim)
        cells = jnp.concatenate(
            [
                lax.ppermute(tail, axis, [(i, (i + 1) % count) for i in range(ends)]),
                cells,
                lax.ppermute(head, axis, [((i + 1) % count, i) for i in range(ends)]),
            ],
            axis=dim,
        )
    return cells


def from_behind(x, axis, by):
    peers = lax.axis_size(axis)
    pairs = [(i, i + by) for i in range(peers) if 0 <= i + by < peers]
    return lax.ppermute(x, axis, pairs)


def attend_block(carry, shard_pair, query_heads, query_frame, lookback_heads, frame_len):
    running_max, row_total, accumulated = carry
    key_block, value_block = shard_pair
    key_count = key_block.shape[0]
    head_count = query_heads.shape[1]
    key_heads = key_block.reshape(key_count, head_count, DH)
    value_heads = value_block.reshape(key_count, head_count, DH)
    scores = jnp.einsum(
        "qhd,khd->hqk", query_heads, key_heads, preferred_element_type=jnp.float32
    ) * DH ** (-0.5)
    key_pos = jnp.arange(key_count, dtype=jnp.int32)
    key_frame = key_pos // frame_len
    visible = (
        (key_pos >= 0)[None, None, :]
        & (key_frame[None, None, :] <= query_frame[None, :, None])
        & (key_frame[None, None, :] >= query_frame[None, :, None] - lookback_heads[:, None, None])
    )
    masked = jnp.where(visible, scores, -1e30)
    newest_max = jnp.maximum(running_max, jnp.max(masked, axis=2))
    weights = jnp.where(visible, jnp.exp(scores - newest_max[:, :, None]), 0.0).astype(jnp.bfloat16)
    row_total = jnp.sum(weights.astype(jnp.float32), axis=2)
    accumulated = jnp.einsum(
        "hqk,khd->hqd", weights, value_heads, preferred_element_type=jnp.float32
    )
    return (newest_max, row_total, accumulated)


def per_device(
    queries,
    key_vectors,
    values,
    lookback,
    residual,
    out_weight,
    branch_gate,
    final_shift,
    final_scale,
    final_weight,
    decoder_kernel,
    decoder_bias,
):
    slab_rows = queries.shape[0]
    head_count = queries.shape[1] // DH
    blocks = lax.axis_size("blk")
    block_index = lax.axis_index("blk")
    frame_len = slab_rows * blocks // FRAMES
    query_heads = queries.reshape(slab_rows, head_count, DH)
    query_frame = (block_index * slab_rows + jnp.arange(slab_rows, dtype=jnp.int32)) // frame_len
    lookback_heads = lax.dynamic_slice_in_dim(
        lookback, lax.axis_index(("head", "dec")) * head_count, head_count
    )
    initial = (
        jnp.full((head_count, slab_rows), -1e30, jnp.float32),
        jnp.zeros((head_count, slab_rows), jnp.float32),
        jnp.zeros((head_count, slab_rows, DH), jnp.float32),
    )
    carry = attend_block(
        initial,
        (
            lax.all_gather(key_vectors, "blk", axis=0, tiled=True),
            lax.all_gather(values, "blk", axis=0, tiled=True),
        ),
        query_heads,
        query_frame,
        lookback_heads,
        frame_len,
    )
    newest_max, row_total, accumulated = carry
    attended = (
        (accumulated / row_total[:, :, None])
        .transpose(1, 0, 2)
        .reshape(slab_rows, head_count * DH)
        .astype(jnp.bfloat16)
    )
    tokens_dev = slab_rows // lax.axis_size(("head", "dec"))
    projected = lax.psum_scatter(
        jnp.dot(attended, out_weight, preferred_element_type=jnp.float32).astype(jnp.bfloat16),
        ("head", "dec"),
        scatter_dimension=0,
        tiled=True,
    ).astype(jnp.float32)
    hidden = residual.astype(jnp.float32) + branch_gate[None, :] * projected
    center = jnp.mean(hidden, axis=1, keepdims=True)
    spread = jnp.mean((hidden - center) ** 2, axis=1, keepdims=True)
    normed = (
        (hidden - center) * lax.rsqrt(spread + 1e-06) * (1.0 + final_scale[None, :])
        + final_shift[None, :]
    ).astype(jnp.bfloat16)
    patches = jnp.dot(normed, final_weight, preferred_element_type=jnp.float32).astype(jnp.bfloat16)
    patch_rows = tokens_dev // PW
    tile_rows = 2 * patch_rows
    width = 2 * PW
    tile = (
        patches.reshape(patch_rows, PW, 2, 2, LC)
        .transpose(0, 2, 1, 3, 4)
        .reshape(tile_rows, width * LC)
    )
    padded = padded_2(tile, ((("blk", "head", "dec"), 0),), 1)
    frame_stride = blocks // FRAMES
    frame_index = block_index // frame_stride
    prior_one = from_behind(padded, "blk", frame_stride)
    prior_one = jnp.where(frame_index >= 1, prior_one, padded)
    prior_two = from_behind(prior_one, "blk", frame_stride)
    prior_two = jnp.where(frame_index >= 1, prior_two, padded)
    history = jnp.stack([prior_two, prior_one, padded]).reshape(3, tile_rows + 2, width, LC)
    history = jnp.pad(history, ((0, 0), (0, 0), (1, 1), (0, 0)))
    windows = [
        history[time_tap, row_tap : row_tap + tile_rows, column_tap : column_tap + width, :]
        for time_tap in range(3)
        for row_tap in range(3)
        for column_tap in range(3)
    ]
    columns = jnp.concatenate(windows, axis=-1).reshape(tile_rows * width, 27 * LC)
    summed = (
        jnp.dot(columns, decoder_kernel, preferred_element_type=jnp.float32) + decoder_bias[None, :]
    )
    return summed.astype(jnp.bfloat16).reshape(tile_rows, width, decoder_kernel.shape[1])


HIGH = 3
CHUNKS = 4
MESH = pl.DeviceIdType.MESH


def fused_kernel(
    q_hbm, k_hbm, v_hbm, look_hbm, res_hbm, w_hbm, gate_hbm, shift_hbm, scale_hbm, fw_hbm, dk_hbm, db_hbm,
    out_ref,
    lookback, kz, kx, qv, wv, resv, gatev, shiftv, scalev, fwv, dkv, dbv,
    top, total, acc, att, part, from_dec, to_y, from_y, hid, halo, wide, canvas,
    load_sem, kv_sem, zs, zr, xs, xr, ds, dr, ys, yr, hs, hr,
):
    f = lax.axis_index("blk")
    hd = lax.axis_index("head")
    dc = lax.axis_index("dec")
    z, x = f // 2, f % 2
    n = f * 4 + hd * 2 + dc
    slab = q_hbm.shape[0]
    columns = w_hbm.shape[1] // CHUNKS

    barrier = pltpu.get_barrier_semaphore()
    greeted = jnp.int32(1)
    pl.semaphore_signal(barrier, inc=1, device_id=(f, 1 - hd, dc), device_id_type=MESH)
    for apart in (1, 3, 4, 5, 7, 8, 9):
        for m in (n - apart, n + apart):
            there = (m >= 0) & (m < 32)
            greeted = greeted + jnp.where(there, 1, 0)

            @pl.when(there)
            def _():
                pl.semaphore_signal(
                    barrier, inc=1, device_id=(m // 4, (m % 4) // 2, m % 2), device_id_type=MESH
                )

    kv_loads = []
    for h in range(HIGH):
        for which, src in enumerate((k_hbm, v_hbm)):
            kv_loads.append(
                pltpu.make_async_copy(
                    src.at[:, pl.ds(h * DH, DH)], kz.at[0, h, which], kv_sem.at[2 * h + which]
                )
            )
    loads = [
        pltpu.make_async_copy(src, dst, load_sem.at[i])
        for i, (src, dst) in enumerate(
            (
                (q_hbm, qv), (dk_hbm, dkv), (look_hbm, lookback), (w_hbm, wv), (res_hbm, resv), (gate_hbm, gatev),
                (shift_hbm, shiftv), (scale_hbm, scalev), (fw_hbm, fwv), (db_hbm, dbv),
            )
        )
    ]
    for c in kv_loads + loads:
        c.start()

    def up(j, h):
        return pltpu.make_async_remote_copy(
            src_ref=kz.at[j, h], dst_ref=kz.at[j + 1, h], send_sem=zs.at[j, h], recv_sem=zr.at[j + 1, h],
            device_id=(f + 2, hd, dc), device_id_type=MESH,
        )

    def across(j, h):
        return pltpu.make_async_remote_copy(
            src_ref=kz.at[j + x, h], dst_ref=kx.at[j, h], send_sem=xs.at[j, h], recv_sem=xr.at[j, h],
            device_id=(f + 1 - 2 * x, hd, dc), device_id_type=MESH,
        )

    def up_goes(j):
        return (z >= j) & (z < 3) & ((x == 1) | (j < 2))

    def up_comes(j):
        return (z >= j) & ((x == 1) | (j < 3))

    def across_goes(j):
        return z >= j + x

    def across_comes(j):
        return z >= j + 1 - x

    for c in kv_loads:
        c.wait()
    pl.semaphore_wait(barrier, greeted)

    for h in range(HIGH):
        @pl.when(up_goes(0))
        def _():
            up(0, h).start()

        @pl.when(x == 0)
        def _():
            across(0, h).start()

    def attend(h, key, value, distance):
        query = qv[:, h * DH : (h + 1) * DH]
        scores = lax.dot_general(
            query, key, (((1,), (1,)), ((), ())), preferred_element_type=jnp.float32
        ) * DH ** (-0.5)
        if distance == 0:
            newest = jnp.max(scores, axis=1, keepdims=True)
        else:
            seen = lookback[0, (hd * 2 + dc) * HIGH + h] >= distance
            scores = scores + jnp.where(seen, 0.0, -1e30)
            newest = jnp.maximum(top[h], jnp.max(scores, axis=1, keepdims=True))
        weights = jnp.exp(scores - newest).astype(jnp.bfloat16)
        added = jnp.sum(weights.astype(jnp.float32), axis=1, keepdims=True)
        mixed = jnp.dot(weights, value, preferred_element_type=jnp.float32)
        if distance == 0:
            total[h] = added
            acc[h] = mixed
        else:
            shrink = jnp.exp(top[h] - newest)
            total[h] = total[h] * shrink + added
            acc[h] = acc[h] * shrink + mixed
        top[h] = newest

    loads[0].wait()
    for h in range(HIGH):
        attend(h, kz[0, h, 0], kz[0, h, 1], 0)

    loads[1].wait()
    loads[2].wait()
    wide[...] = jnp.zeros_like(wide)
    for a in range(2):
        for b in range(2):
            for t in range(3):
                for i in range(3):
                    for j in range(3):
                        ya, xb = a + i - 1, b + j - 1
                        row = ((t * 2 + ya // 2 - (a - 1)) * 2 + xb // 2 - (b - 1)) * 64
                        row += ((ya % 2) * 2 + xb % 2) * LC
                        tap = (t * 3 + i) * 3 + j
                        wide[a * 2 + b, row : row + LC, :] = dkv[tap * LC : (tap + 1) * LC, :]

    def z_part(j, h):
        @pl.when(up_comes(j))
        def _():
            up(j - 1, h).wait_recv()
            if j <= 2:

                @pl.when(up_goes(j))
                def _():
                    up(j, h).start()

                @pl.when(x == 0)
                def _():
                    across(j, h).start()

            @pl.when(x == 1)
            def _():
                across(j - 1, h).start()

            if j <= 2:
                attend(h, kz[j, h, 0], kz[j, h, 1], 2 * j)

    def x_part(j, h):
        @pl.when(across_comes(j))
        def _():
            across(j, h).wait_recv()
            attend(h, kx[j, h, 0], kx[j, h, 1], 2 * j + 1)

    order = [(j, h) for j in range(1, 4) for h in range(HIGH)]
    for place, (j, h) in enumerate(order):
        z_part(j, h)
        if place:
            x_part(order[place - 1][0] - 1, order[place - 1][1])
    x_part(order[-1][0] - 1, order[-1][1])

    for h in range(HIGH):
        att[:, h * DH : (h + 1) * DH] = (acc[h] / total[h]).astype(jnp.bfloat16)

    def to_core(c):
        return pltpu.make_async_remote_copy(
            src_ref=part.at[c, :, 1 - dc], dst_ref=from_dec.at[c], send_sem=ds.at[c], recv_sem=dr.at[c],
            device_id=(f, hd, 1 - dc), device_id_type=MESH,
        )

    def to_row(c):
        return pltpu.make_async_remote_copy(
            src_ref=to_y.at[c], dst_ref=from_y.at[c], send_sem=ys.at[c], recv_sem=yr.at[c],
            device_id=(f, 1 - hd, dc), device_id_type=MESH,
        )

    loads[3].wait()
    for c in range(CHUNKS):
        share = jnp.dot(
            att[...], wv[:, c * columns : (c + 1) * columns], preferred_element_type=jnp.float32
        ).astype(jnp.bfloat16)
        part[c] = share.reshape(2, 2, slab // 4, columns)
        to_core(c).start()
    for c in range(CHUNKS):
        to_core(c).wait_recv()
        to_y[c] = (
            part[c, 1 - hd, dc].astype(jnp.float32) + from_dec[c, 1 - hd].astype(jnp.float32)
        ).astype(jnp.bfloat16)
        to_row(c).start()
    for load in loads[4:]:
        load.wait()
    summed = jnp.zeros((slab // 4, 1), jnp.float32)
    for c in range(CHUNKS):
        cols = slice(c * columns, (c + 1) * columns)
        mine = part[c, hd, dc].astype(jnp.float32) + from_dec[c, hd].astype(jnp.float32)
        to_row(c).wait_recv()
        hidden = resv[:, cols].astype(jnp.float32) + gatev[:, cols] * (mine + from_y[c].astype(jnp.float32))
        hid[c] = hidden
        summed = summed + jnp.sum(hidden, axis=1, keepdims=True)
    center = summed / (CHUNKS * columns)
    squares = jnp.zeros((slab // 4, 1), jnp.float32)
    for c in range(CHUNKS):
        squares = squares + jnp.sum((hid[c] - center) ** 2, axis=1, keepdims=True)
    inverse = lax.rsqrt(squares / (CHUNKS * columns) + 1e-06)
    patches = jnp.zeros((slab // 4, fwv.shape[0]), jnp.float32)
    for c in range(CHUNKS):
        cols = slice(c * columns, (c + 1) * columns)
        normed = ((hid[c] - center) * inverse * (1.0 + scalev[:, cols]) + shiftv[:, cols]).astype(jnp.bfloat16)
        patches = patches + lax.dot_general(
            normed, fwv[:, cols], (((1,), (1,)), ((), ())), preferred_element_type=jnp.float32
        )
    halo[0, 1] = jnp.concatenate([patches, patches], axis=1).astype(jnp.bfloat16)

    def tile_to(back, side):
        m = n + 4 * back - side
        copy = pltpu.make_async_remote_copy(
            src_ref=halo.at[0, 1], dst_ref=halo.at[back, side + 1],
            send_sem=hs.at[back, side + 1], recv_sem=hr.at[back, side + 1],
            device_id=(m // 4, (m % 4) // 2, m % 2), device_id_type=MESH,
        )
        return copy, (m >= 4 * back) & (m < 32)

    def tile_comes(back, side):
        source = n - 4 * back + side
        return (f >= back) & (source >= 0) & (source < 32)

    reach = [(back, side) for back in (2, 1, 0) for side in (-1, 0, 1) if (back, side) != (0, 0)]
    for back, side in reach:
        copy, goes = tile_to(back, side)

        @pl.when(goes)
        def _():
            copy.start()

    for back, side in reach:

        @pl.when(tile_comes(back, side))
        def _():
            tile_to(back, side)[0].wait_recv()

    rows = 4 * PW
    lane = lax.broadcasted_iota(jnp.int32, (rows, 128), 1)
    token = lax.broadcasted_iota(jnp.int32, (rows, 128), 0) % PW
    pairs = []
    for t in range(3):
        back = jnp.minimum(2 - t, f)
        first = n - 4 * back
        above = jnp.where(first >= 1, halo[back, 0, PW:, :].astype(jnp.float32), 0.0)
        below = jnp.where(first <= 30, halo[back, 2, :PW, :].astype(jnp.float32), 0.0)
        ext = jnp.concatenate([above, halo[back, 1].astype(jnp.float32), below], axis=0)
        before = jnp.where(token == 0, 0.0, pltpu.roll(ext, 1, 0))
        after = jnp.where(token == PW - 1, 0.0, pltpu.roll(ext, rows - 1, 0))
        pairs.append(
            (
                jnp.where(lane < 64, before, ext).astype(jnp.bfloat16),
                jnp.where(lane < 64, ext, after).astype(jnp.bfloat16),
            )
        )
    for a in range(2):
        for b in range(2):
            lhs = jnp.concatenate(
                [
                    pairs[t][b][(a + d) * PW : (a + d) * PW + 2 * PW]
                    for t in range(3)
                    for d in range(2)
                ],
                axis=1,
            )
            got = jnp.dot(lhs, wide[a * 2 + b], preferred_element_type=jnp.float32) + dbv[...]
            for r in range(2):
                for g in range(got.shape[1] // 128):
                    canvas[g, pl.ds((2 * r + a) * 2 * PW + b, PW, stride=2), :] = got[
                        r * PW : (r + 1) * PW, g * 128 : (g + 1) * 128
                    ]
    for y in range(4):
        for g in range(canvas.shape[0]):
            out_ref[y, :, g * 128 : (g + 1) * 128] = canvas[g, y * 2 * PW : (y + 1) * 2 * PW, :].astype(jnp.bfloat16)

    for j in range(3):
        for h in range(HIGH):

            @pl.when(up_goes(j))
            def _():
                up(j, h).wait_send()

            @pl.when(across_goes(j))
            def _():
                across(j, h).wait_send()

    for c in range(CHUNKS):
        to_core(c).wait_send()
        to_row(c).wait_send()
    for back, side in reach:
        copy, goes = tile_to(back, side)

        @pl.when(goes)
        def _():
            copy.wait_send()


def fused(
    queries, key_vectors, values, lookback, residual, out_weight,
    branch_gate, final_shift, final_scale, final_weight, decoder_kernel, decoder_bias,
):
    slab, width = queries.shape
    model = out_weight.shape[1]
    quarter, columns = slab // 4, model // CHUNKS
    outputs = decoder_kernel.shape[1]
    bf, f32 = jnp.bfloat16, jnp.float32
    vm, dma = pltpu.VMEM, pltpu.SemaphoreType.DMA
    hbm = pl.BlockSpec(memory_space=pltpu.HBM)
    return pl.pallas_call(
        fused_kernel,
        out_shape=jax.ShapeDtypeStruct((4, 2 * PW, outputs), bf),
        in_specs=[hbm] * 12,
        out_specs=pl.BlockSpec(memory_space=pltpu.VMEM),
        scratch_shapes=[
            pltpu.SMEM((1, lookback.shape[0]), jnp.int32),
            vm((4, HIGH, 2, slab, DH), bf), vm((3, HIGH, 2, slab, DH), bf), vm((slab, width), bf),
            vm((width, model), bf), vm((quarter, model), bf),
            vm((1, model), f32), vm((1, model), f32), vm((1, model), f32),
            vm(final_weight.shape[::-1], bf), vm(decoder_kernel.shape, bf), vm((1, outputs), f32),
            vm((HIGH, slab, 1), f32), vm((HIGH, slab, 1), f32), vm((HIGH, slab, DH), f32),
            vm((slab, width), bf), vm((CHUNKS, 2, 2, quarter, columns), bf),
            vm((CHUNKS, 2, quarter, columns), bf), vm((CHUNKS, quarter, columns), bf),
            vm((CHUNKS, quarter, columns), bf), vm((CHUNKS, quarter, columns), f32),
            vm((3, 3, quarter, 128), bf), vm((4, 768, outputs), bf), vm((outputs // 128, 256, 128), f32),
            dma((10,)), dma((6,)), dma((3, HIGH)), dma((4, HIGH)), dma((3, HIGH)), dma((3, HIGH)),
            dma((CHUNKS,)), dma((CHUNKS,)), dma((CHUNKS,)), dma((CHUNKS,)), dma((3, 3)), dma((3, 3)),
        ],
        compiler_params=pltpu.CompilerParams(collective_id=0, has_side_effects=True, vmem_limit_bytes=60 * 1024 * 1024),
    )(
        queries, key_vectors, values, lookback.reshape(1, -1), residual, out_weight,
        branch_gate.reshape(1, -1), final_shift.reshape(1, -1), final_scale.reshape(1, -1),
        final_weight.T, decoder_kernel, decoder_bias.reshape(1, -1),
    )


def one_slab_a_frame(mesh):
    return (mesh.shape["blk"], mesh.shape["head"], mesh.shape["dec"]) == (FRAMES, 2, 2)


def solution(mesh):
    in_specs = (
        P("blk", ("head", "dec")),
        P("blk", ("head", "dec")),
        P("blk", ("head", "dec")),
        P(),
        P(("blk", "head", "dec"), None),
        P(("head", "dec"), None),
        P(),
        P(),
        P(),
        P(),
        P(),
        P(),
    )
    out_specs = P(("blk", "head", "dec"), None, None)
    body = fused if one_slab_a_frame(mesh) else per_device
    return jax.shard_map(
        body, mesh=mesh, in_specs=in_specs, out_specs=out_specs, check_vma=False
    )
```

```python
import functools

import jax
import jax.numpy as jnp
from jax import lax
from jax.experimental import pallas as pl
from jax.experimental.pallas import tpu as pltpu
from jax.sharding import PartitionSpec as P

DH = 128
LC = 16
FRAMES = 8
PW = 32


def padded_2(cells, sides, width):
    for axis, dim in sides:
        count = lax.axis_size(axis)
        ends = count - 1
        head = lax.slice_in_dim(cells, 0, width, axis=dim)
        tail = lax.slice_in_dim(cells, cells.shape[dim] - width, cells.shape[dim], axis=dim)
        cells = jnp.concatenate(
            [
                lax.ppermute(tail, axis, [(i, (i + 1) % count) for i in range(ends)]),
                cells,
                lax.ppermute(head, axis, [((i + 1) % count, i) for i in range(ends)]),
            ],
            axis=dim,
        )
    return cells


def from_behind(x, axis, by):
    peers = lax.axis_size(axis)
    pairs = [(i, i + by) for i in range(peers) if 0 <= i + by < peers]
    return lax.ppermute(x, axis, pairs)


def attend_block(carry, shard_pair, query_heads, query_frame, lookback_heads, frame_len):
    running_max, row_total, accumulated = carry
    key_block, value_block = shard_pair
    key_count = key_block.shape[0]
    head_count = query_heads.shape[1]
    key_heads = key_block.reshape(key_count, head_count, DH)
    value_heads = value_block.reshape(key_count, head_count, DH)
    scores = jnp.einsum(
        "qhd,khd->hqk", query_heads, key_heads, preferred_element_type=jnp.float32
    ) * DH ** (-0.5)
    key_pos = jnp.arange(key_count, dtype=jnp.int32)
    key_frame = key_pos // frame_len
    visible = (
        (key_pos >= 0)[None, None, :]
        & (key_frame[None, None, :] <= query_frame[None, :, None])
        & (key_frame[None, None, :] >= query_frame[None, :, None] - lookback_heads[:, None, None])
    )
    masked = jnp.where(visible, scores, -1e30)
    newest_max = jnp.maximum(running_max, jnp.max(masked, axis=2))
    weights = jnp.where(visible, jnp.exp(scores - newest_max[:, :, None]), 0.0).astype(jnp.bfloat16)
    row_total = jnp.sum(weights.astype(jnp.float32), axis=2)
    accumulated = jnp.einsum(
        "hqk,khd->hqd", weights, value_heads, preferred_element_type=jnp.float32
    )
    return (newest_max, row_total, accumulated)


def per_device(
    queries,
    key_vectors,
    values,
    lookback,
    residual,
    out_weight,
    branch_gate,
    final_shift,
    final_scale,
    final_weight,
    decoder_kernel,
    decoder_bias,
):
    slab_rows = queries.shape[0]
    head_count = queries.shape[1] // DH
    blocks = lax.axis_size("blk")
    block_index = lax.axis_index("blk")
    frame_len = slab_rows * blocks // FRAMES
    query_heads = queries.reshape(slab_rows, head_count, DH)
    query_frame = (block_index * slab_rows + jnp.arange(slab_rows, dtype=jnp.int32)) // frame_len
    lookback_heads = lax.dynamic_slice_in_dim(
        lookback, lax.axis_index(("head", "dec")) * head_count, head_count
    )
    initial = (
        jnp.full((head_count, slab_rows), -1e30, jnp.float32),
        jnp.zeros((head_count, slab_rows), jnp.float32),
        jnp.zeros((head_count, slab_rows, DH), jnp.float32),
    )
    carry = attend_block(
        initial,
        (
            lax.all_gather(key_vectors, "blk", axis=0, tiled=True),
            lax.all_gather(values, "blk", axis=0, tiled=True),
        ),
        query_heads,
        query_frame,
        lookback_heads,
        frame_len,
    )
    newest_max, row_total, accumulated = carry
    attended = (
        (accumulated / row_total[:, :, None])
        .transpose(1, 0, 2)
        .reshape(slab_rows, head_count * DH)
        .astype(jnp.bfloat16)
    )
    tokens_dev = slab_rows // lax.axis_size(("head", "dec"))
    projected = lax.psum_scatter(
        jnp.dot(attended, out_weight, preferred_element_type=jnp.float32).astype(jnp.bfloat16),
        ("head", "dec"),
        scatter_dimension=0,
        tiled=True,
    ).astype(jnp.float32)
    hidden = residual.astype(jnp.float32) + branch_gate[None, :] * projected
    center = jnp.mean(hidden, axis=1, keepdims=True)
    spread = jnp.mean((hidden - center) ** 2, axis=1, keepdims=True)
    normed = (
        (hidden - center) * lax.rsqrt(spread + 1e-06) * (1.0 + final_scale[None, :])
        + final_shift[None, :]
    ).astype(jnp.bfloat16)
    patches = jnp.dot(normed, final_weight, preferred_element_type=jnp.float32).astype(jnp.bfloat16)
    patch_rows = tokens_dev // PW
    tile_rows = 2 * patch_rows
    width = 2 * PW
    tile = (
        patches.reshape(patch_rows, PW, 2, 2, LC)
        .transpose(0, 2, 1, 3, 4)
        .reshape(tile_rows, width * LC)
    )
    padded = padded_2(tile, ((("blk", "head", "dec"), 0),), 1)
    frame_stride = blocks // FRAMES
    frame_index = block_index // frame_stride
    prior_one = from_behind(padded, "blk", frame_stride)
    prior_one = jnp.where(frame_index >= 1, prior_one, padded)
    prior_two = from_behind(prior_one, "blk", frame_stride)
    prior_two = jnp.where(frame_index >= 1, prior_two, padded)
    history = jnp.stack([prior_two, prior_one, padded]).reshape(3, tile_rows + 2, width, LC)
    history = jnp.pad(history, ((0, 0), (0, 0), (1, 1), (0, 0)))
    windows = [
        history[time_tap, row_tap : row_tap + tile_rows, column_tap : column_tap + width, :]
        for time_tap in range(3)
        for row_tap in range(3)
        for column_tap in range(3)
    ]
    columns = jnp.concatenate(windows, axis=-1).reshape(tile_rows * width, 27 * LC)
    summed = (
        jnp.dot(columns, decoder_kernel, preferred_element_type=jnp.float32) + decoder_bias[None, :]
    )
    return summed.astype(jnp.bfloat16).reshape(tile_rows, width, decoder_kernel.shape[1])


HIGH = 3
CHUNKS = 4
MESH = pl.DeviceIdType.MESH


def fused_kernel(
    q_hbm, k_hbm, v_hbm, look_hbm, res_hbm, w_hbm, gate_hbm, shift_hbm, scale_hbm, fw_hbm, dk_hbm, db_hbm,
    out_ref,
    lookback, kz, kx, qv, asked, mixed_out, mixed_in, level_out, level_in, wv, resv, gatev, shiftv, scalev, fwv, dkv, dbv,
    top, total, acc, att, part, from_dec, to_y, from_y, hid, halo, wide, canvas,
    load_sem, kv_sem, zs, zr, xs, xr, qs, qr, os, orr, ls, lr, ds, dr, ys, yr, hs, hr,
):
    f = lax.axis_index("blk")
    hd = lax.axis_index("head")
    dc = lax.axis_index("dec")
    z, x = f // 2, f % 2
    n = f * 4 + hd * 2 + dc
    slab = q_hbm.shape[0]
    columns = w_hbm.shape[1] // CHUNKS

    barrier = pltpu.get_barrier_semaphore()
    greeted = jnp.int32(1)
    pl.semaphore_signal(barrier, inc=1, device_id=(f, 1 - hd, dc), device_id_type=MESH)
    for apart in (1, 3, 4, 5, 7, 8, 9):
        for m in (n - apart, n + apart):
            there = (m >= 0) & (m < 32)
            greeted = greeted + jnp.where(there, 1, 0)

            @pl.when(there)
            def _():
                pl.semaphore_signal(
                    barrier, inc=1, device_id=(m // 4, (m % 4) // 2, m % 2), device_id_type=MESH
                )

    @pl.when((f == 2) | (f == 6))
    def _():
        pl.semaphore_signal(barrier, inc=1, device_id=(8 - f, hd, dc), device_id_type=MESH)

    greeted = greeted + jnp.where((f == 2) | (f == 6), 1, 0)

    kv_loads = []
    for h in range(HIGH):
        for which, src in enumerate((k_hbm, v_hbm)):
            kv_loads.append(
                pltpu.make_async_copy(
                    src.at[:, pl.ds(h * DH, DH)], kz.at[0, h, which], kv_sem.at[2 * h + which]
                )
            )
    loads = [
        pltpu.make_async_copy(src, dst, load_sem.at[i])
        for i, (src, dst) in enumerate(
            (
                *[(q_hbm.at[:, pl.ds(h * DH, DH)], qv.at[h]) for h in range(HIGH)],
                (dk_hbm, dkv), (look_hbm, lookback), (w_hbm, wv), (res_hbm, resv), (gate_hbm, gatev),
                (shift_hbm, shiftv), (scale_hbm, scalev), (fw_hbm, fwv), (db_hbm, dbv),
            )
        )
    ]
    for c in kv_loads + loads:
        c.start()

    def up(h):
        return pltpu.make_async_remote_copy(
            src_ref=kz.at[0, h], dst_ref=kz.at[1, h], send_sem=zs.at[h], recv_sem=zr.at[h],
            device_id=(f + 2, hd, dc), device_id_type=MESH,
        )

    def own_across(h):
        return pltpu.make_async_remote_copy(
            src_ref=kz.at[0, h], dst_ref=kx.at[0, h], send_sem=xs.at[0, h], recv_sem=xr.at[0, h],
            device_id=(f + 1, hd, dc), device_id_type=MESH,
        )

    def lower_across(h):
        return pltpu.make_async_remote_copy(
            src_ref=kz.at[1, h], dst_ref=kx.at[1 - x, h], send_sem=xs.at[1, h], recv_sem=xr.at[1 - x, h],
            device_id=(f + 1 - 2 * x, hd, dc), device_id_type=MESH,
        )

    def arrived(slot, h):
        pltpu.make_async_remote_copy(
            src_ref=kz.at[1, h], dst_ref=kx.at[slot, h], send_sem=xs.at[1, h], recv_sem=xr.at[slot, h],
            device_id=(f + 1 - 2 * x, hd, dc), device_id_type=MESH,
        ).wait_recv()

    def ask(far, h):
        return pltpu.make_async_remote_copy(
            src_ref=qv.at[h], dst_ref=asked.at[far, h], send_sem=qs.at[far, h], recv_sem=qr.at[far, h],
            device_id=(f - 2 - 2 * far, hd, dc), device_id_type=MESH,
        )

    def answer(far, h):
        to = (f + 2 + 2 * far, hd, dc)
        return (
            pltpu.make_async_remote_copy(
                src_ref=mixed_out.at[far, h], dst_ref=mixed_in.at[far, h],
                send_sem=os.at[far, h], recv_sem=orr.at[far, h], device_id=to, device_id_type=MESH,
            ),
            pltpu.make_async_remote_copy(
                src_ref=level_out.at[far, h], dst_ref=level_in.at[far, h],
                send_sem=ls.at[far, h], recv_sem=lr.at[far, h], device_id=to, device_id_type=MESH,
            ),
        )

    asks = (z >= 2, f == 6)
    helps = ((z >= 1) & (z <= 2), f == 2)

    for c in kv_loads:
        c.wait()
    for h in range(HIGH):
        loads[h].wait()
    pl.semaphore_wait(barrier, greeted)

    for h in range(HIGH):

        @pl.when(z < 3)
        def _():
            up(h).start()

        for far in range(2):

            @pl.when(asks[far])
            def _():
                ask(far, h).start()

        @pl.when((x == 0) & ((z == 0) | (h == 0)))
        def _():
            own_across(h).start()

    def scored(query, key, h, distance):
        scores = lax.dot_general(
            query, key, (((1,), (1,)), ((), ())), preferred_element_type=jnp.float32
        ) * DH ** (-0.5)
        if isinstance(distance, int) and distance == 0:
            return scores
        seen = lookback[0, (hd * 2 + dc) * HIGH + h] >= distance
        return scores + jnp.where(seen, 0.0, -1e30)

    def weighed(scores, newest, value):
        weights = jnp.exp(scores - newest).astype(jnp.bfloat16)
        added = jnp.sum(weights.astype(jnp.float32), axis=1, keepdims=True)
        return added, jnp.dot(weights, value, preferred_element_type=jnp.float32)

    def attend(h, key, value, distance):
        scores = scored(qv[h], key, h, distance)
        newest = jnp.max(scores, axis=1, keepdims=True)
        if isinstance(distance, int) and distance == 0:
            total[h], acc[h] = weighed(scores, newest, value)
        else:
            newest = jnp.maximum(top[h], newest)
            added, mixed = weighed(scores, newest, value)
            shrink = jnp.exp(top[h] - newest)
            total[h] = total[h] * shrink + added
            acc[h] = acc[h] * shrink + mixed
        top[h] = newest

    def help_with(far, h, blocks):
        @pl.when(helps[far])
        def _():
            ask(far, h).wait_recv()
            query = asked[far, h]
            scores = [scored(query, key, h, distance) for key, _, distance in blocks]
            newest = functools.reduce(
                jnp.maximum, [jnp.max(each, axis=1, keepdims=True) for each in scores]
            )
            parts = [weighed(each, newest, block[1]) for each, block in zip(scores, blocks)]
            added = functools.reduce(jnp.add, [part[0] for part in parts])
            mixed = functools.reduce(jnp.add, [part[1] for part in parts])
            mixed_out[far, h] = (mixed / added).astype(jnp.bfloat16)
            level = jnp.broadcast_to(newest + jnp.log(added), (slab, 128))
            level_out[far, h] = level.T[:8]
            for copy in answer(far, h):
                copy.start()

    loads[HIGH].wait()
    loads[HIGH + 1].wait()
    for h in range(HIGH):
        attend(h, kz[0, h, 0], kz[0, h, 1], 0)

    for h in range(HIGH):

        @pl.when(z >= 1)
        def _():
            up(h).wait_recv()
            lower_across(h).start()
            if h == HIGH - 1:

                @pl.when(x == 0)
                def _():
                    for late in range(1, HIGH):
                        own_across(late).start()

            attend(h, kz[1, h, 0], kz[1, h, 1], 2)

    for h in range(HIGH):

        @pl.when(z >= 1)
        def _():
            arrived(x, h)
            lower = (kx[x, h, 0], kx[x, h, 1], 3 + 2 * x)
            help_with(0, h, (lower, (kz[1, h, 0], kz[1, h, 1], 4)))
            help_with(1, h, ((lower[0], lower[1], 5),))
            attend(h, kx[x, h, 0], kx[x, h, 1], 1 + 2 * x)

    for h in range(HIGH):

        @pl.when(x == 1)
        def _():
            arrived(0, h)
            attend(h, kx[0, h, 0], kx[0, h, 1], 1)

    wide[...] = jnp.zeros_like(wide)
    for a in range(2):
        for b in range(2):
            for t in range(3):
                for i in range(3):
                    for j in range(3):
                        ya, xb = a + i - 1, b + j - 1
                        row = ((t * 2 + ya // 2 - (a - 1)) * 2 + xb // 2 - (b - 1)) * 64
                        row += ((ya % 2) * 2 + xb % 2) * LC
                        tap = (t * 3 + i) * 3 + j
                        wide[a * 2 + b, row : row + LC, :] = dkv[tap * LC : (tap + 1) * LC, :]


    for far in range(2):
        for h in range(HIGH):

            @pl.when(asks[far])
            def _():
                for copy in answer(far, h):
                    copy.wait_recv()
                level = jnp.broadcast_to(level_in[far, h][:1], (128, slab)).T[:, :1]
                newest = jnp.maximum(top[h], level)
                shrink, grow = jnp.exp(top[h] - newest), jnp.exp(level - newest)
                total[h] = total[h] * shrink + grow
                acc[h] = acc[h] * shrink + mixed_in[far, h].astype(jnp.float32) * grow
                top[h] = newest

    for h in range(HIGH):
        att[:, h * DH : (h + 1) * DH] = (acc[h] / total[h]).astype(jnp.bfloat16)

    def to_core(c):
        return pltpu.make_async_remote_copy(
            src_ref=part.at[c, :, 1 - dc], dst_ref=from_dec.at[c], send_sem=ds.at[c], recv_sem=dr.at[c],
            device_id=(f, hd, 1 - dc), device_id_type=MESH,
        )

    def to_row(c):
        return pltpu.make_async_remote_copy(
            src_ref=to_y.at[c], dst_ref=from_y.at[c], send_sem=ys.at[c], recv_sem=yr.at[c],
            device_id=(f, 1 - hd, dc), device_id_type=MESH,
        )

    loads[HIGH + 2].wait()
    for c in range(CHUNKS):
        share = jnp.dot(
            att[...], wv[:, c * columns : (c + 1) * columns], preferred_element_type=jnp.float32
        ).astype(jnp.bfloat16)
        part[c] = share.reshape(2, 2, slab // 4, columns)
        to_core(c).start()
    for c in range(CHUNKS):
        to_core(c).wait_recv()
        to_y[c] = (
            part[c, 1 - hd, dc].astype(jnp.float32) + from_dec[c, 1 - hd].astype(jnp.float32)
        ).astype(jnp.bfloat16)
        to_row(c).start()
    for load in loads[HIGH + 3 :]:
        load.wait()
    summed = jnp.zeros((slab // 4, 1), jnp.float32)
    for c in range(CHUNKS):
        cols = slice(c * columns, (c + 1) * columns)
        mine = part[c, hd, dc].astype(jnp.float32) + from_dec[c, hd].astype(jnp.float32)
        to_row(c).wait_recv()
        hidden = resv[:, cols].astype(jnp.float32) + gatev[:, cols] * (mine + from_y[c].astype(jnp.float32))
        hid[c] = hidden
        summed = summed + jnp.sum(hidden, axis=1, keepdims=True)
    center = summed / (CHUNKS * columns)
    squares = jnp.zeros((slab // 4, 1), jnp.float32)
    for c in range(CHUNKS):
        squares = squares + jnp.sum((hid[c] - center) ** 2, axis=1, keepdims=True)
    inverse = lax.rsqrt(squares / (CHUNKS * columns) + 1e-06)
    patches = jnp.zeros((slab // 4, fwv.shape[0]), jnp.float32)
    for c in range(CHUNKS):
        cols = slice(c * columns, (c + 1) * columns)
        normed = ((hid[c] - center) * inverse * (1.0 + scalev[:, cols]) + shiftv[:, cols]).astype(jnp.bfloat16)
        patches = patches + lax.dot_general(
            normed, fwv[:, cols], (((1,), (1,)), ((), ())), preferred_element_type=jnp.float32
        )
    halo[0, 1] = jnp.concatenate([patches, patches], axis=1).astype(jnp.bfloat16)

    def tile_to(back, side):
        m = n + 4 * back - side
        copy = pltpu.make_async_remote_copy(
            src_ref=halo.at[0, 1], dst_ref=halo.at[back, side + 1],
            send_sem=hs.at[back, side + 1], recv_sem=hr.at[back, side + 1],
            device_id=(m // 4, (m % 4) // 2, m % 2), device_id_type=MESH,
        )
        return copy, (m >= 4 * back) & (m < 32)

    def tile_comes(back, side):
        source = n - 4 * back + side
        return (f >= back) & (source >= 0) & (source < 32)

    reach = [(back, side) for back in (2, 1, 0) for side in (-1, 0, 1) if (back, side) != (0, 0)]
    for back, side in reach:
        copy, goes = tile_to(back, side)

        @pl.when(goes)
        def _():
            copy.start()

    for back, side in reach:

        @pl.when(tile_comes(back, side))
        def _():
            tile_to(back, side)[0].wait_recv()

    rows = 4 * PW
    lane = lax.broadcasted_iota(jnp.int32, (rows, 128), 1)
    token = lax.broadcasted_iota(jnp.int32, (rows, 128), 0) % PW
    pairs = []
    for t in range(3):
        back = jnp.minimum(2 - t, f)
        first = n - 4 * back
        above = jnp.where(first >= 1, halo[back, 0, PW:, :].astype(jnp.float32), 0.0)
        below = jnp.where(first <= 30, halo[back, 2, :PW, :].astype(jnp.float32), 0.0)
        ext = jnp.concatenate([above, halo[back, 1].astype(jnp.float32), below], axis=0)
        before = jnp.where(token == 0, 0.0, pltpu.roll(ext, 1, 0))
        after = jnp.where(token == PW - 1, 0.0, pltpu.roll(ext, rows - 1, 0))
        pairs.append(
            (
                jnp.where(lane < 64, before, ext).astype(jnp.bfloat16),
                jnp.where(lane < 64, ext, after).astype(jnp.bfloat16),
            )
        )
    for a in range(2):
        for b in range(2):
            lhs = jnp.concatenate(
                [
                    pairs[t][b][(a + d) * PW : (a + d) * PW + 2 * PW]
                    for t in range(3)
                    for d in range(2)
                ],
                axis=1,
            )
            got = jnp.dot(lhs, wide[a * 2 + b], preferred_element_type=jnp.float32) + dbv[...]
            for r in range(2):
                for g in range(got.shape[1] // 128):
                    canvas[g, pl.ds((2 * r + a) * 2 * PW + b, PW, stride=2), :] = got[
                        r * PW : (r + 1) * PW, g * 128 : (g + 1) * 128
                    ]
    for y in range(4):
        for g in range(canvas.shape[0]):
            out_ref[y, :, g * 128 : (g + 1) * 128] = canvas[g, y * 2 * PW : (y + 1) * 2 * PW, :].astype(jnp.bfloat16)

    for h in range(HIGH):

        @pl.when(z < 3)
        def _():
            up(h).wait_send()

        @pl.when(z >= 1)
        def _():
            lower_across(h).wait_send()

        @pl.when(x == 0)
        def _():
            own_across(h).wait_send()

        for far in range(2):

            @pl.when(asks[far])
            def _():
                ask(far, h).wait_send()

            @pl.when(helps[far])
            def _():
                for copy in answer(far, h):
                    copy.wait_send()

    for c in range(CHUNKS):
        to_core(c).wait_send()
        to_row(c).wait_send()
    for back, side in reach:
        copy, goes = tile_to(back, side)

        @pl.when(goes)
        def _():
            copy.wait_send()


def fused(
    queries, key_vectors, values, lookback, residual, out_weight,
    branch_gate, final_shift, final_scale, final_weight, decoder_kernel, decoder_bias,
):
    slab, width = queries.shape
    model = out_weight.shape[1]
    quarter, columns = slab // 4, model // CHUNKS
    outputs = decoder_kernel.shape[1]
    bf, f32 = jnp.bfloat16, jnp.float32
    vm, dma = pltpu.VMEM, pltpu.SemaphoreType.DMA
    hbm = pl.BlockSpec(memory_space=pltpu.HBM)
    return pl.pallas_call(
        fused_kernel,
        out_shape=jax.ShapeDtypeStruct((4, 2 * PW, outputs), bf),
        in_specs=[hbm] * 12,
        out_specs=pl.BlockSpec(memory_space=pltpu.VMEM),
        scratch_shapes=[
            pltpu.SMEM((1, lookback.shape[0]), jnp.int32),
            vm((2, HIGH, 2, slab, DH), bf), vm((2, HIGH, 2, slab, DH), bf), vm((HIGH, slab, DH), bf),
            *[vm((2, HIGH, slab, DH), bf)] * 3, *[vm((2, HIGH, 8, slab), f32)] * 2,
            vm((width, model), bf), vm((quarter, model), bf),
            vm((1, model), f32), vm((1, model), f32), vm((1, model), f32),
            vm(final_weight.shape[::-1], bf), vm(decoder_kernel.shape, bf), vm((1, outputs), f32),
            vm((HIGH, slab, 1), f32), vm((HIGH, slab, 1), f32), vm((HIGH, slab, DH), f32),
            vm((slab, width), bf), vm((CHUNKS, 2, 2, quarter, columns), bf),
            vm((CHUNKS, 2, quarter, columns), bf), vm((CHUNKS, quarter, columns), bf),
            vm((CHUNKS, quarter, columns), bf), vm((CHUNKS, quarter, columns), f32),
            vm((3, 3, quarter, 128), bf), vm((4, 768, outputs), bf), vm((outputs // 128, 256, 128), f32),
            dma((HIGH + 9,)), dma((6,)), dma((HIGH,)), dma((HIGH,)), dma((2, HIGH)), dma((2, HIGH)),
            *[dma((2, HIGH))] * 6,
            dma((CHUNKS,)), dma((CHUNKS,)), dma((CHUNKS,)), dma((CHUNKS,)), dma((3, 3)), dma((3, 3)),
        ],
        compiler_params=pltpu.CompilerParams(collective_id=0, has_side_effects=True, vmem_limit_bytes=60 * 1024 * 1024),
    )(
        queries, key_vectors, values, lookback.reshape(1, -1), residual, out_weight,
        branch_gate.reshape(1, -1), final_shift.reshape(1, -1), final_scale.reshape(1, -1),
        final_weight.T, decoder_kernel, decoder_bias.reshape(1, -1),
    )


def one_slab_a_frame(mesh):
    return (mesh.shape["blk"], mesh.shape["head"], mesh.shape["dec"]) == (FRAMES, 2, 2)


def solution(mesh):
    in_specs = (
        P("blk", ("head", "dec")),
        P("blk", ("head", "dec")),
        P("blk", ("head", "dec")),
        P(),
        P(("blk", "head", "dec"), None),
        P(("head", "dec"), None),
        P(),
        P(),
        P(),
        P(),
        P(),
        P(),
    )
    out_specs = P(("blk", "head", "dec"), None, None)
    body = fused if one_slab_a_frame(mesh) else per_device
    return jax.shard_map(
        body, mesh=mesh, in_specs=in_specs, out_specs=out_specs, check_vma=False
    )
```

```python
import functools

import jax
import jax.numpy as jnp
from jax import lax
from jax.experimental import pallas as pl
from jax.experimental.pallas import tpu as pltpu
from jax.sharding import PartitionSpec as P

DH = 128
LC = 16
FRAMES = 8
PW = 32


def padded_2(cells, sides, width):
    for axis, dim in sides:
        count = lax.axis_size(axis)
        ends = count - 1
        head = lax.slice_in_dim(cells, 0, width, axis=dim)
        tail = lax.slice_in_dim(cells, cells.shape[dim] - width, cells.shape[dim], axis=dim)
        cells = jnp.concatenate(
            [
                lax.ppermute(tail, axis, [(i, (i + 1) % count) for i in range(ends)]),
                cells,
                lax.ppermute(head, axis, [((i + 1) % count, i) for i in range(ends)]),
            ],
            axis=dim,
        )
    return cells


def from_behind(x, axis, by):
    peers = lax.axis_size(axis)
    pairs = [(i, i + by) for i in range(peers) if 0 <= i + by < peers]
    return lax.ppermute(x, axis, pairs)


def attend_block(carry, shard_pair, query_heads, query_frame, lookback_heads, frame_len):
    running_max, row_total, accumulated = carry
    key_block, value_block = shard_pair
    key_count = key_block.shape[0]
    head_count = query_heads.shape[1]
    key_heads = key_block.reshape(key_count, head_count, DH)
    value_heads = value_block.reshape(key_count, head_count, DH)
    scores = jnp.einsum(
        "qhd,khd->hqk", query_heads, key_heads, preferred_element_type=jnp.float32
    ) * DH ** (-0.5)
    key_pos = jnp.arange(key_count, dtype=jnp.int32)
    key_frame = key_pos // frame_len
    visible = (
        (key_pos >= 0)[None, None, :]
        & (key_frame[None, None, :] <= query_frame[None, :, None])
        & (key_frame[None, None, :] >= query_frame[None, :, None] - lookback_heads[:, None, None])
    )
    masked = jnp.where(visible, scores, -1e30)
    newest_max = jnp.maximum(running_max, jnp.max(masked, axis=2))
    weights = jnp.where(visible, jnp.exp(scores - newest_max[:, :, None]), 0.0).astype(jnp.bfloat16)
    row_total = jnp.sum(weights.astype(jnp.float32), axis=2)
    accumulated = jnp.einsum(
        "hqk,khd->hqd", weights, value_heads, preferred_element_type=jnp.float32
    )
    return (newest_max, row_total, accumulated)


def per_device(
    queries,
    key_vectors,
    values,
    lookback,
    residual,
    out_weight,
    branch_gate,
    final_shift,
    final_scale,
    final_weight,
    decoder_kernel,
    decoder_bias,
):
    slab_rows = queries.shape[0]
    head_count = queries.shape[1] // DH
    blocks = lax.axis_size("blk")
    block_index = lax.axis_index("blk")
    frame_len = slab_rows * blocks // FRAMES
    query_heads = queries.reshape(slab_rows, head_count, DH)
    query_frame = (block_index * slab_rows + jnp.arange(slab_rows, dtype=jnp.int32)) // frame_len
    lookback_heads = lax.dynamic_slice_in_dim(
        lookback, lax.axis_index(("head", "dec")) * head_count, head_count
    )
    initial = (
        jnp.full((head_count, slab_rows), -1e30, jnp.float32),
        jnp.zeros((head_count, slab_rows), jnp.float32),
        jnp.zeros((head_count, slab_rows, DH), jnp.float32),
    )
    carry = attend_block(
        initial,
        (
            lax.all_gather(key_vectors, "blk", axis=0, tiled=True),
            lax.all_gather(values, "blk", axis=0, tiled=True),
        ),
        query_heads,
        query_frame,
        lookback_heads,
        frame_len,
    )
    newest_max, row_total, accumulated = carry
    attended = (
        (accumulated / row_total[:, :, None])
        .transpose(1, 0, 2)
        .reshape(slab_rows, head_count * DH)
        .astype(jnp.bfloat16)
    )
    tokens_dev = slab_rows // lax.axis_size(("head", "dec"))
    projected = lax.psum_scatter(
        jnp.dot(attended, out_weight, preferred_element_type=jnp.float32).astype(jnp.bfloat16),
        ("head", "dec"),
        scatter_dimension=0,
        tiled=True,
    ).astype(jnp.float32)
    hidden = residual.astype(jnp.float32) + branch_gate[None, :] * projected
    center = jnp.mean(hidden, axis=1, keepdims=True)
    spread = jnp.mean((hidden - center) ** 2, axis=1, keepdims=True)
    normed = (
        (hidden - center) * lax.rsqrt(spread + 1e-06) * (1.0 + final_scale[None, :])
        + final_shift[None, :]
    ).astype(jnp.bfloat16)
    patches = jnp.dot(normed, final_weight, preferred_element_type=jnp.float32).astype(jnp.bfloat16)
    patch_rows = tokens_dev // PW
    tile_rows = 2 * patch_rows
    width = 2 * PW
    tile = (
        patches.reshape(patch_rows, PW, 2, 2, LC)
        .transpose(0, 2, 1, 3, 4)
        .reshape(tile_rows, width * LC)
    )
    padded = padded_2(tile, ((("blk", "head", "dec"), 0),), 1)
    frame_stride = blocks // FRAMES
    frame_index = block_index // frame_stride
    prior_one = from_behind(padded, "blk", frame_stride)
    prior_one = jnp.where(frame_index >= 1, prior_one, padded)
    prior_two = from_behind(prior_one, "blk", frame_stride)
    prior_two = jnp.where(frame_index >= 1, prior_two, padded)
    history = jnp.stack([prior_two, prior_one, padded]).reshape(3, tile_rows + 2, width, LC)
    history = jnp.pad(history, ((0, 0), (0, 0), (1, 1), (0, 0)))
    windows = [
        history[time_tap, row_tap : row_tap + tile_rows, column_tap : column_tap + width, :]
        for time_tap in range(3)
        for row_tap in range(3)
        for column_tap in range(3)
    ]
    columns = jnp.concatenate(windows, axis=-1).reshape(tile_rows * width, 27 * LC)
    summed = (
        jnp.dot(columns, decoder_kernel, preferred_element_type=jnp.float32) + decoder_bias[None, :]
    )
    return summed.astype(jnp.bfloat16).reshape(tile_rows, width, decoder_kernel.shape[1])


HIGH = 3
CHUNKS = 6
STEPS = (2, 4, 1)
SIDE = (1, 2)
MESH = pl.DeviceIdType.MESH


def fused_kernel(
    q_hbm, k_hbm, v_hbm, look_hbm, res_hbm, w_hbm, gate_hbm, shift_hbm, scale_hbm, fw_hbm, dk_hbm, db_hbm,
    out_ref,
    lookback, kz, kx, qv, asked, mixed_out, mixed_in, level_out, level_in, wv, resv, gatev, shiftv, scalev, fwv, dkv, dbv,
    top, total, acc, att, part, from_dec, to_y, from_y, hid, halo, wide, canvas,
    load_sem, kv_sem, zs, zr, xs, xr, qs, qr, os, orr, ls, lr, ds, dr, ys, yr, hs, hr,
):
    f = lax.axis_index("blk")
    hd = lax.axis_index("head")
    dc = lax.axis_index("dec")
    z, x = f // 2, f % 2
    n = f * 4 + hd * 2 + dc
    slab = q_hbm.shape[0]
    columns = w_hbm.shape[1] // CHUNKS

    barrier = pltpu.get_barrier_semaphore()
    greeted = jnp.int32(1)
    pl.semaphore_signal(barrier, inc=1, device_id=(f, 1 - hd, dc), device_id_type=MESH)
    for apart in (1, 3, 4, 5, 7, 8, 9):
        for m in (n - apart, n + apart):
            there = (m >= 0) & (m < 32)
            greeted = greeted + jnp.where(there, 1, 0)

            @pl.when(there)
            def _():
                pl.semaphore_signal(
                    barrier, inc=1, device_id=(m // 4, (m % 4) // 2, m % 2), device_id_type=MESH
                )

    @pl.when((f == 2) | (f == 6))
    def _():
        pl.semaphore_signal(barrier, inc=1, device_id=(8 - f, hd, dc), device_id_type=MESH)

    greeted = greeted + jnp.where((f == 2) | (f == 6), 1, 0)

    kv_loads = []
    for h in range(HIGH):
        for which, src in enumerate((k_hbm, v_hbm)):
            kv_loads.append(
                pltpu.make_async_copy(
                    src.at[:, pl.ds(h * DH, DH)], kz.at[0, h, which], kv_sem.at[2 * h + which]
                )
            )
    loads = [
        pltpu.make_async_copy(src, dst, load_sem.at[i])
        for i, (src, dst) in enumerate(
            (
                *[(q_hbm.at[:, pl.ds(h * DH, DH)], qv.at[h]) for h in range(HIGH)],
                (dk_hbm, dkv), (look_hbm, lookback), (w_hbm, wv), (res_hbm, resv), (gate_hbm, gatev),
                (shift_hbm, shiftv), (scale_hbm, scalev), (fw_hbm, fwv), (db_hbm, dbv),
            )
        )
    ]
    for c in kv_loads + loads:
        c.start()

    def up(h):
        return pltpu.make_async_remote_copy(
            src_ref=kz.at[0, h], dst_ref=kz.at[1, h], send_sem=zs.at[h], recv_sem=zr.at[h],
            device_id=(f + 2, hd, dc), device_id_type=MESH,
        )

    def own_across(h):
        return pltpu.make_async_remote_copy(
            src_ref=kz.at[0, h], dst_ref=kx.at[0, h], send_sem=xs.at[0, h], recv_sem=xr.at[0, h],
            device_id=(f + 1, hd, dc), device_id_type=MESH,
        )

    def lower_across(h):
        return pltpu.make_async_remote_copy(
            src_ref=kz.at[1, h], dst_ref=kx.at[1 - x, h], send_sem=xs.at[1, h], recv_sem=xr.at[1 - x, h],
            device_id=(f + 1 - 2 * x, hd, dc), device_id_type=MESH,
        )

    def arrived(slot, h):
        pltpu.make_async_remote_copy(
            src_ref=kz.at[1, h], dst_ref=kx.at[slot, h], send_sem=xs.at[1, h], recv_sem=xr.at[slot, h],
            device_id=(f + 1 - 2 * x, hd, dc), device_id_type=MESH,
        ).wait_recv()

    def ask(far, h):
        return pltpu.make_async_remote_copy(
            src_ref=qv.at[h], dst_ref=asked.at[far, h], send_sem=qs.at[far, h], recv_sem=qr.at[far, h],
            device_id=(f - STEPS[far], hd, dc), device_id_type=MESH,
        )

    def answer(far, h):
        to = (f + STEPS[far], hd, dc)
        return (
            pltpu.make_async_remote_copy(
                src_ref=mixed_out.at[far, h], dst_ref=mixed_in.at[far, h],
                send_sem=os.at[far, h], recv_sem=orr.at[far, h], device_id=to, device_id_type=MESH,
            ),
            pltpu.make_async_remote_copy(
                src_ref=level_out.at[far, h], dst_ref=level_in.at[far, h],
                send_sem=ls.at[far, h], recv_sem=lr.at[far, h], device_id=to, device_id_type=MESH,
            ),
        )

    asks = (z >= 2, f == 6, x == 1)
    helps = ((z >= 1) & (z <= 2), f == 2, x == 0)

    def kinds(h):
        return (0, 1, 2) if h in SIDE else (0, 1)


    for c in kv_loads:
        c.wait()
    for h in range(HIGH):
        loads[h].wait()
    pl.semaphore_wait(barrier, greeted)

    for h in range(HIGH):

        @pl.when(z < 3)
        def _():
            up(h).start()

        for far in kinds(h):

            @pl.when(asks[far])
            def _():
                ask(far, h).start()

        if h not in SIDE:

            @pl.when(x == 0)
            def _():
                own_across(h).start()

    def scored(query, key, h, distance):
        scores = lax.dot_general(
            query, key, (((1,), (1,)), ((), ())), preferred_element_type=jnp.float32
        ) * DH ** (-0.5)
        if isinstance(distance, int) and distance == 0:
            return scores
        seen = lookback[0, (hd * 2 + dc) * HIGH + h] >= distance
        return scores + jnp.where(seen, 0.0, -1e30)

    def weighed(scores, newest, value):
        weights = jnp.exp(scores - newest).astype(jnp.bfloat16)
        added = jnp.sum(weights.astype(jnp.float32), axis=1, keepdims=True)
        return added, jnp.dot(weights, value, preferred_element_type=jnp.float32)

    def attend(h, key, value, distance):
        scores = scored(qv[h], key, h, distance)
        newest = jnp.max(scores, axis=1, keepdims=True)
        if isinstance(distance, int) and distance == 0:
            total[h], acc[h] = weighed(scores, newest, value)
        else:
            newest = jnp.maximum(top[h], newest)
            added, mixed = weighed(scores, newest, value)
            shrink = jnp.exp(top[h] - newest)
            total[h] = total[h] * shrink + added
            acc[h] = acc[h] * shrink + mixed
        top[h] = newest

    def help_with(far, h, blocks):
        @pl.when(helps[far])
        def _():
            ask(far, h).wait_recv()
            query = asked[far, h]
            scores = [scored(query, key, h, distance) for key, _, distance in blocks]
            newest = functools.reduce(
                jnp.maximum, [jnp.max(each, axis=1, keepdims=True) for each in scores]
            )
            parts = [weighed(each, newest, block[1]) for each, block in zip(scores, blocks)]
            added = functools.reduce(jnp.add, [part[0] for part in parts])
            mixed = functools.reduce(jnp.add, [part[1] for part in parts])
            mixed_out[far, h] = (mixed / added).astype(jnp.bfloat16)
            level = jnp.broadcast_to(newest + jnp.log(added), (slab, 128))
            level_out[far, h] = level.T[:8]
            for copy in answer(far, h):
                copy.start()

    loads[HIGH].wait()
    loads[HIGH + 1].wait()
    for h in range(HIGH):
        attend(h, kz[0, h, 0], kz[0, h, 1], 0)

    for h in range(HIGH):

        @pl.when(z >= 1)
        def _():
            up(h).wait_recv()
            lower_across(h).start()
            attend(h, kz[1, h, 0], kz[1, h, 1], 2)

    for h in SIDE:
        help_with(2, h, ((kz[0, h, 0], kz[0, h, 1], 1),))

    wide[...] = jnp.zeros_like(wide)
    for a in range(2):
        for b in range(2):
            for t in range(3):
                for i in range(3):
                    for j in range(3):
                        ya, xb = a + i - 1, b + j - 1
                        row = ((t * 2 + ya // 2 - (a - 1)) * 2 + xb // 2 - (b - 1)) * 64
                        row += ((ya % 2) * 2 + xb % 2) * LC
                        tap = (t * 3 + i) * 3 + j
                        wide[a * 2 + b, row : row + LC, :] = dkv[tap * LC : (tap + 1) * LC, :]

    for h in range(HIGH):

        @pl.when(z >= 1)
        def _():
            arrived(x, h)
            lower = (kx[x, h, 0], kx[x, h, 1], 3 + 2 * x)
            help_with(0, h, (lower, (kz[1, h, 0], kz[1, h, 1], 4)))
            help_with(1, h, ((lower[0], lower[1], 5),))
            attend(h, kx[x, h, 0], kx[x, h, 1], 1 + 2 * x)

    for h in range(HIGH):
        if h in SIDE:
            continue

        @pl.when(x == 1)
        def _():
            arrived(0, h)
            attend(h, kx[0, h, 0], kx[0, h, 1], 1)

    for far in (2, 1, 0):
        for h in SIDE if far == 2 else range(HIGH):

            @pl.when(asks[far])
            def _():
                for copy in answer(far, h):
                    copy.wait_recv()
                level = jnp.broadcast_to(level_in[far, h][:1], (128, slab)).T[:, :1]
                newest = jnp.maximum(top[h], level)
                shrink, grow = jnp.exp(top[h] - newest), jnp.exp(level - newest)
                total[h] = total[h] * shrink + grow
                acc[h] = acc[h] * shrink + mixed_in[far, h].astype(jnp.float32) * grow
                top[h] = newest

    for h in range(HIGH):
        att[:, :, h * DH : (h + 1) * DH] = (acc[h] / total[h]).astype(jnp.bfloat16).reshape(2, slab // 2, DH)

    def to_core(half, c):
        return pltpu.make_async_remote_copy(
            src_ref=part.at[c, half, 1 - dc], dst_ref=from_dec.at[c, half],
            send_sem=ds.at[half, c], recv_sem=dr.at[half, c],
            device_id=(f, hd, 1 - dc), device_id_type=MESH,
        )

    def to_row(c):
        return pltpu.make_async_remote_copy(
            src_ref=to_y.at[c], dst_ref=from_y.at[c], send_sem=ys.at[c], recv_sem=yr.at[c],
            device_id=(f, 1 - hd, dc), device_id_type=MESH,
        )

    loads[HIGH + 2].wait()
    def share(half, c):
        got = jnp.dot(
            att[half], wv[:, c * columns : (c + 1) * columns], preferred_element_type=jnp.float32
        ).astype(jnp.bfloat16)
        part[c, half] = got.reshape(2, slab // 4, columns)
        to_core(half, c).start()

    def both_cores(half, c):
        to_core(half, c).wait_recv()
        return part[c, half, dc].astype(jnp.float32) + from_dec[c, half].astype(jnp.float32)

    def pass_on(c):
        to_y[c] = both_cores(1 - hd, c).astype(jnp.bfloat16)
        to_row(c).start()

    for c in range(CHUNKS):
        share(1 - hd, c)
        if c >= 2:
            pass_on(c - 2)
    pass_on(CHUNKS - 2)
    pass_on(CHUNKS - 1)
    for c in range(CHUNKS):
        share(hd, c)
    for load in loads[HIGH + 3 :]:
        load.wait()
    for c in range(CHUNKS):
        cols = slice(c * columns, (c + 1) * columns)
        hid[c] = resv[:, cols].astype(jnp.float32) + gatev[:, cols] * both_cores(hd, c)
    summed = jnp.zeros((slab // 4, 1), jnp.float32)
    for c in range(CHUNKS):
        cols = slice(c * columns, (c + 1) * columns)
        to_row(c).wait_recv()
        hidden = hid[c] + gatev[:, cols] * from_y[c].astype(jnp.float32)
        hid[c] = hidden
        summed = summed + jnp.sum(hidden, axis=1, keepdims=True)
    center = summed / (CHUNKS * columns)
    squares = jnp.zeros((slab // 4, 1), jnp.float32)
    for c in range(CHUNKS):
        squares = squares + jnp.sum((hid[c] - center) ** 2, axis=1, keepdims=True)
    inverse = lax.rsqrt(squares / (CHUNKS * columns) + 1e-06)
    patches = jnp.zeros((slab // 4, fwv.shape[0]), jnp.float32)
    for c in range(CHUNKS):
        cols = slice(c * columns, (c + 1) * columns)
        normed = ((hid[c] - center) * inverse * (1.0 + scalev[:, cols]) + shiftv[:, cols]).astype(jnp.bfloat16)
        patches = patches + lax.dot_general(
            normed, fwv[:, cols], (((1,), (1,)), ((), ())), preferred_element_type=jnp.float32
        )
    halo[0, 1] = jnp.concatenate([patches, patches], axis=1).astype(jnp.bfloat16)

    def tile_to(back, side):
        m = n + 4 * back - side
        copy = pltpu.make_async_remote_copy(
            src_ref=halo.at[0, 1], dst_ref=halo.at[back, side + 1],
            send_sem=hs.at[back, side + 1], recv_sem=hr.at[back, side + 1],
            device_id=(m // 4, (m % 4) // 2, m % 2), device_id_type=MESH,
        )
        return copy, (m >= 4 * back) & (m < 32)

    def tile_comes(back, side):
        source = n - 4 * back + side
        return (f >= back) & (source >= 0) & (source < 32)

    reach = [(back, side) for back in (2, 1, 0) for side in (-1, 0, 1) if (back, side) != (0, 0)]
    for back, side in reach:
        copy, goes = tile_to(back, side)

        @pl.when(goes)
        def _():
            copy.start()

    for back, side in reach:

        @pl.when(tile_comes(back, side))
        def _():
            tile_to(back, side)[0].wait_recv()

    rows = 4 * PW
    lane = lax.broadcasted_iota(jnp.int32, (rows, 128), 1)
    token = lax.broadcasted_iota(jnp.int32, (rows, 128), 0) % PW
    pairs = []
    for t in range(3):
        back = jnp.minimum(2 - t, f)
        first = n - 4 * back
        above = jnp.where(first >= 1, halo[back, 0, PW:, :].astype(jnp.float32), 0.0)
        below = jnp.where(first <= 30, halo[back, 2, :PW, :].astype(jnp.float32), 0.0)
        ext = jnp.concatenate([above, halo[back, 1].astype(jnp.float32), below], axis=0)
        before = jnp.where(token == 0, 0.0, pltpu.roll(ext, 1, 0))
        after = jnp.where(token == PW - 1, 0.0, pltpu.roll(ext, rows - 1, 0))
        pairs.append(
            (
                jnp.where(lane < 64, before, ext).astype(jnp.bfloat16),
                jnp.where(lane < 64, ext, after).astype(jnp.bfloat16),
            )
        )
    for a in range(2):
        for b in range(2):
            lhs = jnp.concatenate(
                [
                    pairs[t][b][(a + d) * PW : (a + d) * PW + 2 * PW]
                    for t in range(3)
                    for d in range(2)
                ],
                axis=1,
            )
            got = jnp.dot(lhs, wide[a * 2 + b], preferred_element_type=jnp.float32) + dbv[...]
            for r in range(2):
                for g in range(got.shape[1] // 128):
                    canvas[g, pl.ds((2 * r + a) * 2 * PW + b, PW, stride=2), :] = got[
                        r * PW : (r + 1) * PW, g * 128 : (g + 1) * 128
                    ]
    for y in range(4):
        for g in range(canvas.shape[0]):
            out_ref[y, :, g * 128 : (g + 1) * 128] = canvas[g, y * 2 * PW : (y + 1) * 2 * PW, :].astype(jnp.bfloat16)

    for h in range(HIGH):

        @pl.when(z < 3)
        def _():
            up(h).wait_send()

        @pl.when(z >= 1)
        def _():
            lower_across(h).wait_send()

        if h not in SIDE:

            @pl.when(x == 0)
            def _():
                own_across(h).wait_send()

        for far in kinds(h):

            @pl.when(asks[far])
            def _():
                ask(far, h).wait_send()

            @pl.when(helps[far])
            def _():
                for copy in answer(far, h):
                    copy.wait_send()

    for c in range(CHUNKS):
        to_core(hd, c).wait_send()
        to_core(1 - hd, c).wait_send()
        to_row(c).wait_send()
    for back, side in reach:
        copy, goes = tile_to(back, side)

        @pl.when(goes)
        def _():
            copy.wait_send()


def fused(
    queries, key_vectors, values, lookback, residual, out_weight,
    branch_gate, final_shift, final_scale, final_weight, decoder_kernel, decoder_bias,
):
    slab, width = queries.shape
    model = out_weight.shape[1]
    quarter, columns = slab // 4, model // CHUNKS
    outputs = decoder_kernel.shape[1]
    bf, f32 = jnp.bfloat16, jnp.float32
    vm, dma = pltpu.VMEM, pltpu.SemaphoreType.DMA
    hbm = pl.BlockSpec(memory_space=pltpu.HBM)
    return pl.pallas_call(
        fused_kernel,
        out_shape=pltpu.VMEM((4, 2 * PW, outputs), bf),
        in_specs=[hbm] * 12,
        out_specs=pl.BlockSpec(memory_space=pltpu.VMEM),
        scratch_shapes=[
            pltpu.SMEM((1, lookback.shape[0]), jnp.int32),
            vm((2, HIGH, 2, slab, DH), bf), vm((2, HIGH, 2, slab, DH), bf), vm((HIGH, slab, DH), bf),
            *[vm((3, HIGH, slab, DH), bf)] * 3, *[vm((3, HIGH, 8, slab), f32)] * 2,
            vm((width, model), bf), vm((quarter, model), bf),
            vm((1, model), f32), vm((1, model), f32), vm((1, model), f32),
            vm(final_weight.shape[::-1], bf), vm(decoder_kernel.shape, bf), vm((1, outputs), f32),
            vm((HIGH, slab, 1), f32), vm((HIGH, slab, 1), f32), vm((HIGH, slab, DH), f32),
            vm((2, slab // 2, width), bf), vm((CHUNKS, 2, 2, quarter, columns), bf),
            vm((CHUNKS, 2, quarter, columns), bf), vm((CHUNKS, quarter, columns), bf),
            vm((CHUNKS, quarter, columns), bf), vm((CHUNKS, quarter, columns), f32),
            vm((3, 3, quarter, 128), bf), vm((4, 768, outputs), bf), vm((outputs // 128, 256, 128), f32),
            dma((HIGH + 9,)), dma((6,)), dma((HIGH,)), dma((HIGH,)), dma((2, HIGH)), dma((2, HIGH)),
            *[dma((3, HIGH))] * 6,
            dma((2, CHUNKS)), dma((2, CHUNKS)), dma((CHUNKS,)), dma((CHUNKS,)), dma((3, 3)), dma((3, 3)),
        ],
        compiler_params=pltpu.CompilerParams(collective_id=0, has_side_effects=True, vmem_limit_bytes=60 * 1024 * 1024),
    )(
        queries, key_vectors, values, lookback.reshape(1, -1), residual, out_weight,
        branch_gate.reshape(1, -1), final_shift.reshape(1, -1), final_scale.reshape(1, -1),
        final_weight.T, decoder_kernel, decoder_bias.reshape(1, -1),
    )


def one_slab_a_frame(mesh):
    return (mesh.shape["blk"], mesh.shape["head"], mesh.shape["dec"]) == (FRAMES, 2, 2)


def solution(mesh):
    in_specs = (
        P("blk", ("head", "dec")),
        P("blk", ("head", "dec")),
        P("blk", ("head", "dec")),
        P(),
        P(("blk", "head", "dec"), None),
        P(("head", "dec"), None),
        P(),
        P(),
        P(),
        P(),
        P(),
        P(),
    )
    out_specs = P(("blk", "head", "dec"), None, None)
    body = fused if one_slab_a_frame(mesh) else per_device
    return jax.shard_map(
        body, mesh=mesh, in_specs=in_specs, out_specs=out_specs, check_vma=False
    )
```

```python
import functools

import jax
import jax.numpy as jnp
from jax import lax
from jax.experimental import pallas as pl
from jax.experimental.pallas import tpu as pltpu
from jax.sharding import PartitionSpec as P

DH = 128
LC = 16
FRAMES = 8
PW = 32


def padded_2(cells, sides, width):
    for axis, dim in sides:
        count = lax.axis_size(axis)
        ends = count - 1
        head = lax.slice_in_dim(cells, 0, width, axis=dim)
        tail = lax.slice_in_dim(cells, cells.shape[dim] - width, cells.shape[dim], axis=dim)
        cells = jnp.concatenate(
            [
                lax.ppermute(tail, axis, [(i, (i + 1) % count) for i in range(ends)]),
                cells,
                lax.ppermute(head, axis, [((i + 1) % count, i) for i in range(ends)]),
            ],
            axis=dim,
        )
    return cells


def from_behind(x, axis, by):
    peers = lax.axis_size(axis)
    pairs = [(i, i + by) for i in range(peers) if 0 <= i + by < peers]
    return lax.ppermute(x, axis, pairs)


def attend_block(carry, shard_pair, query_heads, query_frame, lookback_heads, frame_len):
    running_max, row_total, accumulated = carry
    key_block, value_block = shard_pair
    key_count = key_block.shape[0]
    head_count = query_heads.shape[1]
    key_heads = key_block.reshape(key_count, head_count, DH)
    value_heads = value_block.reshape(key_count, head_count, DH)
    scores = jnp.einsum(
        "qhd,khd->hqk", query_heads, key_heads, preferred_element_type=jnp.float32
    ) * DH ** (-0.5)
    key_pos = jnp.arange(key_count, dtype=jnp.int32)
    key_frame = key_pos // frame_len
    visible = (
        (key_pos >= 0)[None, None, :]
        & (key_frame[None, None, :] <= query_frame[None, :, None])
        & (key_frame[None, None, :] >= query_frame[None, :, None] - lookback_heads[:, None, None])
    )
    masked = jnp.where(visible, scores, -1e30)
    newest_max = jnp.maximum(running_max, jnp.max(masked, axis=2))
    weights = jnp.where(visible, jnp.exp(scores - newest_max[:, :, None]), 0.0).astype(jnp.bfloat16)
    row_total = jnp.sum(weights.astype(jnp.float32), axis=2)
    accumulated = jnp.einsum(
        "hqk,khd->hqd", weights, value_heads, preferred_element_type=jnp.float32
    )
    return (newest_max, row_total, accumulated)


def per_device(
    queries,
    key_vectors,
    values,
    lookback,
    residual,
    out_weight,
    branch_gate,
    final_shift,
    final_scale,
    final_weight,
    decoder_kernel,
    decoder_bias,
):
    slab_rows = queries.shape[0]
    head_count = queries.shape[1] // DH
    blocks = lax.axis_size("blk")
    block_index = lax.axis_index("blk")
    frame_len = slab_rows * blocks // FRAMES
    query_heads = queries.reshape(slab_rows, head_count, DH)
    query_frame = (block_index * slab_rows + jnp.arange(slab_rows, dtype=jnp.int32)) // frame_len
    lookback_heads = lax.dynamic_slice_in_dim(
        lookback, lax.axis_index(("head", "dec")) * head_count, head_count
    )
    initial = (
        jnp.full((head_count, slab_rows), -1e30, jnp.float32),
        jnp.zeros((head_count, slab_rows), jnp.float32),
        jnp.zeros((head_count, slab_rows, DH), jnp.float32),
    )
    carry = attend_block(
        initial,
        (
            lax.all_gather(key_vectors, "blk", axis=0, tiled=True),
            lax.all_gather(values, "blk", axis=0, tiled=True),
        ),
        query_heads,
        query_frame,
        lookback_heads,
        frame_len,
    )
    newest_max, row_total, accumulated = carry
    attended = (
        (accumulated / row_total[:, :, None])
        .transpose(1, 0, 2)
        .reshape(slab_rows, head_count * DH)
        .astype(jnp.bfloat16)
    )
    tokens_dev = slab_rows // lax.axis_size(("head", "dec"))
    projected = lax.psum_scatter(
        jnp.dot(attended, out_weight, preferred_element_type=jnp.float32).astype(jnp.bfloat16),
        ("head", "dec"),
        scatter_dimension=0,
        tiled=True,
    ).astype(jnp.float32)
    hidden = residual.astype(jnp.float32) + branch_gate[None, :] * projected
    center = jnp.mean(hidden, axis=1, keepdims=True)
    spread = jnp.mean((hidden - center) ** 2, axis=1, keepdims=True)
    normed = (
        (hidden - center) * lax.rsqrt(spread + 1e-06) * (1.0 + final_scale[None, :])
        + final_shift[None, :]
    ).astype(jnp.bfloat16)
    patches = jnp.dot(normed, final_weight, preferred_element_type=jnp.float32).astype(jnp.bfloat16)
    patch_rows = tokens_dev // PW
    tile_rows = 2 * patch_rows
    width = 2 * PW
    tile = (
        patches.reshape(patch_rows, PW, 2, 2, LC)
        .transpose(0, 2, 1, 3, 4)
        .reshape(tile_rows, width * LC)
    )
    padded = padded_2(tile, ((("blk", "head", "dec"), 0),), 1)
    frame_stride = blocks // FRAMES
    frame_index = block_index // frame_stride
    prior_one = from_behind(padded, "blk", frame_stride)
    prior_one = jnp.where(frame_index >= 1, prior_one, padded)
    prior_two = from_behind(prior_one, "blk", frame_stride)
    prior_two = jnp.where(frame_index >= 1, prior_two, padded)
    history = jnp.stack([prior_two, prior_one, padded]).reshape(3, tile_rows + 2, width, LC)
    history = jnp.pad(history, ((0, 0), (0, 0), (1, 1), (0, 0)))
    windows = [
        history[time_tap, row_tap : row_tap + tile_rows, column_tap : column_tap + width, :]
        for time_tap in range(3)
        for row_tap in range(3)
        for column_tap in range(3)
    ]
    columns = jnp.concatenate(windows, axis=-1).reshape(tile_rows * width, 27 * LC)
    summed = (
        jnp.dot(columns, decoder_kernel, preferred_element_type=jnp.float32) + decoder_bias[None, :]
    )
    return summed.astype(jnp.bfloat16).reshape(tile_rows, width, decoder_kernel.shape[1])


HIGH = 3
CHUNKS = 6
STEPS = (2, 4, 1)
SIDE = (1, 2)
LOG2_E = 1.4426950408889634
MESH = pl.DeviceIdType.MESH


def fused_kernel(
    q_hbm, k_hbm, v_hbm, look_hbm, res_hbm, w_hbm, gate_hbm, shift_hbm, scale_hbm, fw_hbm, dk_hbm, db_hbm,
    out_ref,
    lookback, kz, kx, qv, asked, mixed_out, mixed_in, level_out, level_in, wv, resv, gatev, shiftv, scalev, fwv, dkv, dbv,
    top, total, acc, att, part, from_dec, to_y, from_y, hid, halo, wide, canvas,
    load_sem, kv_sem, zs, zr, xs, xr, qs, qr, os, orr, ls, lr, ds, dr, ys, yr, hs, hr,
):
    f = lax.axis_index("blk")
    hd = lax.axis_index("head")
    dc = lax.axis_index("dec")
    z, x = f // 2, f % 2
    n = f * 4 + hd * 2 + dc
    slab = q_hbm.shape[0]
    columns = w_hbm.shape[1] // CHUNKS

    barrier = pltpu.get_barrier_semaphore()
    greeted = jnp.int32(1)
    pl.semaphore_signal(barrier, inc=1, device_id=(f, 1 - hd, dc), device_id_type=MESH)
    for apart in (1, 3, 4, 5, 7, 8, 9):
        for m in (n - apart, n + apart):
            there = (m >= 0) & (m < 32)
            greeted = greeted + jnp.where(there, 1, 0)

            @pl.when(there)
            def _():
                pl.semaphore_signal(
                    barrier, inc=1, device_id=(m // 4, (m % 4) // 2, m % 2), device_id_type=MESH
                )

    @pl.when((f == 2) | (f == 6))
    def _():
        pl.semaphore_signal(barrier, inc=1, device_id=(8 - f, hd, dc), device_id_type=MESH)

    greeted = greeted + jnp.where((f == 2) | (f == 6), 1, 0)

    kv_loads = []
    for h in range(HIGH):
        for which, src in enumerate((k_hbm, v_hbm)):
            kv_loads.append(
                pltpu.make_async_copy(
                    src.at[:, pl.ds(h * DH, DH)], kz.at[0, h, which], kv_sem.at[2 * h + which]
                )
            )
    loads = [
        pltpu.make_async_copy(src, dst, load_sem.at[i])
        for i, (src, dst) in enumerate(
            (
                *[(q_hbm.at[:, pl.ds(h * DH, DH)], qv.at[h]) for h in range(HIGH)],
                (dk_hbm, dkv), (look_hbm, lookback), (w_hbm, wv), (res_hbm, resv), (gate_hbm, gatev),
                (shift_hbm, shiftv), (scale_hbm, scalev), (fw_hbm, fwv), (db_hbm, dbv),
            )
        )
    ]
    for c in kv_loads + loads:
        c.start()

    def up(h):
        return pltpu.make_async_remote_copy(
            src_ref=kz.at[0, h], dst_ref=kz.at[1, h], send_sem=zs.at[h], recv_sem=zr.at[h],
            device_id=(f + 2, hd, dc), device_id_type=MESH,
        )

    def own_across(h):
        return pltpu.make_async_remote_copy(
            src_ref=kz.at[0, h], dst_ref=kx.at[0, h], send_sem=xs.at[0, h], recv_sem=xr.at[0, h],
            device_id=(f + 1, hd, dc), device_id_type=MESH,
        )

    def lower_across(h):
        return pltpu.make_async_remote_copy(
            src_ref=kz.at[1, h], dst_ref=kx.at[1 - x, h], send_sem=xs.at[1, h], recv_sem=xr.at[1 - x, h],
            device_id=(f + 1 - 2 * x, hd, dc), device_id_type=MESH,
        )

    def arrived(slot, h):
        pltpu.make_async_remote_copy(
            src_ref=kz.at[1, h], dst_ref=kx.at[slot, h], send_sem=xs.at[1, h], recv_sem=xr.at[slot, h],
            device_id=(f + 1 - 2 * x, hd, dc), device_id_type=MESH,
        ).wait_recv()

    def ask(far, h):
        return pltpu.make_async_remote_copy(
            src_ref=qv.at[h], dst_ref=asked.at[far, h], send_sem=qs.at[far, h], recv_sem=qr.at[far, h],
            device_id=(f - STEPS[far], hd, dc), device_id_type=MESH,
        )

    def answer(far, h):
        to = (f + STEPS[far], hd, dc)
        return (
            pltpu.make_async_remote_copy(
                src_ref=mixed_out.at[far, h], dst_ref=mixed_in.at[far, h],
                send_sem=os.at[far, h], recv_sem=orr.at[far, h], device_id=to, device_id_type=MESH,
            ),
            pltpu.make_async_remote_copy(
                src_ref=level_out.at[far, h], dst_ref=level_in.at[far, h],
                send_sem=ls.at[far, h], recv_sem=lr.at[far, h], device_id=to, device_id_type=MESH,
            ),
        )

    asks = (z >= 2, f == 6, x == 1)
    helps = ((z >= 1) & (z <= 2), f == 2, x == 0)

    def kinds(h):
        return (0, 1, 2) if h in SIDE else (0, 1)


    for c in kv_loads:
        c.wait()
    for h in range(HIGH):
        loads[h].wait()
    pl.semaphore_wait(barrier, greeted)

    for h in range(HIGH):

        @pl.when(z < 3)
        def _():
            up(h).start()

        for far in kinds(h):

            @pl.when(asks[far])
            def _():
                ask(far, h).start()

        if h not in SIDE:

            @pl.when(x == 0)
            def _():
                own_across(h).start()

    def scored(query, key):
        return lax.dot_general(
            key, query, (((1,), (1,)), ((), ())), preferred_element_type=jnp.float32
        ) * (DH ** (-0.5) * LOG2_E)

    def visible(h, distance):
        return lookback[0, (hd * 2 + dc) * HIGH + h] >= distance

    def weighed(scores, shift, value):
        weights = jnp.exp2(scores + shift)
        mixed = lax.dot_general(
            value, weights.astype(jnp.bfloat16), (((0,), (0,)), ((), ())), preferred_element_type=jnp.float32
        )
        return jnp.sum(weights, axis=0, keepdims=True), mixed

    def attend(h, key, value, distance):
        scores = scored(qv[h], key)
        highest = jnp.max(scores, axis=0, keepdims=True)
        if isinstance(distance, int) and distance == 0:
            total[h], acc[h] = weighed(scores, -highest, value)
            top[h] = highest
        else:
            seen = visible(h, distance)
            newest = jnp.maximum(top[h], jnp.where(seen, highest, -1e30))
            added, mixed = weighed(scores, jnp.where(seen, -newest, -1e30), value)
            shrink = jnp.exp2(top[h] - newest)
            total[h] = total[h] * shrink + added
            acc[h] = acc[h] * shrink + mixed
            top[h] = newest

    def help_with(far, h, blocks):
        @pl.when(helps[far])
        def _():
            ask(far, h).wait_recv()
            query = asked[far, h]
            newest, scores = jnp.full((1, slab), -1e30, jnp.float32), []
            for key, _, distance in blocks:
                scores.append(scored(query, key))
                highest = jnp.max(scores[-1], axis=0, keepdims=True)
                newest = jnp.maximum(newest, jnp.where(visible(h, distance), highest, -1e30))
            added, mixed = 0.0, 0.0
            for each, (_, value, distance) in zip(scores, blocks):
                part_of = weighed(each, jnp.where(visible(h, distance), -newest, -1e30), value)
                added, mixed = added + part_of[0], mixed + part_of[1]
            added = jnp.where(added > 0.0, added, 1.0)
            mixed_out[far, h] = (mixed / added).astype(jnp.bfloat16)
            level_out[far, h] = jnp.broadcast_to(newest + jnp.log2(added), (8, slab))
            for copy in answer(far, h):
                copy.start()

    loads[HIGH].wait()
    loads[HIGH + 1].wait()
    for h in range(HIGH):
        attend(h, kz[0, h, 0], kz[0, h, 1], 0)

    for h in range(HIGH):

        @pl.when(z >= 1)
        def _():
            up(h).wait_recv()
            lower_across(h).start()
            attend(h, kz[1, h, 0], kz[1, h, 1], 2)

    for h in SIDE:
        help_with(2, h, ((kz[0, h, 0], kz[0, h, 1], 1),))

    wide[...] = jnp.zeros_like(wide)
    for a in range(2):
        for b in range(2):
            for t in range(3):
                for i in range(3):
                    for j in range(3):
                        ya, xb = a + i - 1, b + j - 1
                        row = ((t * 2 + ya // 2 - (a - 1)) * 2 + xb // 2 - (b - 1)) * 64
                        row += ((ya % 2) * 2 + xb % 2) * LC
                        tap = (t * 3 + i) * 3 + j
                        wide[a * 2 + b, row : row + LC, :] = dkv[tap * LC : (tap + 1) * LC, :]

    for h in range(HIGH):

        @pl.when(z >= 1)
        def _():
            arrived(x, h)
            lower = (kx[x, h, 0], kx[x, h, 1], 3 + 2 * x)
            help_with(0, h, (lower, (kz[1, h, 0], kz[1, h, 1], 4)))
            help_with(1, h, ((lower[0], lower[1], 5),))
            attend(h, kx[x, h, 0], kx[x, h, 1], 1 + 2 * x)

    for h in range(HIGH):
        if h in SIDE:
            continue

        @pl.when(x == 1)
        def _():
            arrived(0, h)
            attend(h, kx[0, h, 0], kx[0, h, 1], 1)

    for far in (2, 1, 0):
        for h in SIDE if far == 2 else range(HIGH):

            @pl.when(asks[far])
            def _():
                for copy in answer(far, h):
                    copy.wait_recv()
                level = level_in[far, h][:1]
                newest = jnp.maximum(top[h], level)
                shrink, grow = jnp.exp2(top[h] - newest), jnp.exp2(level - newest)
                total[h] = total[h] * shrink + grow
                acc[h] = acc[h] * shrink + mixed_in[far, h].astype(jnp.float32) * grow
                top[h] = newest

    for h in range(HIGH):
        att[:, :, h * DH : (h + 1) * DH] = (acc[h] / total[h]).T.astype(jnp.bfloat16).reshape(2, slab // 2, DH)

    def to_core(half, c):
        return pltpu.make_async_remote_copy(
            src_ref=part.at[c, half, 1 - dc], dst_ref=from_dec.at[c, half],
            send_sem=ds.at[half, c], recv_sem=dr.at[half, c],
            device_id=(f, hd, 1 - dc), device_id_type=MESH,
        )

    def to_row(c):
        return pltpu.make_async_remote_copy(
            src_ref=to_y.at[c], dst_ref=from_y.at[c], send_sem=ys.at[c], recv_sem=yr.at[c],
            device_id=(f, 1 - hd, dc), device_id_type=MESH,
        )

    loads[HIGH + 2].wait()
    def share(half, c):
        got = jnp.dot(
            att[half], wv[:, c * columns : (c + 1) * columns], preferred_element_type=jnp.float32
        ).astype(jnp.bfloat16)
        part[c, half] = got.reshape(2, slab // 4, columns)
        to_core(half, c).start()

    def both_cores(half, c):
        to_core(half, c).wait_recv()
        return part[c, half, dc].astype(jnp.float32) + from_dec[c, half].astype(jnp.float32)

    def pass_on(c):
        to_y[c] = both_cores(1 - hd, c).astype(jnp.bfloat16)
        to_row(c).start()

    for c in range(CHUNKS):
        share(1 - hd, c)
        if c >= 2:
            pass_on(c - 2)
    pass_on(CHUNKS - 2)
    pass_on(CHUNKS - 1)
    for c in range(CHUNKS):
        share(hd, c)
    for load in loads[HIGH + 3 :]:
        load.wait()
    for c in range(CHUNKS):
        cols = slice(c * columns, (c + 1) * columns)
        hid[c] = resv[:, cols].astype(jnp.float32) + gatev[:, cols] * both_cores(hd, c)
    summed = jnp.zeros((slab // 4, 1), jnp.float32)
    for c in range(CHUNKS):
        cols = slice(c * columns, (c + 1) * columns)
        to_row(c).wait_recv()
        hidden = hid[c] + gatev[:, cols] * from_y[c].astype(jnp.float32)
        hid[c] = hidden
        summed = summed + jnp.sum(hidden, axis=1, keepdims=True)
    center = summed / (CHUNKS * columns)
    squares = jnp.zeros((slab // 4, 1), jnp.float32)
    for c in range(CHUNKS):
        squares = squares + jnp.sum((hid[c] - center) ** 2, axis=1, keepdims=True)
    inverse = lax.rsqrt(squares / (CHUNKS * columns) + 1e-06)
    patches = jnp.zeros((slab // 4, fwv.shape[0]), jnp.float32)
    for c in range(CHUNKS):
        cols = slice(c * columns, (c + 1) * columns)
        normed = ((hid[c] - center) * inverse * (1.0 + scalev[:, cols]) + shiftv[:, cols]).astype(jnp.bfloat16)
        patches = patches + lax.dot_general(
            normed, fwv[:, cols], (((1,), (1,)), ((), ())), preferred_element_type=jnp.float32
        )
    halo[0, 1] = jnp.concatenate([patches, patches], axis=1).astype(jnp.bfloat16)

    def tile_to(back, side):
        m = n + 4 * back - side
        copy = pltpu.make_async_remote_copy(
            src_ref=halo.at[0, 1], dst_ref=halo.at[back, side + 1],
            send_sem=hs.at[back, side + 1], recv_sem=hr.at[back, side + 1],
            device_id=(m // 4, (m % 4) // 2, m % 2), device_id_type=MESH,
        )
        return copy, (m >= 4 * back) & (m < 32)

    def tile_comes(back, side):
        source = n - 4 * back + side
        return (f >= back) & (source >= 0) & (source < 32)

    reach = [(back, side) for back in (2, 1, 0) for side in (-1, 0, 1) if (back, side) != (0, 0)]
    for back, side in reach:
        copy, goes = tile_to(back, side)

        @pl.when(goes)
        def _():
            copy.start()

    for back, side in reach:

        @pl.when(tile_comes(back, side))
        def _():
            tile_to(back, side)[0].wait_recv()

    rows = 4 * PW
    lane = lax.broadcasted_iota(jnp.int32, (rows, 128), 1)
    token = lax.broadcasted_iota(jnp.int32, (rows, 128), 0) % PW
    pairs = []
    for t in range(3):
        back = jnp.minimum(2 - t, f)
        first = n - 4 * back
        above = jnp.where(first >= 1, halo[back, 0, PW:, :].astype(jnp.float32), 0.0)
        below = jnp.where(first <= 30, halo[back, 2, :PW, :].astype(jnp.float32), 0.0)
        ext = jnp.concatenate([above, halo[back, 1].astype(jnp.float32), below], axis=0)
        before = jnp.where(token == 0, 0.0, pltpu.roll(ext, 1, 0))
        after = jnp.where(token == PW - 1, 0.0, pltpu.roll(ext, rows - 1, 0))
        pairs.append(
            (
                jnp.where(lane < 64, before, ext).astype(jnp.bfloat16),
                jnp.where(lane < 64, ext, after).astype(jnp.bfloat16),
            )
        )
    for a in range(2):
        for b in range(2):
            lhs = jnp.concatenate(
                [
                    pairs[t][b][(a + d) * PW : (a + d) * PW + 2 * PW]
                    for t in range(3)
                    for d in range(2)
                ],
                axis=1,
            )
            got = jnp.dot(lhs, wide[a * 2 + b], preferred_element_type=jnp.float32) + dbv[...]
            for r in range(2):
                for g in range(got.shape[1] // 128):
                    canvas[g, pl.ds((2 * r + a) * 2 * PW + b, PW, stride=2), :] = got[
                        r * PW : (r + 1) * PW, g * 128 : (g + 1) * 128
                    ]
    for y in range(4):
        for g in range(canvas.shape[0]):
            out_ref[y, :, g * 128 : (g + 1) * 128] = canvas[g, y * 2 * PW : (y + 1) * 2 * PW, :].astype(jnp.bfloat16)

    for h in range(HIGH):

        @pl.when(z < 3)
        def _():
            up(h).wait_send()

        @pl.when(z >= 1)
        def _():
            lower_across(h).wait_send()

        if h not in SIDE:

            @pl.when(x == 0)
            def _():
                own_across(h).wait_send()

        for far in kinds(h):

            @pl.when(asks[far])
            def _():
                ask(far, h).wait_send()

            @pl.when(helps[far])
            def _():
                for copy in answer(far, h):
                    copy.wait_send()

    for c in range(CHUNKS):
        to_core(hd, c).wait_send()
        to_core(1 - hd, c).wait_send()
        to_row(c).wait_send()
    for back, side in reach:
        copy, goes = tile_to(back, side)

        @pl.when(goes)
        def _():
            copy.wait_send()


def fused(
    queries, key_vectors, values, lookback, residual, out_weight,
    branch_gate, final_shift, final_scale, final_weight, decoder_kernel, decoder_bias,
):
    slab, width = queries.shape
    model = out_weight.shape[1]
    quarter, columns = slab // 4, model // CHUNKS
    outputs = decoder_kernel.shape[1]
    bf, f32 = jnp.bfloat16, jnp.float32
    vm, dma = pltpu.VMEM, pltpu.SemaphoreType.DMA
    hbm = pl.BlockSpec(memory_space=pltpu.HBM)
    return pl.pallas_call(
        fused_kernel,
        out_shape=pltpu.VMEM((4, 2 * PW, outputs), bf),
        in_specs=[hbm] * 12,
        out_specs=pl.BlockSpec(memory_space=pltpu.VMEM),
        scratch_shapes=[
            pltpu.SMEM((1, lookback.shape[0]), jnp.int32),
            vm((2, HIGH, 2, slab, DH), bf), vm((2, HIGH, 2, slab, DH), bf), vm((HIGH, slab, DH), bf),
            vm((3, HIGH, slab, DH), bf), *[vm((3, HIGH, DH, slab), bf)] * 2, *[vm((3, HIGH, 8, slab), f32)] * 2,
            vm((width, model), bf), vm((quarter, model), bf),
            vm((1, model), f32), vm((1, model), f32), vm((1, model), f32),
            vm(final_weight.shape[::-1], bf), vm(decoder_kernel.shape, bf), vm((1, outputs), f32),
            vm((HIGH, 1, slab), f32), vm((HIGH, 1, slab), f32), vm((HIGH, DH, slab), f32),
            vm((2, slab // 2, width), bf), vm((CHUNKS, 2, 2, quarter, columns), bf),
            vm((CHUNKS, 2, quarter, columns), bf), vm((CHUNKS, quarter, columns), bf),
            vm((CHUNKS, quarter, columns), bf), vm((CHUNKS, quarter, columns), f32),
            vm((3, 3, quarter, 128), bf), vm((4, 768, outputs), bf), vm((outputs // 128, 256, 128), f32),
            dma((HIGH + 9,)), dma((6,)), dma((HIGH,)), dma((HIGH,)), dma((2, HIGH)), dma((2, HIGH)),
            *[dma((3, HIGH))] * 6,
            dma((2, CHUNKS)), dma((2, CHUNKS)), dma((CHUNKS,)), dma((CHUNKS,)), dma((3, 3)), dma((3, 3)),
        ],
        compiler_params=pltpu.CompilerParams(collective_id=0, has_side_effects=True, vmem_limit_bytes=60 * 1024 * 1024),
    )(
        queries, key_vectors, values, lookback.reshape(1, -1), residual, out_weight,
        branch_gate.reshape(1, -1), final_shift.reshape(1, -1), final_scale.reshape(1, -1),
        final_weight.T, decoder_kernel, decoder_bias.reshape(1, -1),
    )


def one_slab_a_frame(mesh):
    return (mesh.shape["blk"], mesh.shape["head"], mesh.shape["dec"]) == (FRAMES, 2, 2)


def solution(mesh):
    in_specs = (
        P("blk", ("head", "dec")),
        P("blk", ("head", "dec")),
        P("blk", ("head", "dec")),
        P(),
        P(("blk", "head", "dec"), None),
        P(("head", "dec"), None),
        P(),
        P(),
        P(),
        P(),
        P(),
        P(),
    )
    out_specs = P(("blk", "head", "dec"), None, None)
    body = fused if one_slab_a_frame(mesh) else per_device
    return jax.shard_map(
        body, mesh=mesh, in_specs=in_specs, out_specs=out_specs, check_vma=False
    )
```

```python
import functools

import jax
import jax.numpy as jnp
from jax import lax
from jax.experimental import pallas as pl
from jax.experimental.pallas import tpu as pltpu
from jax.sharding import PartitionSpec as P

DH = 128
LC = 16
FRAMES = 8
PW = 32


def padded_2(cells, sides, width):
    for axis, dim in sides:
        count = lax.axis_size(axis)
        ends = count - 1
        head = lax.slice_in_dim(cells, 0, width, axis=dim)
        tail = lax.slice_in_dim(cells, cells.shape[dim] - width, cells.shape[dim], axis=dim)
        cells = jnp.concatenate(
            [
                lax.ppermute(tail, axis, [(i, (i + 1) % count) for i in range(ends)]),
                cells,
                lax.ppermute(head, axis, [((i + 1) % count, i) for i in range(ends)]),
            ],
            axis=dim,
        )
    return cells


def from_behind(x, axis, by):
    peers = lax.axis_size(axis)
    pairs = [(i, i + by) for i in range(peers) if 0 <= i + by < peers]
    return lax.ppermute(x, axis, pairs)


def attend_block(carry, shard_pair, query_heads, query_frame, lookback_heads, frame_len):
    running_max, row_total, accumulated = carry
    key_block, value_block = shard_pair
    key_count = key_block.shape[0]
    head_count = query_heads.shape[1]
    key_heads = key_block.reshape(key_count, head_count, DH)
    value_heads = value_block.reshape(key_count, head_count, DH)
    scores = jnp.einsum(
        "qhd,khd->hqk", query_heads, key_heads, preferred_element_type=jnp.float32
    ) * DH ** (-0.5)
    key_pos = jnp.arange(key_count, dtype=jnp.int32)
    key_frame = key_pos // frame_len
    visible = (
        (key_pos >= 0)[None, None, :]
        & (key_frame[None, None, :] <= query_frame[None, :, None])
        & (key_frame[None, None, :] >= query_frame[None, :, None] - lookback_heads[:, None, None])
    )
    masked = jnp.where(visible, scores, -1e30)
    newest_max = jnp.maximum(running_max, jnp.max(masked, axis=2))
    weights = jnp.where(visible, jnp.exp(scores - newest_max[:, :, None]), 0.0).astype(jnp.bfloat16)
    row_total = jnp.sum(weights.astype(jnp.float32), axis=2)
    accumulated = jnp.einsum(
        "hqk,khd->hqd", weights, value_heads, preferred_element_type=jnp.float32
    )
    return (newest_max, row_total, accumulated)


def per_device(
    queries,
    key_vectors,
    values,
    lookback,
    residual,
    out_weight,
    branch_gate,
    final_shift,
    final_scale,
    final_weight,
    decoder_kernel,
    decoder_bias,
):
    slab_rows = queries.shape[0]
    head_count = queries.shape[1] // DH
    blocks = lax.axis_size("blk")
    block_index = lax.axis_index("blk")
    frame_len = slab_rows * blocks // FRAMES
    query_heads = queries.reshape(slab_rows, head_count, DH)
    query_frame = (block_index * slab_rows + jnp.arange(slab_rows, dtype=jnp.int32)) // frame_len
    lookback_heads = lax.dynamic_slice_in_dim(
        lookback, lax.axis_index(("head", "dec")) * head_count, head_count
    )
    initial = (
        jnp.full((head_count, slab_rows), -1e30, jnp.float32),
        jnp.zeros((head_count, slab_rows), jnp.float32),
        jnp.zeros((head_count, slab_rows, DH), jnp.float32),
    )
    carry = attend_block(
        initial,
        (
            lax.all_gather(key_vectors, "blk", axis=0, tiled=True),
            lax.all_gather(values, "blk", axis=0, tiled=True),
        ),
        query_heads,
        query_frame,
        lookback_heads,
        frame_len,
    )
    newest_max, row_total, accumulated = carry
    attended = (
        (accumulated / row_total[:, :, None])
        .transpose(1, 0, 2)
        .reshape(slab_rows, head_count * DH)
        .astype(jnp.bfloat16)
    )
    tokens_dev = slab_rows // lax.axis_size(("head", "dec"))
    projected = lax.psum_scatter(
        jnp.dot(attended, out_weight, preferred_element_type=jnp.float32).astype(jnp.bfloat16),
        ("head", "dec"),
        scatter_dimension=0,
        tiled=True,
    ).astype(jnp.float32)
    hidden = residual.astype(jnp.float32) + branch_gate[None, :] * projected
    center = jnp.mean(hidden, axis=1, keepdims=True)
    spread = jnp.mean((hidden - center) ** 2, axis=1, keepdims=True)
    normed = (
        (hidden - center) * lax.rsqrt(spread + 1e-06) * (1.0 + final_scale[None, :])
        + final_shift[None, :]
    ).astype(jnp.bfloat16)
    patches = jnp.dot(normed, final_weight, preferred_element_type=jnp.float32).astype(jnp.bfloat16)
    patch_rows = tokens_dev // PW
    tile_rows = 2 * patch_rows
    width = 2 * PW
    tile = (
        patches.reshape(patch_rows, PW, 2, 2, LC)
        .transpose(0, 2, 1, 3, 4)
        .reshape(tile_rows, width * LC)
    )
    padded = padded_2(tile, ((("blk", "head", "dec"), 0),), 1)
    frame_stride = blocks // FRAMES
    frame_index = block_index // frame_stride
    prior_one = from_behind(padded, "blk", frame_stride)
    prior_one = jnp.where(frame_index >= 1, prior_one, padded)
    prior_two = from_behind(prior_one, "blk", frame_stride)
    prior_two = jnp.where(frame_index >= 1, prior_two, padded)
    history = jnp.stack([prior_two, prior_one, padded]).reshape(3, tile_rows + 2, width, LC)
    history = jnp.pad(history, ((0, 0), (0, 0), (1, 1), (0, 0)))
    windows = [
        history[time_tap, row_tap : row_tap + tile_rows, column_tap : column_tap + width, :]
        for time_tap in range(3)
        for row_tap in range(3)
        for column_tap in range(3)
    ]
    columns = jnp.concatenate(windows, axis=-1).reshape(tile_rows * width, 27 * LC)
    summed = (
        jnp.dot(columns, decoder_kernel, preferred_element_type=jnp.float32) + decoder_bias[None, :]
    )
    return summed.astype(jnp.bfloat16).reshape(tile_rows, width, decoder_kernel.shape[1])


HIGH = 3
CHUNKS = 6
STEPS = (2, 4, 1)
SIDE = (1, 2)
LOG2_E = 1.4426950408889634
MESH = pl.DeviceIdType.MESH


def fused_kernel(
    q_hbm, k_hbm, v_hbm, look_hbm, res_hbm, w_hbm, gate_hbm, shift_hbm, scale_hbm, fw_hbm, dk_hbm, db_hbm,
    out_ref,
    lookback, kz, kx, qv, asked, mixed_out, mixed_in, level_out, level_in, wv, resv, gatev, shiftv, scalev, fwv, dkv, dbv,
    top, total, acc, att, part, from_dec, to_y, from_y, hid, halo, wide, canvas,
    load_sem, kv_sem, zs, zr, xs, xr, qs, qr, os, orr, ls, lr, ds, dr, ys, yr, hs, hr,
):
    f = lax.axis_index("blk")
    hd = lax.axis_index("head")
    dc = lax.axis_index("dec")
    z, x = f // 2, f % 2
    n = f * 4 + hd * 2 + dc
    slab = q_hbm.shape[0]
    columns = w_hbm.shape[1] // CHUNKS

    barrier = pltpu.get_barrier_semaphore()
    greeted = jnp.int32(1)
    pl.semaphore_signal(barrier, inc=1, device_id=(f, 1 - hd, dc), device_id_type=MESH)
    for apart in (1, 3, 4, 5, 7, 8, 9):
        for m in (n - apart, n + apart):
            there = (m >= 0) & (m < 32)
            greeted = greeted + jnp.where(there, 1, 0)

            @pl.when(there)
            def _():
                pl.semaphore_signal(
                    barrier, inc=1, device_id=(m // 4, (m % 4) // 2, m % 2), device_id_type=MESH
                )

    @pl.when((f == 2) | (f == 6))
    def _():
        pl.semaphore_signal(barrier, inc=1, device_id=(8 - f, hd, dc), device_id_type=MESH)

    greeted = greeted + jnp.where((f == 2) | (f == 6), 1, 0)

    kv_loads = []
    for h in range(HIGH):
        for which, src in enumerate((k_hbm, v_hbm)):
            kv_loads.append(
                pltpu.make_async_copy(
                    src.at[:, pl.ds(h * DH, DH)], kz.at[0, h, which], kv_sem.at[2 * h + which]
                )
            )
    loads = [
        pltpu.make_async_copy(src, dst, load_sem.at[i])
        for i, (src, dst) in enumerate(
            (
                *[(q_hbm.at[:, pl.ds(h * DH, DH)], qv.at[h]) for h in range(HIGH)],
                (dk_hbm, dkv), (look_hbm, lookback), (w_hbm, wv), (res_hbm, resv), (gate_hbm, gatev),
                (shift_hbm, shiftv), (scale_hbm, scalev), (fw_hbm, fwv), (db_hbm, dbv),
            )
        )
    ]
    for c in kv_loads + loads:
        c.start()

    def up(h):
        return pltpu.make_async_remote_copy(
            src_ref=kz.at[0, h], dst_ref=kz.at[1, h], send_sem=zs.at[h], recv_sem=zr.at[h],
            device_id=(f + 2, hd, dc), device_id_type=MESH,
        )

    def own_across(h):
        return pltpu.make_async_remote_copy(
            src_ref=kz.at[0, h], dst_ref=kx.at[0, h], send_sem=xs.at[0, h], recv_sem=xr.at[0, h],
            device_id=(f + 1, hd, dc), device_id_type=MESH,
        )

    def lower_across(h):
        return pltpu.make_async_remote_copy(
            src_ref=kz.at[1, h], dst_ref=kx.at[1 - x, h], send_sem=xs.at[1, h], recv_sem=xr.at[1 - x, h],
            device_id=(f + 1 - 2 * x, hd, dc), device_id_type=MESH,
        )

    def arrived(slot, h):
        pltpu.make_async_remote_copy(
            src_ref=kz.at[1, h], dst_ref=kx.at[slot, h], send_sem=xs.at[1, h], recv_sem=xr.at[slot, h],
            device_id=(f + 1 - 2 * x, hd, dc), device_id_type=MESH,
        ).wait_recv()

    def ask(far, h):
        return pltpu.make_async_remote_copy(
            src_ref=qv.at[h], dst_ref=asked.at[far, h], send_sem=qs.at[far, h], recv_sem=qr.at[far, h],
            device_id=(f - STEPS[far], hd, dc), device_id_type=MESH,
        )

    def answer(far, h):
        to = (f + STEPS[far], hd, dc)
        return (
            pltpu.make_async_remote_copy(
                src_ref=mixed_out.at[far, h], dst_ref=mixed_in.at[far, h],
                send_sem=os.at[far, h], recv_sem=orr.at[far, h], device_id=to, device_id_type=MESH,
            ),
            pltpu.make_async_remote_copy(
                src_ref=level_out.at[far, h], dst_ref=level_in.at[far, h],
                send_sem=ls.at[far, h], recv_sem=lr.at[far, h], device_id=to, device_id_type=MESH,
            ),
        )

    asks = (z >= 2, f == 6, x == 1)
    helps = ((z >= 1) & (z <= 2), f == 2, x == 0)

    def kinds(h):
        return (0, 1, 2) if h in SIDE else (0, 1)


    for c in kv_loads:
        c.wait()
    for h in range(HIGH):
        loads[h].wait()
    pl.semaphore_wait(barrier, greeted)

    for far in (2, 0, 1):
        for h in SIDE if far == 2 else range(HIGH):

            @pl.when(asks[far])
            def _():
                ask(far, h).start()

    for h in range(HIGH):

        @pl.when(z < 3)
        def _():
            up(h).start()

        if h not in SIDE:

            @pl.when(x == 0)
            def _():
                own_across(h).start()

    def scored(query, key):
        return lax.dot_general(
            key, query, (((1,), (1,)), ((), ())), preferred_element_type=jnp.float32
        ) * (DH ** (-0.5) * LOG2_E)

    def visible(h, distance):
        return lookback[0, (hd * 2 + dc) * HIGH + h] >= distance

    def weighed(scores, shift, value):
        weights = jnp.exp2(scores + shift)
        mixed = lax.dot_general(
            value, weights.astype(jnp.bfloat16), (((0,), (0,)), ((), ())), preferred_element_type=jnp.float32
        )
        return jnp.sum(weights, axis=0, keepdims=True), mixed

    def attend(h, key, value, distance):
        scores = scored(qv[h], key)
        highest = jnp.max(scores, axis=0, keepdims=True)
        if isinstance(distance, int) and distance == 0:
            total[h], acc[h] = weighed(scores, -highest, value)
            top[h] = highest
        else:
            seen = visible(h, distance)
            newest = jnp.maximum(top[h], jnp.where(seen, highest, -1e30))
            added, mixed = weighed(scores, jnp.where(seen, -newest, -1e30), value)
            shrink = jnp.exp2(top[h] - newest)
            total[h] = total[h] * shrink + added
            acc[h] = acc[h] * shrink + mixed
            top[h] = newest

    def help_with(far, h, blocks):
        @pl.when(helps[far])
        def _():
            ask(far, h).wait_recv()
            query = asked[far, h]
            newest, scores = jnp.full((1, slab), -1e30, jnp.float32), []
            for key, _, distance in blocks:
                scores.append(scored(query, key))
                highest = jnp.max(scores[-1], axis=0, keepdims=True)
                newest = jnp.maximum(newest, jnp.where(visible(h, distance), highest, -1e30))
            added, mixed = 0.0, 0.0
            for each, (_, value, distance) in zip(scores, blocks):
                part_of = weighed(each, jnp.where(visible(h, distance), -newest, -1e30), value)
                added, mixed = added + part_of[0], mixed + part_of[1]
            added = jnp.where(added > 0.0, added, 1.0)
            mixed_out[far, h] = (mixed / added).astype(jnp.bfloat16)
            level_out[far, h] = jnp.broadcast_to(newest + jnp.log2(added), (8, slab))
            for copy in answer(far, h):
                copy.start()

    loads[HIGH].wait()
    loads[HIGH + 1].wait()
    for h in range(HIGH):
        attend(h, kz[0, h, 0], kz[0, h, 1], 0)

    wide[...] = jnp.zeros_like(wide)
    for a in range(2):
        for b in range(2):
            for t in range(3):
                for i in range(3):
                    for j in range(3):
                        ya, xb = a + i - 1, b + j - 1
                        row = ((t * 2 + ya // 2 - (a - 1)) * 2 + xb // 2 - (b - 1)) * 64
                        row += ((ya % 2) * 2 + xb % 2) * LC
                        tap = (t * 3 + i) * 3 + j
                        wide[a * 2 + b, row : row + LC, :] = dkv[tap * LC : (tap + 1) * LC, :]

    for h in SIDE:
        help_with(2, h, ((kz[0, h, 0], kz[0, h, 1], 1),))

    def from_below(h):
        @pl.when(z >= 1)
        def _():
            up(h).wait_recv()
            lower_across(h).start()
            attend(h, kz[1, h, 0], kz[1, h, 1], 2)

    def from_beside(h):
        @pl.when(z >= 1)
        def _():
            arrived(x, h)
            lower = (kx[x, h, 0], kx[x, h, 1], 3 + 2 * x)
            help_with(0, h, (lower, (kz[1, h, 0], kz[1, h, 1], 4)))
            help_with(1, h, ((lower[0], lower[1], 5),))
            attend(h, kx[x, h, 0], kx[x, h, 1], 1 + 2 * x)

    for h in range(HIGH):
        from_below(h)
        if h:
            from_beside(h - 1)
    from_beside(HIGH - 1)

    for h in range(HIGH):
        if h in SIDE:
            continue

        @pl.when(x == 1)
        def _():
            arrived(0, h)
            attend(h, kx[0, h, 0], kx[0, h, 1], 1)

    for far in (2, 1, 0):
        for h in SIDE if far == 2 else range(HIGH):

            @pl.when(asks[far])
            def _():
                for copy in answer(far, h):
                    copy.wait_recv()
                level = level_in[far, h][:1]
                newest = jnp.maximum(top[h], level)
                shrink, grow = jnp.exp2(top[h] - newest), jnp.exp2(level - newest)
                total[h] = total[h] * shrink + grow
                acc[h] = acc[h] * shrink + mixed_in[far, h].astype(jnp.float32) * grow
                top[h] = newest

    for h in range(HIGH):
        att[:, :, h * DH : (h + 1) * DH] = (acc[h] / total[h]).T.astype(jnp.bfloat16).reshape(2, slab // 2, DH)

    def to_core(half, c):
        return pltpu.make_async_remote_copy(
            src_ref=part.at[c, half, 1 - dc], dst_ref=from_dec.at[c, half],
            send_sem=ds.at[half, c], recv_sem=dr.at[half, c],
            device_id=(f, hd, 1 - dc), device_id_type=MESH,
        )

    def to_row(c):
        return pltpu.make_async_remote_copy(
            src_ref=to_y.at[c], dst_ref=from_y.at[c], send_sem=ys.at[c], recv_sem=yr.at[c],
            device_id=(f, 1 - hd, dc), device_id_type=MESH,
        )

    loads[HIGH + 2].wait()
    def share(half, c):
        got = jnp.dot(
            att[half], wv[:, c * columns : (c + 1) * columns], preferred_element_type=jnp.float32
        ).astype(jnp.bfloat16)
        part[c, half] = got.reshape(2, slab // 4, columns)
        to_core(half, c).start()

    def both_cores(half, c):
        to_core(half, c).wait_recv()
        return part[c, half, dc].astype(jnp.float32) + from_dec[c, half].astype(jnp.float32)

    def pass_on(c):
        to_y[c] = both_cores(1 - hd, c).astype(jnp.bfloat16)
        to_row(c).start()

    for c in range(CHUNKS):
        share(1 - hd, c)
        if c >= 2:
            pass_on(c - 2)
    pass_on(CHUNKS - 2)
    pass_on(CHUNKS - 1)
    for c in range(CHUNKS):
        share(hd, c)
    for load in loads[HIGH + 3 :]:
        load.wait()
    for c in range(CHUNKS):
        cols = slice(c * columns, (c + 1) * columns)
        hid[c] = resv[:, cols].astype(jnp.float32) + gatev[:, cols] * both_cores(hd, c)
    summed = jnp.zeros((slab // 4, 1), jnp.float32)
    for c in range(CHUNKS):
        cols = slice(c * columns, (c + 1) * columns)
        to_row(c).wait_recv()
        hidden = hid[c] + gatev[:, cols] * from_y[c].astype(jnp.float32)
        hid[c] = hidden
        summed = summed + jnp.sum(hidden, axis=1, keepdims=True)
    center = summed / (CHUNKS * columns)
    squares = jnp.zeros((slab // 4, 1), jnp.float32)
    for c in range(CHUNKS):
        squares = squares + jnp.sum((hid[c] - center) ** 2, axis=1, keepdims=True)
    inverse = lax.rsqrt(squares / (CHUNKS * columns) + 1e-06)
    patches = jnp.zeros((slab // 4, fwv.shape[0]), jnp.float32)
    for c in range(CHUNKS):
        cols = slice(c * columns, (c + 1) * columns)
        normed = ((hid[c] - center) * inverse * (1.0 + scalev[:, cols]) + shiftv[:, cols]).astype(jnp.bfloat16)
        patches = patches + lax.dot_general(
            normed, fwv[:, cols], (((1,), (1,)), ((), ())), preferred_element_type=jnp.float32
        )
    halo[0, 1] = jnp.concatenate([patches, patches], axis=1).astype(jnp.bfloat16)

    def tile_to(back, side):
        m = n + 4 * back - side
        copy = pltpu.make_async_remote_copy(
            src_ref=halo.at[0, 1], dst_ref=halo.at[back, side + 1],
            send_sem=hs.at[back, side + 1], recv_sem=hr.at[back, side + 1],
            device_id=(m // 4, (m % 4) // 2, m % 2), device_id_type=MESH,
        )
        return copy, (m >= 4 * back) & (m < 32)

    def tile_comes(back, side):
        source = n - 4 * back + side
        return (f >= back) & (source >= 0) & (source < 32)

    reach = [(back, side) for back in (2, 1, 0) for side in (-1, 0, 1) if (back, side) != (0, 0)]
    for back, side in reach:
        copy, goes = tile_to(back, side)

        @pl.when(goes)
        def _():
            copy.start()

    for back, side in reach:

        @pl.when(tile_comes(back, side))
        def _():
            tile_to(back, side)[0].wait_recv()

    rows = 4 * PW
    lane = lax.broadcasted_iota(jnp.int32, (rows, 128), 1)
    token = lax.broadcasted_iota(jnp.int32, (rows, 128), 0) % PW
    pairs = []
    for t in range(3):
        back = jnp.minimum(2 - t, f)
        first = n - 4 * back
        above = jnp.where(first >= 1, halo[back, 0, PW:, :].astype(jnp.float32), 0.0)
        below = jnp.where(first <= 30, halo[back, 2, :PW, :].astype(jnp.float32), 0.0)
        ext = jnp.concatenate([above, halo[back, 1].astype(jnp.float32), below], axis=0)
        before = jnp.where(token == 0, 0.0, pltpu.roll(ext, 1, 0))
        after = jnp.where(token == PW - 1, 0.0, pltpu.roll(ext, rows - 1, 0))
        pairs.append(
            (
                jnp.where(lane < 64, before, ext).astype(jnp.bfloat16),
                jnp.where(lane < 64, ext, after).astype(jnp.bfloat16),
            )
        )
    for a in range(2):
        for b in range(2):
            lhs = jnp.concatenate(
                [
                    pairs[t][b][(a + d) * PW : (a + d) * PW + 2 * PW]
                    for t in range(3)
                    for d in range(2)
                ],
                axis=1,
            )
            got = jnp.dot(lhs, wide[a * 2 + b], preferred_element_type=jnp.float32) + dbv[...]
            for r in range(2):
                for g in range(got.shape[1] // 128):
                    canvas[g, pl.ds((2 * r + a) * 2 * PW + b, PW, stride=2), :] = got[
                        r * PW : (r + 1) * PW, g * 128 : (g + 1) * 128
                    ]
    for y in range(4):
        for g in range(canvas.shape[0]):
            out_ref[y, :, g * 128 : (g + 1) * 128] = canvas[g, y * 2 * PW : (y + 1) * 2 * PW, :].astype(jnp.bfloat16)

    for h in range(HIGH):

        @pl.when(z < 3)
        def _():
            up(h).wait_send()

        @pl.when(z >= 1)
        def _():
            lower_across(h).wait_send()

        if h not in SIDE:

            @pl.when(x == 0)
            def _():
                own_across(h).wait_send()

        for far in kinds(h):

            @pl.when(asks[far])
            def _():
                ask(far, h).wait_send()

            @pl.when(helps[far])
            def _():
                for copy in answer(far, h):
                    copy.wait_send()

    for c in range(CHUNKS):
        to_core(hd, c).wait_send()
        to_core(1 - hd, c).wait_send()
        to_row(c).wait_send()
    for back, side in reach:
        copy, goes = tile_to(back, side)

        @pl.when(goes)
        def _():
            copy.wait_send()


def fused(
    queries, key_vectors, values, lookback, residual, out_weight,
    branch_gate, final_shift, final_scale, final_weight, decoder_kernel, decoder_bias,
):
    slab, width = queries.shape
    model = out_weight.shape[1]
    quarter, columns = slab // 4, model // CHUNKS
    outputs = decoder_kernel.shape[1]
    bf, f32 = jnp.bfloat16, jnp.float32
    vm, dma = pltpu.VMEM, pltpu.SemaphoreType.DMA
    hbm = pl.BlockSpec(memory_space=pltpu.HBM)
    return pl.pallas_call(
        fused_kernel,
        out_shape=pltpu.VMEM((4, 2 * PW, outputs), bf),
        in_specs=[hbm] * 12,
        out_specs=pl.BlockSpec(memory_space=pltpu.VMEM),
        scratch_shapes=[
            pltpu.SMEM((1, lookback.shape[0]), jnp.int32),
            vm((2, HIGH, 2, slab, DH), bf), vm((2, HIGH, 2, slab, DH), bf), vm((HIGH, slab, DH), bf),
            vm((3, HIGH, slab, DH), bf), *[vm((3, HIGH, DH, slab), bf)] * 2, *[vm((3, HIGH, 8, slab), f32)] * 2,
            vm((width, model), bf), vm((quarter, model), bf),
            vm((1, model), f32), vm((1, model), f32), vm((1, model), f32),
            vm(final_weight.shape[::-1], bf), vm(decoder_kernel.shape, bf), vm((1, outputs), f32),
            vm((HIGH, 1, slab), f32), vm((HIGH, 1, slab), f32), vm((HIGH, DH, slab), f32),
            vm((2, slab // 2, width), bf), vm((CHUNKS, 2, 2, quarter, columns), bf),
            vm((CHUNKS, 2, quarter, columns), bf), vm((CHUNKS, quarter, columns), bf),
            vm((CHUNKS, quarter, columns), bf), vm((CHUNKS, quarter, columns), f32),
            vm((3, 3, quarter, 128), bf), vm((4, 768, outputs), bf), vm((outputs // 128, 256, 128), f32),
            dma((HIGH + 9,)), dma((6,)), dma((HIGH,)), dma((HIGH,)), dma((2, HIGH)), dma((2, HIGH)),
            *[dma((3, HIGH))] * 6,
            dma((2, CHUNKS)), dma((2, CHUNKS)), dma((CHUNKS,)), dma((CHUNKS,)), dma((3, 3)), dma((3, 3)),
        ],
        compiler_params=pltpu.CompilerParams(collective_id=0, has_side_effects=True, vmem_limit_bytes=60 * 1024 * 1024),
    )(
        queries, key_vectors, values, lookback.reshape(1, -1), residual, out_weight,
        branch_gate.reshape(1, -1), final_shift.reshape(1, -1), final_scale.reshape(1, -1),
        final_weight.T, decoder_kernel, decoder_bias.reshape(1, -1),
    )


def one_slab_a_frame(mesh):
    return (mesh.shape["blk"], mesh.shape["head"], mesh.shape["dec"]) == (FRAMES, 2, 2)


def solution(mesh):
    in_specs = (
        P("blk", ("head", "dec")),
        P("blk", ("head", "dec")),
        P("blk", ("head", "dec")),
        P(),
        P(("blk", "head", "dec"), None),
        P(("head", "dec"), None),
        P(),
        P(),
        P(),
        P(),
        P(),
        P(),
    )
    out_specs = P(("blk", "head", "dec"), None, None)
    body = fused if one_slab_a_frame(mesh) else per_device
    return jax.shard_map(
        body, mesh=mesh, in_specs=in_specs, out_specs=out_specs, check_vma=False
    )
```

```python
import functools

import jax
import jax.numpy as jnp
from jax import lax
from jax.experimental import pallas as pl
from jax.experimental.pallas import tpu as pltpu
from jax.sharding import PartitionSpec as P

DH = 128
LC = 16
FRAMES = 8
PW = 32


def padded_2(cells, sides, width):
    for axis, dim in sides:
        count = lax.axis_size(axis)
        ends = count - 1
        head = lax.slice_in_dim(cells, 0, width, axis=dim)
        tail = lax.slice_in_dim(cells, cells.shape[dim] - width, cells.shape[dim], axis=dim)
        cells = jnp.concatenate(
            [
                lax.ppermute(tail, axis, [(i, (i + 1) % count) for i in range(ends)]),
                cells,
                lax.ppermute(head, axis, [((i + 1) % count, i) for i in range(ends)]),
            ],
            axis=dim,
        )
    return cells


def from_behind(x, axis, by):
    peers = lax.axis_size(axis)
    pairs = [(i, i + by) for i in range(peers) if 0 <= i + by < peers]
    return lax.ppermute(x, axis, pairs)


def attend_block(carry, shard_pair, query_heads, query_frame, lookback_heads, frame_len):
    running_max, row_total, accumulated = carry
    key_block, value_block = shard_pair
    key_count = key_block.shape[0]
    head_count = query_heads.shape[1]
    key_heads = key_block.reshape(key_count, head_count, DH)
    value_heads = value_block.reshape(key_count, head_count, DH)
    scores = jnp.einsum(
        "qhd,khd->hqk", query_heads, key_heads, preferred_element_type=jnp.float32
    ) * DH ** (-0.5)
    key_pos = jnp.arange(key_count, dtype=jnp.int32)
    key_frame = key_pos // frame_len
    visible = (
        (key_pos >= 0)[None, None, :]
        & (key_frame[None, None, :] <= query_frame[None, :, None])
        & (key_frame[None, None, :] >= query_frame[None, :, None] - lookback_heads[:, None, None])
    )
    masked = jnp.where(visible, scores, -1e30)
    newest_max = jnp.maximum(running_max, jnp.max(masked, axis=2))
    weights = jnp.where(visible, jnp.exp(scores - newest_max[:, :, None]), 0.0).astype(jnp.bfloat16)
    row_total = jnp.sum(weights.astype(jnp.float32), axis=2)
    accumulated = jnp.einsum(
        "hqk,khd->hqd", weights, value_heads, preferred_element_type=jnp.float32
    )
    return (newest_max, row_total, accumulated)


def per_device(
    queries,
    key_vectors,
    values,
    lookback,
    residual,
    out_weight,
    branch_gate,
    final_shift,
    final_scale,
    final_weight,
    decoder_kernel,
    decoder_bias,
):
    slab_rows = queries.shape[0]
    head_count = queries.shape[1] // DH
    blocks = lax.axis_size("blk")
    block_index = lax.axis_index("blk")
    frame_len = slab_rows * blocks // FRAMES
    query_heads = queries.reshape(slab_rows, head_count, DH)
    query_frame = (block_index * slab_rows + jnp.arange(slab_rows, dtype=jnp.int32)) // frame_len
    lookback_heads = lax.dynamic_slice_in_dim(
        lookback, lax.axis_index(("head", "dec")) * head_count, head_count
    )
    initial = (
        jnp.full((head_count, slab_rows), -1e30, jnp.float32),
        jnp.zeros((head_count, slab_rows), jnp.float32),
        jnp.zeros((head_count, slab_rows, DH), jnp.float32),
    )
    carry = attend_block(
        initial,
        (
            lax.all_gather(key_vectors, "blk", axis=0, tiled=True),
            lax.all_gather(values, "blk", axis=0, tiled=True),
        ),
        query_heads,
        query_frame,
        lookback_heads,
        frame_len,
    )
    newest_max, row_total, accumulated = carry
    attended = (
        (accumulated / row_total[:, :, None])
        .transpose(1, 0, 2)
        .reshape(slab_rows, head_count * DH)
        .astype(jnp.bfloat16)
    )
    tokens_dev = slab_rows // lax.axis_size(("head", "dec"))
    projected = lax.psum_scatter(
        jnp.dot(attended, out_weight, preferred_element_type=jnp.float32).astype(jnp.bfloat16),
        ("head", "dec"),
        scatter_dimension=0,
        tiled=True,
    ).astype(jnp.float32)
    hidden = residual.astype(jnp.float32) + branch_gate[None, :] * projected
    center = jnp.mean(hidden, axis=1, keepdims=True)
    spread = jnp.mean((hidden - center) ** 2, axis=1, keepdims=True)
    normed = (
        (hidden - center) * lax.rsqrt(spread + 1e-06) * (1.0 + final_scale[None, :])
        + final_shift[None, :]
    ).astype(jnp.bfloat16)
    patches = jnp.dot(normed, final_weight, preferred_element_type=jnp.float32).astype(jnp.bfloat16)
    patch_rows = tokens_dev // PW
    tile_rows = 2 * patch_rows
    width = 2 * PW
    tile = (
        patches.reshape(patch_rows, PW, 2, 2, LC)
        .transpose(0, 2, 1, 3, 4)
        .reshape(tile_rows, width * LC)
    )
    padded = padded_2(tile, ((("blk", "head", "dec"), 0),), 1)
    frame_stride = blocks // FRAMES
    frame_index = block_index // frame_stride
    prior_one = from_behind(padded, "blk", frame_stride)
    prior_one = jnp.where(frame_index >= 1, prior_one, padded)
    prior_two = from_behind(prior_one, "blk", frame_stride)
    prior_two = jnp.where(frame_index >= 1, prior_two, padded)
    history = jnp.stack([prior_two, prior_one, padded]).reshape(3, tile_rows + 2, width, LC)
    history = jnp.pad(history, ((0, 0), (0, 0), (1, 1), (0, 0)))
    windows = [
        history[time_tap, row_tap : row_tap + tile_rows, column_tap : column_tap + width, :]
        for time_tap in range(3)
        for row_tap in range(3)
        for column_tap in range(3)
    ]
    columns = jnp.concatenate(windows, axis=-1).reshape(tile_rows * width, 27 * LC)
    summed = (
        jnp.dot(columns, decoder_kernel, preferred_element_type=jnp.float32) + decoder_bias[None, :]
    )
    return summed.astype(jnp.bfloat16).reshape(tile_rows, width, decoder_kernel.shape[1])


HIGH = 3
CHUNKS = 4
STEPS = (2, 4, 1)
SIDE = (1, 2)
LOG2_E = 1.4426950408889634
MESH = pl.DeviceIdType.MESH


def fused_kernel(
    q_hbm, k_hbm, v_hbm, look_hbm, res_hbm, w_hbm, gate_hbm, shift_hbm, scale_hbm, fw_hbm, dk_hbm, db_hbm,
    out_ref,
    lookback, kz, kx, qv, asked, mixed_out, mixed_in, level_out, level_in, wv, resv, gatev, shiftv, scalev, fwv, dkv, dbv,
    top, total, acc, att, part, from_dec, to_y, from_y, hid, halo, wide, canvas,
    load_sem, kv_sem, zs, zr, xs, xr, qs, qr, os, orr, ls, lr, ds, dr, ys, yr, hs, hr,
):
    f = lax.axis_index("blk")
    hd = lax.axis_index("head")
    dc = lax.axis_index("dec")
    z, x = f // 2, f % 2
    n = f * 4 + hd * 2 + dc
    slab = q_hbm.shape[0]
    columns = w_hbm.shape[1] // CHUNKS

    barrier = pltpu.get_barrier_semaphore()
    greeted = jnp.int32(1)
    pl.semaphore_signal(barrier, inc=1, device_id=(f, 1 - hd, dc), device_id_type=MESH)
    for apart in (1, 3, 4, 5, 7, 8, 9):
        for m in (n - apart, n + apart):
            there = (m >= 0) & (m < 32)
            greeted = greeted + jnp.where(there, 1, 0)

            @pl.when(there)
            def _():
                pl.semaphore_signal(
                    barrier, inc=1, device_id=(m // 4, (m % 4) // 2, m % 2), device_id_type=MESH
                )

    @pl.when((f == 2) | (f == 6))
    def _():
        pl.semaphore_signal(barrier, inc=1, device_id=(8 - f, hd, dc), device_id_type=MESH)

    greeted = greeted + jnp.where((f == 2) | (f == 6), 1, 0)

    kv_loads = []
    for h in range(HIGH):
        for which, src in enumerate((k_hbm, v_hbm)):
            kv_loads.append(
                pltpu.make_async_copy(
                    src.at[:, pl.ds(h * DH, DH)], kz.at[0, h, which], kv_sem.at[2 * h + which]
                )
            )
    loads = [
        pltpu.make_async_copy(src, dst, load_sem.at[i])
        for i, (src, dst) in enumerate(
            (
                *[(q_hbm.at[:, pl.ds(h * DH, DH)], qv.at[h]) for h in range(HIGH)],
                (dk_hbm, dkv), (look_hbm, lookback), (w_hbm, wv), (res_hbm, resv), (gate_hbm, gatev),
                (shift_hbm, shiftv), (scale_hbm, scalev), (fw_hbm, fwv), (db_hbm, dbv),
            )
        )
    ]
    for c in kv_loads + loads:
        c.start()

    def up(h):
        return pltpu.make_async_remote_copy(
            src_ref=kz.at[0, h], dst_ref=kz.at[1, h], send_sem=zs.at[h], recv_sem=zr.at[h],
            device_id=(f + 2, hd, dc), device_id_type=MESH,
        )

    def own_across(h):
        return pltpu.make_async_remote_copy(
            src_ref=kz.at[0, h], dst_ref=kx.at[0, h], send_sem=xs.at[0, h], recv_sem=xr.at[0, h],
            device_id=(f + 1, hd, dc), device_id_type=MESH,
        )

    def lower_across(h):
        return pltpu.make_async_remote_copy(
            src_ref=kz.at[1, h], dst_ref=kx.at[1 - x, h], send_sem=xs.at[1, h], recv_sem=xr.at[1 - x, h],
            device_id=(f + 1 - 2 * x, hd, dc), device_id_type=MESH,
        )

    def arrived(slot, h):
        pltpu.make_async_remote_copy(
            src_ref=kz.at[1, h], dst_ref=kx.at[slot, h], send_sem=xs.at[1, h], recv_sem=xr.at[slot, h],
            device_id=(f + 1 - 2 * x, hd, dc), device_id_type=MESH,
        ).wait_recv()

    def ask(far, h):
        return pltpu.make_async_remote_copy(
            src_ref=qv.at[h], dst_ref=asked.at[far, h], send_sem=qs.at[far, h], recv_sem=qr.at[far, h],
            device_id=(f - STEPS[far], hd, dc), device_id_type=MESH,
        )

    def answer(far, h):
        to = (f + STEPS[far], hd, dc)
        return (
            pltpu.make_async_remote_copy(
                src_ref=mixed_out.at[far, h], dst_ref=mixed_in.at[far, h],
                send_sem=os.at[far, h], recv_sem=orr.at[far, h], device_id=to, device_id_type=MESH,
            ),
            pltpu.make_async_remote_copy(
                src_ref=level_out.at[far, h], dst_ref=level_in.at[far, h],
                send_sem=ls.at[far, h], recv_sem=lr.at[far, h], device_id=to, device_id_type=MESH,
            ),
        )

    asks = (z >= 2, f == 6, x == 1)
    helps = ((z >= 1) & (z <= 2), f == 2, x == 0)

    def kinds(h):
        return (0, 1, 2) if h in SIDE else (0, 1)


    for c in kv_loads:
        c.wait()
    for h in range(HIGH):
        loads[h].wait()
    pl.semaphore_wait(barrier, greeted)

    for far in (2, 0, 1):
        for h in SIDE if far == 2 else range(HIGH):

            @pl.when(asks[far])
            def _():
                ask(far, h).start()

    for h in range(HIGH):

        @pl.when((z < 3) & ((z == 0) | (h == 0)))
        def _():
            up(h).start()

        if h not in SIDE:

            @pl.when(x == 0)
            def _():
                own_across(h).start()

    def scored(query, key):
        return lax.dot_general(
            key, query, (((1,), (1,)), ((), ())), preferred_element_type=jnp.float32
        ) * (DH ** (-0.5) * LOG2_E)

    def visible(h, distance):
        return lookback[0, (hd * 2 + dc) * HIGH + h] >= distance

    def weighed(scores, shift, value):
        weights = jnp.exp2(scores + shift)
        mixed = lax.dot_general(
            value, weights.astype(jnp.bfloat16), (((0,), (0,)), ((), ())), preferred_element_type=jnp.float32
        )
        return jnp.sum(weights, axis=0, keepdims=True), mixed

    def attend(h, key, value, distance):
        scores = scored(qv[h], key)
        highest = jnp.max(scores, axis=0, keepdims=True)
        if isinstance(distance, int) and distance == 0:
            total[h], acc[h] = weighed(scores, -highest, value)
            top[h] = highest
        else:
            seen = visible(h, distance)
            newest = jnp.maximum(top[h], jnp.where(seen, highest, -1e30))
            added, mixed = weighed(scores, jnp.where(seen, -newest, -1e30), value)
            shrink = jnp.exp2(top[h] - newest)
            total[h] = total[h] * shrink + added
            acc[h] = acc[h] * shrink + mixed
            top[h] = newest

    def help_with(far, h, blocks):
        @pl.when(helps[far])
        def _():
            ask(far, h).wait_recv()
            query = asked[far, h]
            newest, scores = jnp.full((1, slab), -1e30, jnp.float32), []
            for key, _, distance in blocks:
                scores.append(scored(query, key))
                highest = jnp.max(scores[-1], axis=0, keepdims=True)
                newest = jnp.maximum(newest, jnp.where(visible(h, distance), highest, -1e30))
            added, mixed = 0.0, 0.0
            for each, (_, value, distance) in zip(scores, blocks):
                part_of = weighed(each, jnp.where(visible(h, distance), -newest, -1e30), value)
                added, mixed = added + part_of[0], mixed + part_of[1]
            added = jnp.where(added > 0.0, added, 1.0)
            mixed_out[far, h] = (mixed / added).astype(jnp.bfloat16)
            level_out[far, h] = jnp.broadcast_to(newest + jnp.log2(added), (8, slab))
            for copy in answer(far, h):
                copy.start()

    loads[HIGH].wait()
    loads[HIGH + 1].wait()
    for h in range(HIGH):
        attend(h, kz[0, h, 0], kz[0, h, 1], 0)

    wide[...] = jnp.zeros_like(wide)
    for a in range(2):
        for b in range(2):
            for t in range(3):
                for i in range(3):
                    for j in range(3):
                        ya, xb = a + i - 1, b + j - 1
                        row = ((t * 2 + ya // 2 - (a - 1)) * 2 + xb // 2 - (b - 1)) * 64
                        row += ((ya % 2) * 2 + xb % 2) * LC
                        tap = (t * 3 + i) * 3 + j
                        wide[a * 2 + b, row : row + LC, :] = dkv[tap * LC : (tap + 1) * LC, :]

    for h in SIDE:
        help_with(2, h, ((kz[0, h, 0], kz[0, h, 1], 1),))

    def from_below(h):
        @pl.when(z >= 1)
        def _():
            up(h).wait_recv()
            lower_across(h).start()
            if h < HIGH - 1:

                @pl.when(z < 3)
                def _():
                    up(h + 1).start()

            attend(h, kz[1, h, 0], kz[1, h, 1], 2)

    def from_beside(h):
        @pl.when(z >= 1)
        def _():
            arrived(x, h)
            lower = (kx[x, h, 0], kx[x, h, 1], 3 + 2 * x)
            help_with(0, h, (lower, (kz[1, h, 0], kz[1, h, 1], 4)))
            help_with(1, h, ((lower[0], lower[1], 5),))
            attend(h, kx[x, h, 0], kx[x, h, 1], 1 + 2 * x)

    for h in range(HIGH):
        from_below(h)
        if h:
            from_beside(h - 1)
    from_beside(HIGH - 1)

    for h in range(HIGH):
        if h in SIDE:
            continue

        @pl.when(x == 1)
        def _():
            arrived(0, h)
            attend(h, kx[0, h, 0], kx[0, h, 1], 1)

    for far in (2, 1, 0):
        for h in SIDE if far == 2 else range(HIGH):

            @pl.when(asks[far])
            def _():
                for copy in answer(far, h):
                    copy.wait_recv()
                level = level_in[far, h][:1]
                newest = jnp.maximum(top[h], level)
                shrink, grow = jnp.exp2(top[h] - newest), jnp.exp2(level - newest)
                total[h] = total[h] * shrink + grow
                acc[h] = acc[h] * shrink + mixed_in[far, h].astype(jnp.float32) * grow
                top[h] = newest

    for h in range(HIGH):
        att[:, :, h * DH : (h + 1) * DH] = (acc[h] / total[h]).T.astype(jnp.bfloat16).reshape(2, slab // 2, DH)

    def to_core(half, c):
        return pltpu.make_async_remote_copy(
            src_ref=part.at[c, half, 1 - dc], dst_ref=from_dec.at[c, half],
            send_sem=ds.at[half, c], recv_sem=dr.at[half, c],
            device_id=(f, hd, 1 - dc), device_id_type=MESH,
        )

    def to_row(c):
        return pltpu.make_async_remote_copy(
            src_ref=to_y.at[c], dst_ref=from_y.at[c], send_sem=ys.at[c], recv_sem=yr.at[c],
            device_id=(f, 1 - hd, dc), device_id_type=MESH,
        )

    loads[HIGH + 2].wait()
    def share(half, c):
        got = jnp.dot(
            att[half], wv[:, c * columns : (c + 1) * columns], preferred_element_type=jnp.float32
        ).astype(jnp.bfloat16)
        part[c, half] = got.reshape(2, slab // 4, columns)
        to_core(half, c).start()

    def both_cores(half, c):
        to_core(half, c).wait_recv()
        return part[c, half, dc].astype(jnp.float32) + from_dec[c, half].astype(jnp.float32)

    def pass_on(c):
        to_y[c] = both_cores(1 - hd, c).astype(jnp.bfloat16)
        to_row(c).start()

    for c in range(CHUNKS):
        share(1 - hd, c)
    for c in range(CHUNKS):
        share(hd, c)
    for c in range(CHUNKS):
        pass_on(c)
    for load in loads[HIGH + 3 :]:
        load.wait()
    for c in range(CHUNKS):
        cols = slice(c * columns, (c + 1) * columns)
        hid[c] = resv[:, cols].astype(jnp.float32) + gatev[:, cols] * both_cores(hd, c)
    summed = jnp.zeros((slab // 4, 1), jnp.float32)
    for c in range(CHUNKS):
        cols = slice(c * columns, (c + 1) * columns)
        to_row(c).wait_recv()
        hidden = hid[c] + gatev[:, cols] * from_y[c].astype(jnp.float32)
        hid[c] = hidden
        summed = summed + jnp.sum(hidden, axis=1, keepdims=True)
    center = summed / (CHUNKS * columns)
    squares = jnp.zeros((slab // 4, 1), jnp.float32)
    for c in range(CHUNKS):
        squares = squares + jnp.sum((hid[c] - center) ** 2, axis=1, keepdims=True)
    inverse = lax.rsqrt(squares / (CHUNKS * columns) + 1e-06)
    patches = jnp.zeros((slab // 4, fwv.shape[0]), jnp.float32)
    for c in range(CHUNKS):
        cols = slice(c * columns, (c + 1) * columns)
        normed = ((hid[c] - center) * inverse * (1.0 + scalev[:, cols]) + shiftv[:, cols]).astype(jnp.bfloat16)
        patches = patches + lax.dot_general(
            normed, fwv[:, cols], (((1,), (1,)), ((), ())), preferred_element_type=jnp.float32
        )
    halo[0, 1] = jnp.concatenate([patches, patches], axis=1).astype(jnp.bfloat16)

    def tile_to(back, side):
        m = n + 4 * back - side
        copy = pltpu.make_async_remote_copy(
            src_ref=halo.at[0, 1], dst_ref=halo.at[back, side + 1],
            send_sem=hs.at[back, side + 1], recv_sem=hr.at[back, side + 1],
            device_id=(m // 4, (m % 4) // 2, m % 2), device_id_type=MESH,
        )
        return copy, (m >= 4 * back) & (m < 32)

    def tile_comes(back, side):
        source = n - 4 * back + side
        return (f >= back) & (source >= 0) & (source < 32)

    reach = [(back, side) for back in (2, 1, 0) for side in (-1, 0, 1) if (back, side) != (0, 0)]
    for back, side in reach:
        copy, goes = tile_to(back, side)

        @pl.when(goes)
        def _():
            copy.start()

    for back, side in reach:

        @pl.when(tile_comes(back, side))
        def _():
            tile_to(back, side)[0].wait_recv()

    rows = 4 * PW
    lane = lax.broadcasted_iota(jnp.int32, (rows, 128), 1)
    token = lax.broadcasted_iota(jnp.int32, (rows, 128), 0) % PW
    pairs = []
    for t in range(3):
        back = jnp.minimum(2 - t, f)
        first = n - 4 * back
        above = jnp.where(first >= 1, halo[back, 0, PW:, :].astype(jnp.float32), 0.0)
        below = jnp.where(first <= 30, halo[back, 2, :PW, :].astype(jnp.float32), 0.0)
        ext = jnp.concatenate([above, halo[back, 1].astype(jnp.float32), below], axis=0)
        before = jnp.where(token == 0, 0.0, pltpu.roll(ext, 1, 0))
        after = jnp.where(token == PW - 1, 0.0, pltpu.roll(ext, rows - 1, 0))
        pairs.append(
            (
                jnp.where(lane < 64, before, ext).astype(jnp.bfloat16),
                jnp.where(lane < 64, ext, after).astype(jnp.bfloat16),
            )
        )
    for a in range(2):
        for b in range(2):
            lhs = jnp.concatenate(
                [
                    pairs[t][b][(a + d) * PW : (a + d) * PW + 2 * PW]
                    for t in range(3)
                    for d in range(2)
                ],
                axis=1,
            )
            got = jnp.dot(lhs, wide[a * 2 + b], preferred_element_type=jnp.float32) + dbv[...]
            for r in range(2):
                for g in range(got.shape[1] // 128):
                    canvas[g, pl.ds((2 * r + a) * 2 * PW + b, PW, stride=2), :] = got[
                        r * PW : (r + 1) * PW, g * 128 : (g + 1) * 128
                    ]
    for y in range(4):
        for g in range(canvas.shape[0]):
            out_ref[y, :, g * 128 : (g + 1) * 128] = canvas[g, y * 2 * PW : (y + 1) * 2 * PW, :].astype(jnp.bfloat16)

    for h in range(HIGH):

        @pl.when(z < 3)
        def _():
            up(h).wait_send()

        @pl.when(z >= 1)
        def _():
            lower_across(h).wait_send()

        if h not in SIDE:

            @pl.when(x == 0)
            def _():
                own_across(h).wait_send()

        for far in kinds(h):

            @pl.when(asks[far])
            def _():
                ask(far, h).wait_send()

            @pl.when(helps[far])
            def _():
                for copy in answer(far, h):
                    copy.wait_send()

    for c in range(CHUNKS):
        to_core(hd, c).wait_send()
        to_core(1 - hd, c).wait_send()
        to_row(c).wait_send()
    for back, side in reach:
        copy, goes = tile_to(back, side)

        @pl.when(goes)
        def _():
            copy.wait_send()


def fused(
    queries, key_vectors, values, lookback, residual, out_weight,
    branch_gate, final_shift, final_scale, final_weight, decoder_kernel, decoder_bias,
):
    slab, width = queries.shape
    model = out_weight.shape[1]
    quarter, columns = slab // 4, model // CHUNKS
    outputs = decoder_kernel.shape[1]
    bf, f32 = jnp.bfloat16, jnp.float32
    vm, dma = pltpu.VMEM, pltpu.SemaphoreType.DMA
    hbm = pl.BlockSpec(memory_space=pltpu.HBM)
    return pl.pallas_call(
        fused_kernel,
        out_shape=pltpu.VMEM((4, 2 * PW, outputs), bf),
        in_specs=[hbm] * 12,
        out_specs=pl.BlockSpec(memory_space=pltpu.VMEM),
        scratch_shapes=[
            pltpu.SMEM((1, lookback.shape[0]), jnp.int32),
            vm((2, HIGH, 2, slab, DH), bf), vm((2, HIGH, 2, slab, DH), bf), vm((HIGH, slab, DH), bf),
            vm((3, HIGH, slab, DH), bf), *[vm((3, HIGH, DH, slab), bf)] * 2, *[vm((3, HIGH, 8, slab), f32)] * 2,
            vm((width, model), bf), vm((quarter, model), bf),
            vm((1, model), f32), vm((1, model), f32), vm((1, model), f32),
            vm(final_weight.shape[::-1], bf), vm(decoder_kernel.shape, bf), vm((1, outputs), f32),
            vm((HIGH, 1, slab), f32), vm((HIGH, 1, slab), f32), vm((HIGH, DH, slab), f32),
            vm((2, slab // 2, width), bf), vm((CHUNKS, 2, 2, quarter, columns), bf),
            vm((CHUNKS, 2, quarter, columns), bf), vm((CHUNKS, quarter, columns), bf),
            vm((CHUNKS, quarter, columns), bf), vm((CHUNKS, quarter, columns), f32),
            vm((3, 3, quarter, 128), bf), vm((4, 768, outputs), bf), vm((outputs // 128, 256, 128), f32),
            dma((HIGH + 9,)), dma((6,)), dma((HIGH,)), dma((HIGH,)), dma((2, HIGH)), dma((2, HIGH)),
            *[dma((3, HIGH))] * 6,
            dma((2, CHUNKS)), dma((2, CHUNKS)), dma((CHUNKS,)), dma((CHUNKS,)), dma((3, 3)), dma((3, 3)),
        ],
        compiler_params=pltpu.CompilerParams(collective_id=0, has_side_effects=True, vmem_limit_bytes=60 * 1024 * 1024),
    )(
        queries, key_vectors, values, lookback.reshape(1, -1), residual, out_weight,
        branch_gate.reshape(1, -1), final_shift.reshape(1, -1), final_scale.reshape(1, -1),
        final_weight.T, decoder_kernel, decoder_bias.reshape(1, -1),
    )


def one_slab_a_frame(mesh):
    return (mesh.shape["blk"], mesh.shape["head"], mesh.shape["dec"]) == (FRAMES, 2, 2)


def solution(mesh):
    in_specs = (
        P("blk", ("head", "dec")),
        P("blk", ("head", "dec")),
        P("blk", ("head", "dec")),
        P(),
        P(("blk", "head", "dec"), None),
        P(("head", "dec"), None),
        P(),
        P(),
        P(),
        P(),
        P(),
        P(),
    )
    out_specs = P(("blk", "head", "dec"), None, None)
    body = fused if one_slab_a_frame(mesh) else per_device
    return jax.shard_map(
        body, mesh=mesh, in_specs=in_specs, out_specs=out_specs, check_vma=False
    )
```

```python
import functools

import jax
import jax.numpy as jnp
from jax import lax
from jax.experimental import pallas as pl
from jax.experimental.pallas import tpu as pltpu
from jax.sharding import PartitionSpec as P

DH = 128
LC = 16
FRAMES = 8
PW = 32


def padded_2(cells, sides, width):
    for axis, dim in sides:
        count = lax.axis_size(axis)
        ends = count - 1
        head = lax.slice_in_dim(cells, 0, width, axis=dim)
        tail = lax.slice_in_dim(cells, cells.shape[dim] - width, cells.shape[dim], axis=dim)
        cells = jnp.concatenate(
            [
                lax.ppermute(tail, axis, [(i, (i + 1) % count) for i in range(ends)]),
                cells,
                lax.ppermute(head, axis, [((i + 1) % count, i) for i in range(ends)]),
            ],
            axis=dim,
        )
    return cells


def from_behind(x, axis, by):
    peers = lax.axis_size(axis)
    pairs = [(i, i + by) for i in range(peers) if 0 <= i + by < peers]
    return lax.ppermute(x, axis, pairs)


def attend_block(carry, shard_pair, query_heads, query_frame, lookback_heads, frame_len):
    running_max, row_total, accumulated = carry
    key_block, value_block = shard_pair
    key_count = key_block.shape[0]
    head_count = query_heads.shape[1]
    key_heads = key_block.reshape(key_count, head_count, DH)
    value_heads = value_block.reshape(key_count, head_count, DH)
    scores = jnp.einsum(
        "qhd,khd->hqk", query_heads, key_heads, preferred_element_type=jnp.float32
    ) * DH ** (-0.5)
    key_pos = jnp.arange(key_count, dtype=jnp.int32)
    key_frame = key_pos // frame_len
    visible = (
        (key_pos >= 0)[None, None, :]
        & (key_frame[None, None, :] <= query_frame[None, :, None])
        & (key_frame[None, None, :] >= query_frame[None, :, None] - lookback_heads[:, None, None])
    )
    masked = jnp.where(visible, scores, -1e30)
    newest_max = jnp.maximum(running_max, jnp.max(masked, axis=2))
    weights = jnp.where(visible, jnp.exp(scores - newest_max[:, :, None]), 0.0).astype(jnp.bfloat16)
    row_total = jnp.sum(weights.astype(jnp.float32), axis=2)
    accumulated = jnp.einsum(
        "hqk,khd->hqd", weights, value_heads, preferred_element_type=jnp.float32
    )
    return (newest_max, row_total, accumulated)


def per_device(
    queries,
    key_vectors,
    values,
    lookback,
    residual,
    out_weight,
    branch_gate,
    final_shift,
    final_scale,
    final_weight,
    decoder_kernel,
    decoder_bias,
):
    slab_rows = queries.shape[0]
    head_count = queries.shape[1] // DH
    blocks = lax.axis_size("blk")
    block_index = lax.axis_index("blk")
    frame_len = slab_rows * blocks // FRAMES
    query_heads = queries.reshape(slab_rows, head_count, DH)
    query_frame = (block_index * slab_rows + jnp.arange(slab_rows, dtype=jnp.int32)) // frame_len
    lookback_heads = lax.dynamic_slice_in_dim(
        lookback, lax.axis_index(("head", "dec")) * head_count, head_count
    )
    initial = (
        jnp.full((head_count, slab_rows), -1e30, jnp.float32),
        jnp.zeros((head_count, slab_rows), jnp.float32),
        jnp.zeros((head_count, slab_rows, DH), jnp.float32),
    )
    carry = attend_block(
        initial,
        (
            lax.all_gather(key_vectors, "blk", axis=0, tiled=True),
            lax.all_gather(values, "blk", axis=0, tiled=True),
        ),
        query_heads,
        query_frame,
        lookback_heads,
        frame_len,
    )
    newest_max, row_total, accumulated = carry
    attended = (
        (accumulated / row_total[:, :, None])
        .transpose(1, 0, 2)
        .reshape(slab_rows, head_count * DH)
        .astype(jnp.bfloat16)
    )
    tokens_dev = slab_rows // lax.axis_size(("head", "dec"))
    projected = lax.psum_scatter(
        jnp.dot(attended, out_weight, preferred_element_type=jnp.float32).astype(jnp.bfloat16),
        ("head", "dec"),
        scatter_dimension=0,
        tiled=True,
    ).astype(jnp.float32)
    hidden = residual.astype(jnp.float32) + branch_gate[None, :] * projected
    center = jnp.mean(hidden, axis=1, keepdims=True)
    spread = jnp.mean((hidden - center) ** 2, axis=1, keepdims=True)
    normed = (
        (hidden - center) * lax.rsqrt(spread + 1e-06) * (1.0 + final_scale[None, :])
        + final_shift[None, :]
    ).astype(jnp.bfloat16)
    patches = jnp.dot(normed, final_weight, preferred_element_type=jnp.float32).astype(jnp.bfloat16)
    patch_rows = tokens_dev // PW
    tile_rows = 2 * patch_rows
    width = 2 * PW
    tile = (
        patches.reshape(patch_rows, PW, 2, 2, LC)
        .transpose(0, 2, 1, 3, 4)
        .reshape(tile_rows, width * LC)
    )
    padded = padded_2(tile, ((("blk", "head", "dec"), 0),), 1)
    frame_stride = blocks // FRAMES
    frame_index = block_index // frame_stride
    prior_one = from_behind(padded, "blk", frame_stride)
    prior_one = jnp.where(frame_index >= 1, prior_one, padded)
    prior_two = from_behind(prior_one, "blk", frame_stride)
    prior_two = jnp.where(frame_index >= 1, prior_two, padded)
    history = jnp.stack([prior_two, prior_one, padded]).reshape(3, tile_rows + 2, width, LC)
    history = jnp.pad(history, ((0, 0), (0, 0), (1, 1), (0, 0)))
    windows = [
        history[time_tap, row_tap : row_tap + tile_rows, column_tap : column_tap + width, :]
        for time_tap in range(3)
        for row_tap in range(3)
        for column_tap in range(3)
    ]
    columns = jnp.concatenate(windows, axis=-1).reshape(tile_rows * width, 27 * LC)
    summed = (
        jnp.dot(columns, decoder_kernel, preferred_element_type=jnp.float32) + decoder_bias[None, :]
    )
    return summed.astype(jnp.bfloat16).reshape(tile_rows, width, decoder_kernel.shape[1])


HIGH = 3
CHUNKS = 6
STEPS = (2, 4, 1)
SIDE = (1, 2)
LOG2_E = 1.4426950408889634
MESH = pl.DeviceIdType.MESH


def fused_kernel(
    q_hbm, k_hbm, v_hbm, look_hbm, res_hbm, w_hbm, gate_hbm, shift_hbm, scale_hbm, fw_hbm, dk_hbm, db_hbm,
    out_ref,
    lookback, kz, kx, qv, asked, mixed_out, mixed_in, level_out, level_in, wv, resv, gatev, shiftv, scalev, fwv, dkv, dbv,
    top, total, acc, att, part, from_dec, to_y, from_y, hid, halo, wide, canvas,
    load_sem, kv_sem, zs, zr, xs, xr, qs, qr, os, orr, ls, lr, ds, dr, ys, yr, hs, hr,
):
    f = lax.axis_index("blk")
    hd = lax.axis_index("head")
    dc = lax.axis_index("dec")
    z, x = f // 2, f % 2
    n = f * 4 + hd * 2 + dc
    slab = q_hbm.shape[0]
    columns = w_hbm.shape[1] // CHUNKS

    barrier = pltpu.get_barrier_semaphore()
    greeted = jnp.int32(1)
    pl.semaphore_signal(barrier, inc=1, device_id=(f, 1 - hd, dc), device_id_type=MESH)
    for apart in (1, 3, 4, 5, 7, 8, 9):
        for m in (n - apart, n + apart):
            there = (m >= 0) & (m < 32)
            greeted = greeted + jnp.where(there, 1, 0)

            @pl.when(there)
            def _():
                pl.semaphore_signal(
                    barrier, inc=1, device_id=(m // 4, (m % 4) // 2, m % 2), device_id_type=MESH
                )

    @pl.when((f == 2) | (f == 6))
    def _():
        pl.semaphore_signal(barrier, inc=1, device_id=(8 - f, hd, dc), device_id_type=MESH)

    greeted = greeted + jnp.where((f == 2) | (f == 6), 1, 0)

    kv_loads = []
    for h in range(HIGH):
        for which, src in enumerate((k_hbm, v_hbm)):
            kv_loads.append(
                pltpu.make_async_copy(
                    src.at[:, pl.ds(h * DH, DH)], kz.at[0, h, which], kv_sem.at[2 * h + which]
                )
            )
    loads = [
        pltpu.make_async_copy(src, dst, load_sem.at[i])
        for i, (src, dst) in enumerate(
            (
                *[(q_hbm.at[:, pl.ds(h * DH, DH)], qv.at[h]) for h in range(HIGH)],
                (dk_hbm, dkv), (look_hbm, lookback), (w_hbm, wv), (res_hbm, resv), (gate_hbm, gatev),
                (shift_hbm, shiftv), (scale_hbm, scalev), (fw_hbm, fwv), (db_hbm, dbv),
            )
        )
    ]
    for c in kv_loads + loads:
        c.start()

    def up(h):
        return pltpu.make_async_remote_copy(
            src_ref=kz.at[0, h], dst_ref=kz.at[1, h], send_sem=zs.at[h], recv_sem=zr.at[h],
            device_id=(f + 2, hd, dc), device_id_type=MESH,
        )

    def own_across(h):
        return pltpu.make_async_remote_copy(
            src_ref=kz.at[0, h], dst_ref=kx.at[0, h], send_sem=xs.at[0, h], recv_sem=xr.at[0, h],
            device_id=(f + 1, hd, dc), device_id_type=MESH,
        )

    def lower_across(h):
        return pltpu.make_async_remote_copy(
            src_ref=kz.at[1, h], dst_ref=kx.at[1 - x, h], send_sem=xs.at[1, h], recv_sem=xr.at[1 - x, h],
            device_id=(f + 1 - 2 * x, hd, dc), device_id_type=MESH,
        )

    def arrived(slot, h):
        pltpu.make_async_remote_copy(
            src_ref=kz.at[1, h], dst_ref=kx.at[slot, h], send_sem=xs.at[1, h], recv_sem=xr.at[slot, h],
            device_id=(f + 1 - 2 * x, hd, dc), device_id_type=MESH,
        ).wait_recv()

    def ask(far, h):
        return pltpu.make_async_remote_copy(
            src_ref=qv.at[h], dst_ref=asked.at[far, h], send_sem=qs.at[far, h], recv_sem=qr.at[far, h],
            device_id=(f - STEPS[far], hd, dc), device_id_type=MESH,
        )

    def answer(far, h):
        to = (f + STEPS[far], hd, dc)
        return (
            pltpu.make_async_remote_copy(
                src_ref=mixed_out.at[far, h], dst_ref=mixed_in.at[far, h],
                send_sem=os.at[far, h], recv_sem=orr.at[far, h], device_id=to, device_id_type=MESH,
            ),
            pltpu.make_async_remote_copy(
                src_ref=level_out.at[far, h], dst_ref=level_in.at[far, h],
                send_sem=ls.at[far, h], recv_sem=lr.at[far, h], device_id=to, device_id_type=MESH,
            ),
        )

    asks = (z >= 2, f == 6, x == 1)
    helps = ((z >= 1) & (z <= 2), f == 2, x == 0)

    def kinds(h):
        return (0, 1, 2) if h in SIDE else (0, 1)


    for c in kv_loads:
        c.wait()
    for h in range(HIGH):
        loads[h].wait()
    pl.semaphore_wait(barrier, greeted)

    for far in (2, 0, 1):
        for h in SIDE if far == 2 else range(HIGH):

            @pl.when(asks[far])
            def _():
                ask(far, h).start()

    for h in range(HIGH):

        @pl.when(z < 3)
        def _():
            up(h).start()

        if h not in SIDE:

            @pl.when(x == 0)
            def _():
                own_across(h).start()

    def scored(query, key):
        return lax.dot_general(
            key, query, (((1,), (1,)), ((), ())), preferred_element_type=jnp.float32
        ) * (DH ** (-0.5) * LOG2_E)

    def visible(h, distance):
        return lookback[0, (hd * 2 + dc) * HIGH + h] >= distance

    def weighed(scores, shift, value):
        weights = jnp.exp2(scores + shift)
        mixed = lax.dot_general(
            value, weights.astype(jnp.bfloat16), (((0,), (0,)), ((), ())), preferred_element_type=jnp.float32
        )
        return jnp.sum(weights, axis=0, keepdims=True), mixed

    def attend(h, key, value, distance, scores=None):
        if scores is None:
            scores = scored(qv[h], key)
        highest = jnp.max(scores, axis=0, keepdims=True)
        if isinstance(distance, int) and distance == 0:
            total[h], acc[h] = weighed(scores, -highest, value)
            top[h] = highest
        else:
            seen = visible(h, distance)
            newest = jnp.maximum(top[h], jnp.where(seen, highest, -1e30))
            added, mixed = weighed(scores, jnp.where(seen, -newest, -1e30), value)
            shrink = jnp.exp2(top[h] - newest)
            total[h] = total[h] * shrink + added
            acc[h] = acc[h] * shrink + mixed
            top[h] = newest

    def answered(far, h, scores, blocks):
        newest = jnp.full((1, slab), -1e30, jnp.float32)
        for each, (_, _, distance) in zip(scores, blocks):
            highest = jnp.max(each, axis=0, keepdims=True)
            newest = jnp.maximum(newest, jnp.where(visible(h, distance), highest, -1e30))
        added, mixed = 0.0, 0.0
        for each, (_, value, distance) in zip(scores, blocks):
            part_of = weighed(each, jnp.where(visible(h, distance), -newest, -1e30), value)
            added, mixed = added + part_of[0], mixed + part_of[1]
        added = jnp.where(added > 0.0, added, 1.0)
        mixed_out[far, h] = (mixed / added).astype(jnp.bfloat16)
        level_out[far, h] = jnp.broadcast_to(newest + jnp.log2(added), (8, slab))

    def help_with(far, h, blocks):
        @pl.when(helps[far])
        def _():
            ask(far, h).wait_recv()
            query = asked[far, h]
            answered(far, h, [scored(query, key) for key, _, _ in blocks], blocks)
            for copy in answer(far, h):
                copy.start()

    loads[HIGH].wait()
    loads[HIGH + 1].wait()
    for h in range(HIGH):
        attend(h, kz[0, h, 0], kz[0, h, 1], 0)

    wide[...] = jnp.zeros_like(wide)
    for a in range(2):
        for b in range(2):
            for t in range(3):
                for i in range(3):
                    for j in range(3):
                        ya, xb = a + i - 1, b + j - 1
                        row = ((t * 2 + ya // 2 - (a - 1)) * 2 + xb // 2 - (b - 1)) * 64
                        row += ((ya % 2) * 2 + xb % 2) * LC
                        tap = (t * 3 + i) * 3 + j
                        wide[a * 2 + b, row : row + LC, :] = dkv[tap * LC : (tap + 1) * LC, :]

    for h in SIDE:
        help_with(2, h, ((kz[0, h, 0], kz[0, h, 1], 1),))

    def from_below(h):
        @pl.when(z >= 1)
        def _():
            up(h).wait_recv()
            lower_across(h).start()
            attend(h, kz[1, h, 0], kz[1, h, 1], 2)

    def from_beside(h):
        @pl.when(z >= 1)
        def _():
            arrived(x, h)

        @pl.when(helps[0])
        def _():
            ask(0, h).wait_recv()
            query, key, value = asked[0, h], kx[x, h, 0], kx[x, h, 1]
            mine = scored(qv[h], key)
            answered(
                0, h, [scored(query, key), scored(query, kz[1, h, 0])],
                ((key, value, 3 + 2 * x), (None, kz[1, h, 1], 4)),
            )
            attend(h, key, value, 1 + 2 * x, mine)
            for copy in answer(0, h):
                copy.start()

        @pl.when(helps[1])
        def _():
            help_with(1, h, ((kx[0, h, 0], kx[0, h, 1], 5),))

        @pl.when(z == 3)
        def _():
            attend(h, kx[x, h, 0], kx[x, h, 1], 1 + 2 * x)

    for h in range(HIGH):
        from_below(h)
        if h:
            from_beside(h - 1)
    from_beside(HIGH - 1)

    for h in range(HIGH):
        if h in SIDE:
            continue

        @pl.when(x == 1)
        def _():
            arrived(0, h)
            attend(h, kx[0, h, 0], kx[0, h, 1], 1)

    for far in (2, 1, 0):
        for h in SIDE if far == 2 else range(HIGH):

            @pl.when(asks[far])
            def _():
                for copy in answer(far, h):
                    copy.wait_recv()
                level = level_in[far, h][:1]
                newest = jnp.maximum(top[h], level)
                shrink, grow = jnp.exp2(top[h] - newest), jnp.exp2(level - newest)
                total[h] = total[h] * shrink + grow
                acc[h] = acc[h] * shrink + mixed_in[far, h].astype(jnp.float32) * grow
                top[h] = newest

    for h in range(HIGH):
        att[:, :, h * DH : (h + 1) * DH] = (acc[h] / total[h]).T.astype(jnp.bfloat16).reshape(2, slab // 2, DH)

    def to_core(half, c):
        return pltpu.make_async_remote_copy(
            src_ref=part.at[c, half, 1 - dc], dst_ref=from_dec.at[c, half],
            send_sem=ds.at[half, c], recv_sem=dr.at[half, c],
            device_id=(f, hd, 1 - dc), device_id_type=MESH,
        )

    def to_row(c):
        return pltpu.make_async_remote_copy(
            src_ref=to_y.at[c], dst_ref=from_y.at[c], send_sem=ys.at[c], recv_sem=yr.at[c],
            device_id=(f, 1 - hd, dc), device_id_type=MESH,
        )

    loads[HIGH + 2].wait()
    def share(half, c):
        got = jnp.dot(
            att[half], wv[:, c * columns : (c + 1) * columns], preferred_element_type=jnp.float32
        ).astype(jnp.bfloat16)
        part[c, half] = got.reshape(2, slab // 4, columns)
        to_core(half, c).start()

    def both_cores(half, c):
        to_core(half, c).wait_recv()
        return part[c, half, dc].astype(jnp.float32) + from_dec[c, half].astype(jnp.float32)

    def pass_on(c):
        to_y[c] = both_cores(1 - hd, c).astype(jnp.bfloat16)
        to_row(c).start()

    for c in range(CHUNKS):
        share(1 - hd, c)
        if c >= 2:
            pass_on(c - 2)
    pass_on(CHUNKS - 2)
    pass_on(CHUNKS - 1)
    for c in range(CHUNKS):
        share(hd, c)
    for load in loads[HIGH + 3 :]:
        load.wait()
    for c in range(CHUNKS):
        cols = slice(c * columns, (c + 1) * columns)
        hid[c] = resv[:, cols].astype(jnp.float32) + gatev[:, cols] * both_cores(hd, c)
    summed = jnp.zeros((slab // 4, 1), jnp.float32)
    for c in range(CHUNKS):
        cols = slice(c * columns, (c + 1) * columns)
        to_row(c).wait_recv()
        hidden = hid[c] + gatev[:, cols] * from_y[c].astype(jnp.float32)
        hid[c] = hidden
        summed = summed + jnp.sum(hidden, axis=1, keepdims=True)
    center = summed / (CHUNKS * columns)
    squares = jnp.zeros((slab // 4, 1), jnp.float32)
    for c in range(CHUNKS):
        squares = squares + jnp.sum((hid[c] - center) ** 2, axis=1, keepdims=True)
    inverse = lax.rsqrt(squares / (CHUNKS * columns) + 1e-06)
    patches = jnp.zeros((slab // 4, fwv.shape[0]), jnp.float32)
    for c in range(CHUNKS):
        cols = slice(c * columns, (c + 1) * columns)
        normed = ((hid[c] - center) * inverse * (1.0 + scalev[:, cols]) + shiftv[:, cols]).astype(jnp.bfloat16)
        patches = patches + lax.dot_general(
            normed, fwv[:, cols], (((1,), (1,)), ((), ())), preferred_element_type=jnp.float32
        )
    halo[0, 1] = jnp.concatenate([patches, patches], axis=1).astype(jnp.bfloat16)

    def tile_to(back, side):
        m = n + 4 * back - side
        copy = pltpu.make_async_remote_copy(
            src_ref=halo.at[0, 1], dst_ref=halo.at[back, side + 1],
            send_sem=hs.at[back, side + 1], recv_sem=hr.at[back, side + 1],
            device_id=(m // 4, (m % 4) // 2, m % 2), device_id_type=MESH,
        )
        return copy, (m >= 4 * back) & (m < 32)

    def tile_comes(back, side):
        source = n - 4 * back + side
        return (f >= back) & (source >= 0) & (source < 32)

    reach = [(back, side) for back in (2, 1, 0) for side in (-1, 0, 1) if (back, side) != (0, 0)]
    for back, side in reach:
        copy, goes = tile_to(back, side)

        @pl.when(goes)
        def _():
            copy.start()

    for back, side in reach:

        @pl.when(tile_comes(back, side))
        def _():
            tile_to(back, side)[0].wait_recv()

    rows = 4 * PW
    lane = lax.broadcasted_iota(jnp.int32, (rows, 128), 1)
    token = lax.broadcasted_iota(jnp.int32, (rows, 128), 0) % PW
    pairs = []
    for t in range(3):
        back = jnp.minimum(2 - t, f)
        first = n - 4 * back
        above = jnp.where(first >= 1, halo[back, 0, PW:, :].astype(jnp.float32), 0.0)
        below = jnp.where(first <= 30, halo[back, 2, :PW, :].astype(jnp.float32), 0.0)
        ext = jnp.concatenate([above, halo[back, 1].astype(jnp.float32), below], axis=0)
        before = jnp.where(token == 0, 0.0, pltpu.roll(ext, 1, 0))
        after = jnp.where(token == PW - 1, 0.0, pltpu.roll(ext, rows - 1, 0))
        pairs.append(
            (
                jnp.where(lane < 64, before, ext).astype(jnp.bfloat16),
                jnp.where(lane < 64, ext, after).astype(jnp.bfloat16),
            )
        )
    for a in range(2):
        for b in range(2):
            lhs = jnp.concatenate(
                [
                    pairs[t][b][(a + d) * PW : (a + d) * PW + 2 * PW]
                    for t in range(3)
                    for d in range(2)
                ],
                axis=1,
            )
            got = jnp.dot(lhs, wide[a * 2 + b], preferred_element_type=jnp.float32) + dbv[...]
            for r in range(2):
                for g in range(got.shape[1] // 128):
                    canvas[g, pl.ds((2 * r + a) * 2 * PW + b, PW, stride=2), :] = got[
                        r * PW : (r + 1) * PW, g * 128 : (g + 1) * 128
                    ]
    for y in range(4):
        for g in range(canvas.shape[0]):
            out_ref[y, :, g * 128 : (g + 1) * 128] = canvas[g, y * 2 * PW : (y + 1) * 2 * PW, :].astype(jnp.bfloat16)

    for h in range(HIGH):

        @pl.when(z < 3)
        def _():
            up(h).wait_send()

        @pl.when(z >= 1)
        def _():
            lower_across(h).wait_send()

        if h not in SIDE:

            @pl.when(x == 0)
            def _():
                own_across(h).wait_send()

        for far in kinds(h):

            @pl.when(asks[far])
            def _():
                ask(far, h).wait_send()

            @pl.when(helps[far])
            def _():
                for copy in answer(far, h):
                    copy.wait_send()

    for c in range(CHUNKS):
        to_core(hd, c).wait_send()
        to_core(1 - hd, c).wait_send()
        to_row(c).wait_send()
    for back, side in reach:
        copy, goes = tile_to(back, side)

        @pl.when(goes)
        def _():
            copy.wait_send()


def fused(
    queries, key_vectors, values, lookback, residual, out_weight,
    branch_gate, final_shift, final_scale, final_weight, decoder_kernel, decoder_bias,
):
    slab, width = queries.shape
    model = out_weight.shape[1]
    quarter, columns = slab // 4, model // CHUNKS
    outputs = decoder_kernel.shape[1]
    bf, f32 = jnp.bfloat16, jnp.float32
    vm, dma = pltpu.VMEM, pltpu.SemaphoreType.DMA
    hbm = pl.BlockSpec(memory_space=pltpu.HBM)
    return pl.pallas_call(
        fused_kernel,
        out_shape=pltpu.VMEM((4, 2 * PW, outputs), bf),
        in_specs=[hbm] * 12,
        out_specs=pl.BlockSpec(memory_space=pltpu.VMEM),
        scratch_shapes=[
            pltpu.SMEM((1, lookback.shape[0]), jnp.int32),
            vm((2, HIGH, 2, slab, DH), bf), vm((2, HIGH, 2, slab, DH), bf), vm((HIGH, slab, DH), bf),
            vm((3, HIGH, slab, DH), bf), *[vm((3, HIGH, DH, slab), bf)] * 2, *[vm((3, HIGH, 8, slab), f32)] * 2,
            vm((width, model), bf), vm((quarter, model), bf),
            vm((1, model), f32), vm((1, model), f32), vm((1, model), f32),
            vm(final_weight.shape[::-1], bf), vm(decoder_kernel.shape, bf), vm((1, outputs), f32),
            vm((HIGH, 1, slab), f32), vm((HIGH, 1, slab), f32), vm((HIGH, DH, slab), f32),
            vm((2, slab // 2, width), bf), vm((CHUNKS, 2, 2, quarter, columns), bf),
            vm((CHUNKS, 2, quarter, columns), bf), vm((CHUNKS, quarter, columns), bf),
            vm((CHUNKS, quarter, columns), bf), vm((CHUNKS, quarter, columns), f32),
            vm((3, 3, quarter, 128), bf), vm((4, 768, outputs), bf), vm((outputs // 128, 256, 128), f32),
            dma((HIGH + 9,)), dma((6,)), dma((HIGH,)), dma((HIGH,)), dma((2, HIGH)), dma((2, HIGH)),
            *[dma((3, HIGH))] * 6,
            dma((2, CHUNKS)), dma((2, CHUNKS)), dma((CHUNKS,)), dma((CHUNKS,)), dma((3, 3)), dma((3, 3)),
        ],
        compiler_params=pltpu.CompilerParams(collective_id=0, has_side_effects=True, vmem_limit_bytes=60 * 1024 * 1024),
    )(
        queries, key_vectors, values, lookback.reshape(1, -1), residual, out_weight,
        branch_gate.reshape(1, -1), final_shift.reshape(1, -1), final_scale.reshape(1, -1),
        final_weight.T, decoder_kernel, decoder_bias.reshape(1, -1),
    )


def one_slab_a_frame(mesh):
    return (mesh.shape["blk"], mesh.shape["head"], mesh.shape["dec"]) == (FRAMES, 2, 2)


def solution(mesh):
    in_specs = (
        P("blk", ("head", "dec")),
        P("blk", ("head", "dec")),
        P("blk", ("head", "dec")),
        P(),
        P(("blk", "head", "dec"), None),
        P(("head", "dec"), None),
        P(),
        P(),
        P(),
        P(),
        P(),
        P(),
    )
    out_specs = P(("blk", "head", "dec"), None, None)
    body = fused if one_slab_a_frame(mesh) else per_device
    return jax.shard_map(
        body, mesh=mesh, in_specs=in_specs, out_specs=out_specs, check_vma=False
    )
```
